256 devices in a mesh: mom: 32 (over y, z_hi, x), hist: 8 (over z_lo, core).
Axes of the slice: x: 4, y: 4, z: 8 (z_hi: 2, z_lo: 4; z = z_hi * 4 + z_lo), core: 2. Of those that a mesh axis runs over, the one named last changes fastest.
Arguments:
- green_row: float32 [2, 2, 3, 3, 2048, 4096], P(None, None, None, None, 'hist', 'mom'), may hold values from -6 to 6
- time_step: int32 [1], replicated, may hold values from 0 to 8388607
Outputs:
- collision: float32 [2, 3, 3, 4096], P(None, None, None, ('mom', 'hist'))
The draws below stay inside these ranges and needn't reach their ends.
Inputs may be any that keep to these rules, and one draw needn't show every extreme that they name: History slot j holds the step ((time_step - 1 - j) mod 2048) + 1 steps before the current one.
All inputs are finite; a program needn't handle non-finite values.
Results may differ from the reference program's by a relative error of at most 0.00013.
Values sent between devices are 32-bit elements; how exact they have to be, the bound alone decides.
No kernel may reach another device: no remote copies, remote signals or barrier semaphores. Data moves between devices by JAX's collectives and lax.ppermute only.
A program may use at most 320 MiB of HBM per device.

```python
import jax
import jax.numpy as jnp
from jax import lax

NKX = 64
NKY = 64
ORB = 3
HIST = 2048
NK = 4096


def block_scale(stream_key, extent, shards, smallest, high):
    factor_of, own = 1.0, jax.random.fold_in(stream_key, 6)
    for axis_at, blocks in shards:
        heights = jnp.exp(jax.random.uniform(jax.random.fold_in(own, axis_at), (blocks,), jnp.float32, smallest / len(shards), high / len(shards)))
        factor_of = factor_of * jnp.repeat(heights, extent[axis_at] // blocks).reshape([-1 if axis == axis_at else 1 for axis in range(len(extent))])
    return factor_of


def bell_draw(key, extent, scale, limit, shards=(), kind=jnp.bfloat16):
    drawn = scale * jax.random.normal(key, extent, jnp.float32)
    if shards:
        drawn = drawn * block_scale(key, extent, shards, -0.22, 0.18)
    return jnp.clip(drawn, -limit, limit).astype(kind)


def setup_inputs(seed: int = 0) -> dict:
    arg_keys = jax.random.split(jax.random.key(seed), 3)
    green_row = bell_draw(arg_keys[0], (2, 2, ORB, ORB, HIST, NK), 1.0, 6.0, ((4, 8), (5, 32)), jnp.float32)
    time_step = jax.random.randint(arg_keys[1], (1,), 0, 4096 * HIST).astype(jnp.int32)
    return dict(green_row=green_row, time_step=time_step)


delta_time = 0.01
coupling = 1.0


def memory_weights(time_step):
    slot_ids = jnp.arange(HIST, dtype=jnp.int32)
    slot_age = (time_step[0] - 1 - slot_ids) % HIST + 1
    decays = jnp.exp2(-(slot_age - 1).astype(jnp.float32) / HIST)
    return delta_time * decays * jnp.where(slot_age == HIST, 0.5, 1.0).astype(jnp.float32)


def reference(green_row, time_step):
    moment = green_row[:, 0] + 1j * green_row[:, 1]
    lattice = moment.reshape(moment.shape[:-1] + (NKX, NKY))
    real_space = jnp.fft.ifft2(lattice, axes=(-2, -1), norm="ortho")
    lesser = real_space[0]
    greater = real_space[1]
    sigma_less = -coupling * lesser * lesser * jnp.conj(greater)
    sigma_great = -coupling * greater * greater * jnp.conj(lesser)
    sigma = jnp.fft.fft2(jnp.stack([sigma_less, sigma_great]), axes=(-2, -1), norm="ortho").reshape((2,) + moment.shape[1:])
    weights = memory_weights(time_step)[:, None]
    memory = jnp.einsum("acjk,bcjk->abk", -weights * sigma[1], jnp.conj(moment[0]), precision=lax.Precision.HIGHEST)
    memory = memory + jnp.einsum("acjk,bcjk->abk", weights * sigma[0], jnp.conj(moment[1]), precision=lax.Precision.HIGHEST)
    collision = memory + jnp.conj(jnp.swapaxes(memory, 0, 1))
    return jnp.stack([jnp.real(collision), jnp.imag(collision)]).astype(jnp.float32)
```

```python
import math

import jax
import jax.numpy as jnp
import numpy as np
from jax import lax
from jax.experimental import pallas as pl
from jax.experimental.pallas import tpu as pltpu
from jax.sharding import PartitionSpec as P

NKX = 64
NKY = 64
ORB = 3
PAIRS = ORB * ORB
ROWS = 32
SLOTS = 8
LANES = 128

delta_time = 0.01


def lane_tables():
    index = np.arange(64)
    angle = 2.0 * math.pi * (index[:, None] * index[None, :] % 64) / 64
    sign = np.array([[1.0, 1.0], [1.0, -1.0]])
    cosine = np.kron(sign, np.cos(angle)) / 64
    sine = np.kron(sign, np.sin(angle)) / 64
    table = np.block([[cosine, sine], [-sine, cosine]]).astype(np.float32)
    high = table.astype(jnp.bfloat16)
    low = (table - high.astype(np.float32)).astype(jnp.bfloat16)
    turn = 2.0 * math.pi * np.arange(ROWS)[:, None] * np.repeat([0, 1], 64)[None, :] / 64
    twiddle = np.stack([np.cos(turn), np.sin(turn)], 1).astype(np.float32)
    return high, low, twiddle


def turned(value, step, length):
    real, imag = value
    eighths = step * 8 / length
    if eighths == 0:
        return real, imag
    if eighths == 2:
        return -imag, real
    if eighths == 4:
        return -real, -imag
    if eighths == 6:
        return imag, -real
    root = math.sqrt(0.5)
    if eighths == 1:
        return root * (real - imag), root * (real + imag)
    if eighths == 3:
        return -root * (real + imag), root * (real - imag)
    if eighths == 5:
        return root * (imag - real), -root * (real + imag)
    if eighths == 7:
        return root * (real + imag), root * (imag - real)
    cosine, sine = math.cos(2 * math.pi * step / length), math.sin(2 * math.pi * step / length)
    return real * cosine - imag * sine, real * sine + imag * cosine


def plus(first, second):
    return first[0] + second[0], first[1] + second[1]


def minus(first, second):
    return first[0] - second[0], first[1] - second[1]


def fourier(values):
    length = len(values)
    if length == 1:
        return values
    if length == 2:
        return [plus(*values), minus(*values)]
    quarter = length // 4
    parts = [fourier(values[start::4]) for start in range(4)]
    out = [None] * length
    for m in range(quarter):
        first, second, third, fourth = (turned(parts[p][m], p * m, length) for p in range(4))
        even, odd = plus(first, third), minus(first, third)
        other, cross = plus(second, fourth), minus(second, fourth)
        cross = (-cross[1], cross[0])
        out[m], out[m + 2 * quarter] = plus(even, other), minus(even, other)
        out[m + quarter], out[m + 3 * quarter] = plus(odd, cross), minus(odd, cross)
    return out


def product(values, high, low):
    head = values.astype(jnp.bfloat16)
    tail = (values - head.astype(jnp.float32)).astype(jnp.bfloat16)

    def dot(left, right):
        return jnp.dot(left, right, preferred_element_type=jnp.float32)

    return dot(head, high) + (dot(tail, high) + dot(head, low))


def kernel(green, weight, high_ref, low_ref, twiddle, out, field):
    def spot(part):
        return pl.ds(part * LANES, LANES)

    def twist(n):
        return twiddle[n, 0][None, :], twiddle[n, 1][None, :]

    def times(value, factor):
        return value[0] * factor[0] - value[1] * factor[1], value[0] * factor[1] + value[1] * factor[0]

    @pl.loop(0, 2 * PAIRS)
    def _(s):
        comp, pair = s // PAIRS, s % PAIRS
        at = comp * 2 * PAIRS + pair
        rows = pl.ds(pl.multiple_of(comp * SLOTS, SLOTS), SLOTS)
        values = [(green[m, at], green[m, at + PAIRS]) for m in range(ROWS)]
        for n, value in enumerate(fourier(values)):
            real, imag = times(value, twist(n)) if n else value
            field[n, pair, rows, spot(0)] = real
            field[n, pair, rows, spot(1)] = imag

    block = 4
    size = block * PAIRS * 2 * SLOTS

    @pl.loop(0, ROWS // block)
    def _(b):
        take = pl.ds(b * block, block)
        high, low = high_ref[...], low_ref[...]
        space = product(field[take].reshape(size, 2 * LANES), high, low)
        space = space.reshape(block * PAIRS, 2, SLOTS, 2 * LANES)
        less = space[:, 0, :, :LANES], space[:, 0, :, LANES:]
        great = space[:, 1, :, :LANES], space[:, 1, :, LANES:]

        def bubble(first, other):
            real = first[0] * first[0] - first[1] * first[1]
            imag = 2.0 * first[0] * first[1]
            return -(real * other[0] + imag * other[1]), imag * other[0] - real * other[1]

        sigma = jnp.stack(
            [jnp.concatenate(bubble(less, great), -1), jnp.concatenate(bubble(great, less), -1)], 1
        )
        back = product(sigma.reshape(size, 2 * LANES), high, low)
        field[take] = back.reshape(block, PAIRS, 2 * SLOTS, 2 * LANES)

    @pl.loop(0, 2 * PAIRS)
    def _(s):
        comp, pair = s // PAIRS, s % PAIRS
        rows = pl.ds(pl.multiple_of(comp * SLOTS, SLOTS), SLOTS)
        values = [(field[n, pair, rows, spot(0)], field[n, pair, rows, spot(1)]) for n in range(ROWS)]
        values = [times(value, twist(n)) if n else value for n, value in enumerate(values)]
        for m, (real, imag) in enumerate(fourier(values)):
            field[m, pair, rows, spot(0)] = real
            field[m, pair, rows, spot(1)] = imag

    scale = weight[...]

    @pl.loop(0, ROWS)
    def _(m):
        def sigma(comp, a, c):
            rows = pl.ds(comp * SLOTS, SLOTS)
            return field[m, a * ORB + c, rows, spot(0)], field[m, a * ORB + c, rows, spot(1)]

        def given(comp, b, c):
            at = comp * 2 * PAIRS + b * ORB + c
            return green[m, at], green[m, at + PAIRS]

        def memory(a, b):
            real, imag = 0.0, 0.0
            for c in range(ORB):
                for comp in range(2):
                    left, right = sigma(comp, a, c), given(1 - comp, b, c)
                    term = left[0] * right[0] - left[1] * right[1]
                    cross = left[0] * right[1] + left[1] * right[0] if a != b else 0.0
                    real, imag = (real + term, imag + cross) if comp == 0 else (real - term, imag - cross)
            return real, imag

        results = [2.0 * memory(a, a)[0] for a in range(ORB)]
        for a, b in ((0, 1), (0, 2), (1, 2)):
            one, two = memory(a, b), memory(b, a)
            results += [one[0] + two[0], two[1] - one[1]]
        for i, result in enumerate(results):
            out[i, pl.ds(m, 1), :] = jnp.sum(result * scale, axis=0, keepdims=True)


def collide(green, weights, high, low, twiddle):
    return pl.pallas_call(
        kernel,
        out_shape=jax.ShapeDtypeStruct((PAIRS, ROWS, LANES), jnp.float32),
        in_specs=[pl.BlockSpec(memory_space=pltpu.VMEM)] * 5,
        out_specs=pl.BlockSpec(memory_space=pltpu.VMEM),
        scratch_shapes=[pltpu.VMEM((ROWS, PAIRS, 2 * SLOTS, 2 * LANES), jnp.float32)],
        compiler_params=pltpu.CompilerParams(vmem_limit_bytes=48 * 1024 * 1024),
    )(green, weights, high, low, twiddle)


def per_device(green_row, time_step):
    slot_count = green_row.shape[4]
    hist_count = lax.axis_size("hist")
    history = slot_count * hist_count
    slot_ids = (
        lax.axis_index("hist") * slot_count
        + lax.axis_index("mom") * SLOTS
        + jnp.arange(SLOTS, dtype=jnp.int32)
    )
    slot_age = (time_step[0] - 1 - slot_ids) % history + 1
    decays = jnp.exp2(-(slot_age - 1).astype(jnp.float32) / history)
    weights = delta_time * decays * jnp.where(slot_age == history, 0.5, 1.0).astype(jnp.float32)
    weights = jnp.broadcast_to(weights[:, None], (SLOTS, LANES))
    high, low, twiddle = lane_tables()

    parts = green_row.reshape(4 * PAIRS, ROWS, SLOTS, LANES)
    arrived = lax.all_to_all(parts, "mom", split_axis=1, concat_axis=0)
    partial = collide(arrived, weights, high, low, twiddle)
    flat = partial.reshape(PAIRS, ROWS * LANES)
    summed = lax.psum_scatter(flat, ("mom", "hist"), scatter_dimension=1, tiled=True)
    zero = jnp.zeros_like(summed[0])
    real = [summed[0], summed[3], summed[5], summed[3], summed[1], summed[7], summed[5], summed[7], summed[2]]
    imag = [zero, summed[4], summed[6], -summed[4], zero, summed[8], -summed[6], -summed[8], zero]
    return jnp.stack(real + imag).reshape(2, ORB, ORB, -1)


def solution(mesh):
    placed = (P(None, None, None, None, "hist", "mom"), P())
    return jax.shard_map(
        per_device,
        mesh=mesh,
        in_specs=placed,
        out_specs=P(None, None, None, ("mom", "hist")),
        check_vma=False,
    )
```

```python
import math

import jax
import jax.numpy as jnp
import numpy as np
from jax import lax
from jax.experimental import pallas as pl
from jax.experimental.pallas import tpu as pltpu
from jax.sharding import PartitionSpec as P

NKX = 64
NKY = 64
ORB = 3
PAIRS = ORB * ORB
ROWS = 32
SLOTS = 8
LANES = 128

delta_time = 0.01


def lane_tables():
    index = np.arange(64)
    angle = 2.0 * math.pi * (index[:, None] * index[None, :] % 64) / 64
    sign = np.array([[1.0, 1.0], [1.0, -1.0]])
    cosine = np.kron(sign, np.cos(angle)) / 64
    sine = np.kron(sign, np.sin(angle)) / 64
    table = np.block([[cosine, sine], [-sine, cosine]]).astype(np.float32)
    high = table.astype(jnp.bfloat16)
    low = (table - high.astype(np.float32)).astype(jnp.bfloat16)
    turn = 2.0 * math.pi * np.arange(ROWS)[:, None] * np.repeat([0, 1], 64)[None, :] / 64
    twiddle = np.stack([np.cos(turn), np.sin(turn)], 1).astype(np.float32)
    return high, low, twiddle


def turned(value, step, length):
    real, imag = value
    eighths = step * 8 / length
    if eighths == 0:
        return real, imag
    if eighths == 2:
        return -imag, real
    if eighths == 4:
        return -real, -imag
    if eighths == 6:
        return imag, -real
    root = math.sqrt(0.5)
    if eighths == 1:
        return root * (real - imag), root * (real + imag)
    if eighths == 3:
        return -root * (real + imag), root * (real - imag)
    if eighths == 5:
        return root * (imag - real), -root * (real + imag)
    if eighths == 7:
        return root * (real + imag), root * (imag - real)
    cosine, sine = math.cos(2 * math.pi * step / length), math.sin(2 * math.pi * step / length)
    return real * cosine - imag * sine, real * sine + imag * cosine


def plus(first, second):
    return first[0] + second[0], first[1] + second[1]


def minus(first, second):
    return first[0] - second[0], first[1] - second[1]


def fourier(values):
    length = len(values)
    if length == 1:
        return values
    if length == 2:
        return [plus(*values), minus(*values)]
    quarter = length // 4
    parts = [fourier(values[start::4]) for start in range(4)]
    out = [None] * length
    for m in range(quarter):
        first, second, third, fourth = (turned(parts[p][m], p * m, length) for p in range(4))
        even, odd = plus(first, third), minus(first, third)
        other, cross = plus(second, fourth), minus(second, fourth)
        cross = (-cross[1], cross[0])
        out[m], out[m + 2 * quarter] = plus(even, other), minus(even, other)
        out[m + quarter], out[m + 3 * quarter] = plus(odd, cross), minus(odd, cross)
    return out


def product(values, high, low):
    head = values.astype(jnp.bfloat16)
    tail = (values - head.astype(jnp.float32)).astype(jnp.bfloat16)

    def dot(left, right):
        return jnp.dot(left, right, preferred_element_type=jnp.float32)

    return dot(head, high) + (dot(tail, high) + dot(head, low))


def kernel(green, weight, high_ref, low_ref, twiddle, before, out, field):
    def spot(part):
        return pl.ds(part * LANES, LANES)

    def twist(n):
        return twiddle[n, 0][None, :], twiddle[n, 1][None, :]

    def times(value, factor):
        return value[0] * factor[0] - value[1] * factor[1], value[0] * factor[1] + value[1] * factor[0]

    @pl.loop(0, 2 * ORB)
    def _(s):
        comp, pair = s // ORB, s % ORB
        at = comp * 2 * ORB + pair
        rows = pl.ds(pl.multiple_of(comp * SLOTS, SLOTS), SLOTS)
        values = [(green[m, at], green[m, at + ORB]) for m in range(ROWS)]
        for n, value in enumerate(fourier(values)):
            real, imag = times(value, twist(n)) if n else value
            field[n, pair, rows, spot(0)] = real
            field[n, pair, rows, spot(1)] = imag

    block = 8
    size = block * ORB * 2 * SLOTS

    @pl.loop(0, ROWS // block)
    def _(b):
        take = pl.ds(b * block, block)
        high, low = high_ref[...], low_ref[...]
        space = product(field[take].reshape(size, 2 * LANES), high, low)
        space = space.reshape(block * ORB, 2, SLOTS, 2 * LANES)
        less = space[:, 0, :, :LANES], space[:, 0, :, LANES:]
        great = space[:, 1, :, :LANES], space[:, 1, :, LANES:]

        def bubble(first, other):
            real = first[0] * first[0] - first[1] * first[1]
            imag = 2.0 * first[0] * first[1]
            return -(real * other[0] + imag * other[1]), imag * other[0] - real * other[1]

        sigma = jnp.stack(
            [jnp.concatenate(bubble(less, great), -1), jnp.concatenate(bubble(great, less), -1)], 1
        )
        back = product(sigma.reshape(size, 2 * LANES), high, low)
        field[take] = back.reshape(block, ORB, 2 * SLOTS, 2 * LANES)

    @pl.loop(0, 2 * ORB)
    def _(s):
        comp, pair = s // ORB, s % ORB
        rows = pl.ds(pl.multiple_of(comp * SLOTS, SLOTS), SLOTS)
        values = [(field[n, pair, rows, spot(0)], field[n, pair, rows, spot(1)]) for n in range(ROWS)]
        values = [times(value, twist(n)) if n else value for n, value in enumerate(values)]
        for m, (real, imag) in enumerate(fourier(values)):
            field[m, pair, rows, spot(0)] = real
            field[m, pair, rows, spot(1)] = imag

    scale = weight[...]

    @pl.loop(0, ROWS)
    def _(m):
        def sigma(comp, a):
            rows = pl.ds(comp * SLOTS, SLOTS)
            return field[m, a, rows, spot(0)], field[m, a, rows, spot(1)]

        def given(comp, b):
            at = comp * 2 * ORB + b
            return green[m, at], green[m, at + ORB]

        def memory(a, b):
            left, right = sigma(0, a), given(1, b)
            other, cross = sigma(1, a), given(0, b)
            real = left[0] * right[0] - left[1] * right[1] - other[0] * cross[0] + other[1] * cross[1]
            if a == b:
                return real, None
            imag = left[0] * right[1] + left[1] * right[0] - other[0] * cross[1] - other[1] * cross[0]
            return real, imag

        results = [2.0 * memory(a, a)[0] for a in range(ORB)]
        for a, b in ((0, 1), (0, 2), (1, 2)):
            one, two = memory(a, b), memory(b, a)
            results += [one[0] + two[0], two[1] - one[1]]
        for i, result in enumerate(results):
            row = pl.ds(i, 1)
            out[m, row, :] = before[m, row, :] + jnp.sum(result * scale, axis=0, keepdims=True)


def collide(green, weights, high, low, twiddle, before):
    return pl.pallas_call(
        kernel,
        out_shape=jax.ShapeDtypeStruct((ROWS, PAIRS, LANES), jnp.float32),
        in_specs=[pl.BlockSpec(memory_space=pltpu.VMEM)] * 6,
        out_specs=pl.BlockSpec(memory_space=pltpu.VMEM),
        scratch_shapes=[pltpu.VMEM((ROWS, ORB, 2 * SLOTS, 2 * LANES), jnp.float32)],
        compiler_params=pltpu.CompilerParams(vmem_limit_bytes=24 * 1024 * 1024),
        cost_estimate=pl.CostEstimate(flops=2_000_000_000, bytes_accessed=4_000_000, transcendentals=0),
    )(green, weights, high, low, twiddle, before)


def per_device(green_row, time_step):
    slot_count = green_row.shape[4]
    hist_count = lax.axis_size("hist")
    history = slot_count * hist_count
    slot_ids = (
        lax.axis_index("hist") * slot_count
        + lax.axis_index("mom") * SLOTS
        + jnp.arange(SLOTS, dtype=jnp.int32)
    )
    slot_age = (time_step[0] - 1 - slot_ids) % history + 1
    decays = jnp.exp2(-(slot_age - 1).astype(jnp.float32) / history)
    weights = delta_time * decays * jnp.where(slot_age == history, 0.5, 1.0).astype(jnp.float32)
    weights = jnp.broadcast_to(weights[:, None], (SLOTS, LANES))
    high, low, twiddle = lane_tables()

    parts = green_row.reshape(4 * ORB, ORB, ROWS, SLOTS, LANES)
    arrived = [
        lax.all_to_all(parts[:, c], "mom", split_axis=1, concat_axis=0) for c in range(ORB)
    ]
    partial = jnp.zeros((ROWS, PAIRS, LANES), jnp.float32)
    for part in arrived:
        partial = collide(part, weights, high, low, twiddle, partial)
    owned = jnp.sum(lax.all_to_all(partial, "mom", split_axis=0, concat_axis=0), axis=0)
    shares = owned.reshape(PAIRS, hist_count, LANES // hist_count).transpose(1, 0, 2)
    summed = jnp.sum(lax.all_to_all(shares, "hist", split_axis=0, concat_axis=0), axis=0)
    zero = jnp.zeros_like(summed[0])
    real = [summed[0], summed[3], summed[5], summed[3], summed[1], summed[7], summed[5], summed[7], summed[2]]
    imag = [zero, summed[4], summed[6], -summed[4], zero, summed[8], -summed[6], -summed[8], zero]
    return jnp.stack(real + imag).reshape(2, ORB, ORB, -1)


def solution(mesh):
    placed = (P(None, None, None, None, "hist", "mom"), P())
    return jax.shard_map(
        per_device,
        mesh=mesh,
        in_specs=placed,
        out_specs=P(None, None, None, ("mom", "hist")),
        check_vma=False,
    )
```

```python
import functools
import math

import jax
import jax.numpy as jnp
import numpy as np
from jax import lax
from jax.experimental import pallas as pl
from jax.experimental.pallas import tpu as pltpu
from jax.sharding import Mesh
from jax.sharding import PartitionSpec as P

NKX = 64
NKY = 64
ORB = 3
PAIRS = ORB * ORB
ROWS = 32
PLANE = 16
SLOTS = 8
LANES = 128

delta_time = 0.01


def lane_tables():
    index = np.arange(64)
    angle = 2.0 * math.pi * (index[:, None] * index[None, :] % 64) / 64
    sign = np.array([[1.0, 1.0], [1.0, -1.0]])
    cosine = np.kron(sign, np.cos(angle)) / 64
    sine = np.kron(sign, np.sin(angle)) / 64
    table = np.block([[cosine, sine], [-sine, cosine]]).astype(np.float32)
    high = table.astype(jnp.bfloat16)
    low = (table - high.astype(np.float32)).astype(jnp.bfloat16)
    turn = 2.0 * math.pi * np.arange(ROWS)[:, None] * np.repeat([0, 1], 64)[None, :] / 64
    twiddle = np.stack([np.cos(turn), np.sin(turn)], 1).astype(np.float32)
    return high, low, twiddle


def turned(value, step, length):
    real, imag = value
    eighths = step * 8 / length
    if eighths == 0:
        return real, imag
    if eighths == 2:
        return -imag, real
    if eighths == 4:
        return -real, -imag
    if eighths == 6:
        return imag, -real
    root = math.sqrt(0.5)
    if eighths == 1:
        return root * (real - imag), root * (real + imag)
    if eighths == 3:
        return -root * (real + imag), root * (real - imag)
    if eighths == 5:
        return root * (imag - real), -root * (real + imag)
    if eighths == 7:
        return root * (real + imag), root * (imag - real)
    cosine, sine = math.cos(2 * math.pi * step / length), math.sin(2 * math.pi * step / length)
    return real * cosine - imag * sine, real * sine + imag * cosine


def plus(first, second):
    return first[0] + second[0], first[1] + second[1]


def minus(first, second):
    return first[0] - second[0], first[1] - second[1]


def fourier(values):
    length = len(values)
    if length == 1:
        return values
    if length == 2:
        return [plus(*values), minus(*values)]
    quarter = length // 4
    parts = [fourier(values[start::4]) for start in range(4)]
    out = [None] * length
    for m in range(quarter):
        first, second, third, fourth = (turned(parts[p][m], p * m, length) for p in range(4))
        even, odd = plus(first, third), minus(first, third)
        other, cross = plus(second, fourth), minus(second, fourth)
        cross = (-cross[1], cross[0])
        out[m], out[m + 2 * quarter] = plus(even, other), minus(even, other)
        out[m + quarter], out[m + 3 * quarter] = plus(odd, cross), minus(odd, cross)
    return out


def product(values, high, low):
    head = values.astype(jnp.bfloat16)
    tail = (values - head.astype(jnp.float32)).astype(jnp.bfloat16)

    def dot(left, right):
        return jnp.dot(left, right, preferred_element_type=jnp.float32)

    return dot(head, high) + (dot(tail, high) + dot(head, low))


def kernel(turn, *refs):
    *given_refs, weight, high_ref, low_ref, twiddle, before, out, field = refs
    straight = turn[0] == 0
    if len(given_refs) == 2:
        lower, upper = given_refs
    else:
        lower, upper = given_refs[0].at[:, 0], given_refs[0].at[:, 1]

    def green(m, at):
        plane, half = m // 8 * 4 + m % 4, m // 4 % 2
        one, two = lower[plane, at], upper[plane, at]
        return jnp.where(straight == (half == 0), one, two)

    def spot(part):
        return pl.ds(part * LANES, LANES)

    def twist(n):
        return twiddle[n, 0][None, :], twiddle[n, 1][None, :]

    def times(value, factor):
        return value[0] * factor[0] - value[1] * factor[1], value[0] * factor[1] + value[1] * factor[0]

    @pl.loop(0, 2 * ORB)
    def _(s):
        comp, pair = s // ORB, s % ORB
        at = comp * 2 * ORB + pair
        rows = pl.ds(pl.multiple_of(comp * SLOTS, SLOTS), SLOTS)
        values = [(green(m, at), green(m, at + ORB)) for m in range(ROWS)]
        for n, value in enumerate(fourier(values)):
            real, imag = times(value, twist(n)) if n else value
            field[n, pair, rows, spot(0)] = real
            field[n, pair, rows, spot(1)] = imag

    block = 8
    size = block * ORB * 2 * SLOTS

    @pl.loop(0, ROWS // block)
    def _(b):
        take = pl.ds(b * block, block)
        high, low = high_ref[...], low_ref[...]
        space = product(field[take].reshape(size, 2 * LANES), high, low)
        space = space.reshape(block * ORB, 2, SLOTS, 2 * LANES)
        less = space[:, 0, :, :LANES], space[:, 0, :, LANES:]
        great = space[:, 1, :, :LANES], space[:, 1, :, LANES:]

        def bubble(first, other):
            real = first[0] * first[0] - first[1] * first[1]
            imag = 2.0 * first[0] * first[1]
            return -(real * other[0] + imag * other[1]), imag * other[0] - real * other[1]

        sigma = jnp.stack(
            [jnp.concatenate(bubble(less, great), -1), jnp.concatenate(bubble(great, less), -1)], 1
        )
        back = product(sigma.reshape(size, 2 * LANES), high, low)
        field[take] = back.reshape(block, ORB, 2 * SLOTS, 2 * LANES)

    @pl.loop(0, 2 * ORB)
    def _(s):
        comp, pair = s // ORB, s % ORB
        rows = pl.ds(pl.multiple_of(comp * SLOTS, SLOTS), SLOTS)
        values = [(field[n, pair, rows, spot(0)], field[n, pair, rows, spot(1)]) for n in range(ROWS)]
        values = [times(value, twist(n)) if n else value for n, value in enumerate(values)]
        for m, (real, imag) in enumerate(fourier(values)):
            field[m, pair, rows, spot(0)] = real
            field[m, pair, rows, spot(1)] = imag

    scale = weight[...]

    @pl.loop(0, ROWS)
    def _(m):
        def sigma(comp, a):
            rows = pl.ds(comp * SLOTS, SLOTS)
            return field[m, a, rows, spot(0)], field[m, a, rows, spot(1)]

        def given(comp, b):
            at = comp * 2 * ORB + b
            return green(m, at), green(m, at + ORB)

        def memory(a, b):
            left, right = sigma(0, a), given(1, b)
            other, cross = sigma(1, a), given(0, b)
            real = left[0] * right[0] - left[1] * right[1] - other[0] * cross[0] + other[1] * cross[1]
            if a == b:
                return real, None
            imag = left[0] * right[1] + left[1] * right[0] - other[0] * cross[1] - other[1] * cross[0]
            return real, imag

        results = [2.0 * memory(a, a)[0] for a in range(ORB)]
        for a, b in ((0, 1), (0, 2), (1, 2)):
            one, two = memory(a, b), memory(b, a)
            results += [one[0] + two[0], two[1] - one[1]]
        for i, result in enumerate(results):
            spare, row = (m // 8 * 4 + m % 4) * 2 + m // 4 % 2, pl.ds(i, 1)
            out[spare, row, :] = before[spare, row, :] + jnp.sum(result * scale, axis=0, keepdims=True)


def collide(turn, fields, weights, high, low, twiddle, before):
    return pl.pallas_call(
        kernel,
        out_shape=jax.ShapeDtypeStruct((ROWS, PAIRS, LANES), jnp.float32),
        in_specs=[pl.BlockSpec(memory_space=pltpu.SMEM)] + [pl.BlockSpec(memory_space=pltpu.VMEM)] * (len(fields) + 5),
        out_specs=pl.BlockSpec(memory_space=pltpu.VMEM),
        scratch_shapes=[pltpu.VMEM((ROWS, ORB, 2 * SLOTS, 2 * LANES), jnp.float32)],
        compiler_params=pltpu.CompilerParams(vmem_limit_bytes=24 * 1024 * 1024),
        cost_estimate=pl.CostEstimate(flops=2_000_000_000, bytes_accessed=4_000_000, transcendentals=0),
    )(turn, *fields, weights, high, low, twiddle, before)


def arrange_kernel(c, apart, first, parts, *refs):
    *outs, sems = refs
    copies = []
    for n in range(2):
        half = first[0] if n == 0 else 1 - first[0]
        for at in range(4 * ORB):
            target = outs[n].at[:, at] if apart else outs[0].at[:, n, at]
            copies.append(pltpu.make_async_copy(parts.at[at, c, half], target, sems.at[n, at]))
    for copy in copies:
        copy.start()
    for copy in copies:
        copy.wait()


def arrange(first, parts, c, apart):
    whole = (PLANE, 4 * ORB, SLOTS, LANES) if apart else (PLANE, 2, 4 * ORB, SLOTS, LANES)
    shape = jax.ShapeDtypeStruct(whole, jnp.float32)
    return pl.pallas_call(
        functools.partial(arrange_kernel, c, apart),
        out_shape=[shape] * (2 if apart else 1),
        in_specs=[pl.BlockSpec(memory_space=pltpu.SMEM), pl.BlockSpec(memory_space=pl.ANY)],
        out_specs=[pl.BlockSpec(memory_space=pl.ANY)] * (2 if apart else 1),
        scratch_shapes=[pltpu.SemaphoreType.DMA((2, 4 * ORB))],
        cost_estimate=pl.CostEstimate(flops=0, bytes_accessed=3_200_000, transcendentals=0),
    )(first, parts)


def settle(fields, flops=100_000_000_000):
    count = len(fields)
    return pl.pallas_call(
        lambda *refs: None,
        out_shape=[jax.ShapeDtypeStruct(field.shape, field.dtype) for field in fields],
        in_specs=[pl.BlockSpec(memory_space=pl.ANY)] * count,
        out_specs=[pl.BlockSpec(memory_space=pl.ANY)] * count,
        input_output_aliases={n: n for n in range(count)},
        cost_estimate=pl.CostEstimate(flops=flops, bytes_accessed=0, transcendentals=0),
    )(*fields)


def shifted(step):
    return [(z, (z + step) % 8) for z in range(8)]


def per_device(green_row, time_step):
    slot_count = green_row.shape[4]
    history = slot_count * 8
    zh, zl, core = (lax.axis_index(axis) for axis in ("zh", "zl", "core"))
    plane = lax.axis_index("y") * 4 + lax.axis_index("x")
    turn = ((zh * 4 + zl + 2) // 4 + 1) % 2
    origin = (zl + 2) % 4 * 2 + core
    first = origin * slot_count + turn * (slot_count // 2) + plane * SLOTS
    slot_ids = first + jnp.arange(SLOTS, dtype=jnp.int32)
    slot_age = (time_step[0] - 1 - slot_ids) % history + 1
    decays = jnp.exp2(-(slot_age - 1).astype(jnp.float32) / history)
    weights = delta_time * decays * jnp.where(slot_age == history, 0.5, 1.0).astype(jnp.float32)
    weights = jnp.broadcast_to(weights[:, None], (SLOTS, LANES))
    high, low, twiddle = lane_tables()

    parts = green_row.reshape(4 * ORB, ORB, 2, PLANE, SLOTS, LANES)

    def spread(value):
        return lax.all_to_all(value, ("y", "x"), split_axis=0, concat_axis=0)

    def move(rising, falling):
        return (
            lax.ppermute(rising, ("zh", "zl"), shifted(2)),
            lax.ppermute(falling, ("zh", "zl"), shifted(-2)),
        )

    def work(fields, partial):
        return collide(turn_flag, fields, weights, high, low, twiddle, partial)

    turn_flag = turn.reshape(1).astype(jnp.int32)
    partial = jnp.zeros((ROWS, PAIRS, LANES), jnp.float32)
    fence = lax.optimization_barrier
    side = zh.reshape(1).astype(jnp.int32)
    zero = arrange(side, parts, 0, True)
    zero, side = fence((zero, side))
    zero = move(*zero)
    (one,) = arrange(side, parts, 1, False)
    one = spread(one)
    zero, one, side = fence((settle(zero), one, side))
    one = move(one[:, 0], one[:, 1])
    (two,) = arrange(side, parts, 2, False)
    two = spread(two)
    one, two = fence((settle(one), two))
    two = move(two[:, 0], two[:, 1])
    one, zero = fence((one, jnp.stack(zero, 1)))
    zero = spread(zero)
    partial = work(one, partial)
    partial = work([zero], partial)
    partial, two = fence((partial, two))
    partial = work(two, partial)

    blocks = partial.reshape(PLANE, 2, PAIRS, LANES)
    owned = jnp.sum(spread(blocks), axis=0)
    copies = jnp.broadcast_to(owned[:, None], (2, 8, PAIRS, LANES)).reshape(PLANE, PAIRS, LANES)
    copies = lax.all_to_all(copies, ("zh", "zl", "core"), split_axis=0, concat_axis=0)
    share = LANES // 8
    summed = lax.dynamic_slice_in_dim(jnp.sum(copies, axis=0), (zl * 2 + core) * share, share, 1)
    none = jnp.zeros_like(summed[0])
    real = [summed[0], summed[3], summed[5], summed[3], summed[1], summed[7], summed[5], summed[7], summed[2]]
    imag = [none, summed[4], summed[6], -summed[4], none, summed[8], -summed[6], -summed[8], none]
    return jnp.stack(real + imag).reshape(2, ORB, ORB, -1)


def solution(mesh):
    axes = ("y", "zh", "x", "zl", "core")
    finer = Mesh(mesh.devices.reshape(4, 2, 4, 4, 2), axes)
    mom, hist = axes[:3], axes[3:]
    return jax.shard_map(
        per_device,
        mesh=finer,
        in_specs=(P(None, None, None, None, hist, mom), P()),
        out_specs=P(None, None, None, axes),
        check_vma=False,
    )
```

```python
import functools
import math

import jax
import jax.numpy as jnp
import numpy as np
from jax import lax
from jax.experimental import pallas as pl
from jax.experimental.pallas import tpu as pltpu
from jax.sharding import Mesh
from jax.sharding import PartitionSpec as P

NKX = 64
NKY = 64
ORB = 3
PAIRS = ORB * ORB
ROWS = 32
PLANE = 16
SLOTS = 8
LANES = 128

delta_time = 0.01


def lane_tables():
    index = np.arange(64)
    angle = 2.0 * math.pi * (index[:, None] * index[None, :] % 64) / 64
    sign = np.array([[1.0, 1.0], [1.0, -1.0]])
    cosine = np.kron(sign, np.cos(angle)) / 64
    sine = np.kron(sign, np.sin(angle)) / 64
    table = np.block([[cosine, sine], [-sine, cosine]]).astype(np.float32)
    high = table.astype(jnp.bfloat16)
    low = (table - high.astype(np.float32)).astype(jnp.bfloat16)
    turn = 2.0 * math.pi * np.arange(ROWS)[:, None] * np.repeat([0, 1], 64)[None, :] / 64
    twiddle = np.stack([np.cos(turn), np.sin(turn)], 1).astype(np.float32)
    return high, low, twiddle


def turned(value, step, length):
    real, imag = value
    eighths = step * 8 / length
    if eighths == 0:
        return real, imag
    if eighths == 2:
        return -imag, real
    if eighths == 4:
        return -real, -imag
    if eighths == 6:
        return imag, -real
    root = math.sqrt(0.5)
    if eighths == 1:
        return root * (real - imag), root * (real + imag)
    if eighths == 3:
        return -root * (real + imag), root * (real - imag)
    if eighths == 5:
        return root * (imag - real), -root * (real + imag)
    if eighths == 7:
        return root * (real + imag), root * (imag - real)
    cosine, sine = math.cos(2 * math.pi * step / length), math.sin(2 * math.pi * step / length)
    return real * cosine - imag * sine, real * sine + imag * cosine


def plus(first, second):
    return first[0] + second[0], first[1] + second[1]


def minus(first, second):
    return first[0] - second[0], first[1] - second[1]


def fourier(values):
    length = len(values)
    if length == 1:
        return values
    if length == 2:
        return [plus(*values), minus(*values)]
    quarter = length // 4
    parts = [fourier(values[start::4]) for start in range(4)]
    out = [None] * length
    for m in range(quarter):
        first, second, third, fourth = (turned(parts[p][m], p * m, length) for p in range(4))
        even, odd = plus(first, third), minus(first, third)
        other, cross = plus(second, fourth), minus(second, fourth)
        cross = (-cross[1], cross[0])
        out[m], out[m + 2 * quarter] = plus(even, other), minus(even, other)
        out[m + quarter], out[m + 3 * quarter] = plus(odd, cross), minus(odd, cross)
    return out


def product(values, high, low):
    head = values.astype(jnp.bfloat16)
    tail = (values - head.astype(jnp.float32)).astype(jnp.bfloat16)

    def dot(left, right):
        return jnp.dot(left, right, preferred_element_type=jnp.float32)

    return dot(head, high) + (dot(tail, high) + dot(head, low))


def kernel(turn, *refs):
    *given_refs, weight, high_ref, low_ref, twiddle, before, out, field = refs
    straight = turn[0] == 0
    if len(given_refs) == 2:
        lower, upper = given_refs
    else:
        lower, upper = given_refs[0].at[:, 0], given_refs[0].at[:, 1]

    def green(m, at):
        plane, half = m // 8 * 4 + m % 4, m // 4 % 2
        one, two = lower[plane, at], upper[plane, at]
        return jnp.where(straight == (half == 0), one, two)

    def spot(part):
        return pl.ds(part * LANES, LANES)

    def twist(n):
        return twiddle[n, 0][None, :], twiddle[n, 1][None, :]

    def times(value, factor):
        return value[0] * factor[0] - value[1] * factor[1], value[0] * factor[1] + value[1] * factor[0]

    @pl.loop(0, 2 * ORB)
    def _(s):
        comp, pair = s // ORB, s % ORB
        at = comp * 2 * ORB + pair
        rows = pl.ds(pl.multiple_of(comp * SLOTS, SLOTS), SLOTS)
        values = [(green(m, at), green(m, at + ORB)) for m in range(ROWS)]
        for n, value in enumerate(fourier(values)):
            real, imag = times(value, twist(n)) if n else value
            field[n, pair, rows, spot(0)] = real
            field[n, pair, rows, spot(1)] = imag

    block = 8
    size = block * ORB * 2 * SLOTS

    @pl.loop(0, ROWS // block)
    def _(b):
        take = pl.ds(b * block, block)
        high, low = high_ref[...], low_ref[...]
        space = product(field[take].reshape(size, 2 * LANES), high, low)
        space = space.reshape(block * ORB, 2, SLOTS, 2 * LANES)
        less = space[:, 0, :, :LANES], space[:, 0, :, LANES:]
        great = space[:, 1, :, :LANES], space[:, 1, :, LANES:]

        def bubble(first, other):
            real = first[0] * first[0] - first[1] * first[1]
            imag = 2.0 * first[0] * first[1]
            return -(real * other[0] + imag * other[1]), imag * other[0] - real * other[1]

        sigma = jnp.stack(
            [jnp.concatenate(bubble(less, great), -1), jnp.concatenate(bubble(great, less), -1)], 1
        )
        back = product(sigma.reshape(size, 2 * LANES), high, low)
        field[take] = back.reshape(block, ORB, 2 * SLOTS, 2 * LANES)

    @pl.loop(0, 2 * ORB)
    def _(s):
        comp, pair = s // ORB, s % ORB
        rows = pl.ds(pl.multiple_of(comp * SLOTS, SLOTS), SLOTS)
        values = [(field[n, pair, rows, spot(0)], field[n, pair, rows, spot(1)]) for n in range(ROWS)]
        values = [times(value, twist(n)) if n else value for n, value in enumerate(values)]
        for m, (real, imag) in enumerate(fourier(values)):
            field[m, pair, rows, spot(0)] = real
            field[m, pair, rows, spot(1)] = imag

    scale = weight[...]

    @pl.loop(0, ROWS)
    def _(m):
        def sigma(comp, a):
            rows = pl.ds(comp * SLOTS, SLOTS)
            return field[m, a, rows, spot(0)], field[m, a, rows, spot(1)]

        def given(comp, b):
            at = comp * 2 * ORB + b
            return green(m, at), green(m, at + ORB)

        def memory(a, b):
            left, right = sigma(0, a), given(1, b)
            other, cross = sigma(1, a), given(0, b)
            real = left[0] * right[0] - left[1] * right[1] - other[0] * cross[0] + other[1] * cross[1]
            if a == b:
                return real, None
            imag = left[0] * right[1] + left[1] * right[0] - other[0] * cross[1] - other[1] * cross[0]
            return real, imag

        results = [2.0 * memory(a, a)[0] for a in range(ORB)]
        for a, b in ((0, 1), (0, 2), (1, 2)):
            one, two = memory(a, b), memory(b, a)
            results += [one[0] + two[0], two[1] - one[1]]
        for i, result in enumerate(results):
            spare, row = (m // 8 * 4 + m % 4) * 2 + m // 4 % 2, pl.ds(i, 1)
            out[spare, row, :] = before[spare, row, :] + jnp.sum(result * scale, axis=0, keepdims=True)


def collide(turn, fields, weights, high, low, twiddle, before):
    return pl.pallas_call(
        kernel,
        out_shape=jax.ShapeDtypeStruct((ROWS, PAIRS, LANES), jnp.float32),
        in_specs=[pl.BlockSpec(memory_space=pltpu.SMEM)] + [pl.BlockSpec(memory_space=pltpu.VMEM)] * (len(fields) + 5),
        out_specs=pl.BlockSpec(memory_space=pltpu.VMEM),
        scratch_shapes=[pltpu.VMEM((ROWS, ORB, 2 * SLOTS, 2 * LANES), jnp.float32)],
        compiler_params=pltpu.CompilerParams(vmem_limit_bytes=24 * 1024 * 1024),
        cost_estimate=pl.CostEstimate(flops=1000000000, bytes_accessed=0, transcendentals=0),
    )(turn, *fields, weights, high, low, twiddle, before)


def arrange_kernel(c, apart, first, parts, *refs):
    *outs, sems = refs
    copies = []
    for n in range(2):
        half = first[0] if n == 0 else 1 - first[0]
        for at in range(4 * ORB):
            target = outs[n].at[:, at] if apart else outs[0].at[:, n, at]
            copies.append(pltpu.make_async_copy(parts.at[at, c, half], target, sems.at[n, at]))
    for copy in copies:
        copy.start()
    for copy in copies:
        copy.wait()


def arrange(first, parts, c, apart):
    whole = (PLANE, 4 * ORB, SLOTS, LANES) if apart else (PLANE, 2, 4 * ORB, SLOTS, LANES)
    shape = jax.ShapeDtypeStruct(whole, jnp.float32)
    return pl.pallas_call(
        functools.partial(arrange_kernel, c, apart),
        out_shape=[shape] * (2 if apart else 1),
        in_specs=[pl.BlockSpec(memory_space=pltpu.SMEM), pl.BlockSpec(memory_space=pl.ANY)],
        out_specs=[pl.BlockSpec(memory_space=pltpu.VMEM)] * (2 if apart else 1),
        scratch_shapes=[pltpu.SemaphoreType.DMA((2, 4 * ORB))],
        compiler_params=pltpu.CompilerParams(vmem_limit_bytes=8 * 1024 * 1024),
        cost_estimate=pl.CostEstimate(flops=0, bytes_accessed=3_200_000, transcendentals=0),
    )(first, parts)


def settle(weights, fields, cost):
    def body(given, one, two, out):
        out[...] = given[...]

    return pl.pallas_call(
        body,
        out_shape=jax.ShapeDtypeStruct((SLOTS, LANES), jnp.float32),
        in_specs=[pl.BlockSpec(memory_space=pltpu.VMEM)] * 3,
        out_specs=pl.BlockSpec(memory_space=pltpu.VMEM),
        cost_estimate=pl.CostEstimate(flops=int(cost * 1e9), bytes_accessed=0, transcendentals=0),
    )(weights, *(field[0, 0] for field in fields))


def shifted(step):
    return [(z, (z + step) % 8) for z in range(8)]


def per_device(green_row, time_step):
    slot_count = green_row.shape[4]
    history = slot_count * 8
    zh, zl, core = (lax.axis_index(axis) for axis in ("zh", "zl", "core"))
    plane = lax.axis_index("y") * 4 + lax.axis_index("x")
    turn = ((zh * 4 + zl + 2) // 4 + 1) % 2
    origin = (zl + 2) % 4 * 2 + core
    first = origin * slot_count + turn * (slot_count // 2) + plane * SLOTS
    slot_ids = first + jnp.arange(SLOTS, dtype=jnp.int32)
    slot_age = (time_step[0] - 1 - slot_ids) % history + 1
    decays = jnp.exp2(-(slot_age - 1).astype(jnp.float32) / history)
    weights = delta_time * decays * jnp.where(slot_age == history, 0.5, 1.0).astype(jnp.float32)
    weights = jnp.broadcast_to(weights[:, None], (SLOTS, LANES))
    high, low, twiddle = lane_tables()

    parts = green_row.reshape(4 * ORB, ORB, 2, PLANE, SLOTS, LANES)

    def spread(value):
        return lax.all_to_all(value, ("y", "x"), split_axis=0, concat_axis=0)

    def move(rising, falling):
        return (
            lax.ppermute(rising, ("zh", "zl"), shifted(2)),
            lax.ppermute(falling, ("zh", "zl"), shifted(-2)),
        )

    def work(fields, partial, weights):
        return collide(turn_flag, fields, weights, high, low, twiddle, partial)

    turn_flag = turn.reshape(1).astype(jnp.int32)
    partial = jnp.zeros((ROWS, PAIRS, LANES), jnp.float32)
    fence = lax.optimization_barrier
    side = zh.reshape(1).astype(jnp.int32)
    zero = arrange(side, parts, 0, True)
    zero, side = fence((zero, side))
    zero = move(*zero)
    (one,) = arrange(side, parts, 1, False)
    one, side = fence((spread(one), side))
    (two,) = arrange(side, parts, 2, False)
    two = spread(two)
    one, two = (one[:, 0], one[:, 1]), (two[:, 0], two[:, 1])
    zero, one, weights = fence((zero, one, settle(weights, zero, 0.0)))
    one = move(*one)
    zero, two = fence((jnp.stack(zero, 1), two))
    zero = spread(zero)
    one, two, weights = fence((one, two, settle(weights, one, 0.0)))
    two = move(*two)
    partial = work(one, partial, weights)
    partial = work([zero], partial, weights)
    partial, two = fence((partial, two))
    partial = work(two, partial, weights)

    blocks = partial.reshape(PLANE, 2, PAIRS, LANES)
    owned = jnp.sum(spread(blocks), axis=0)
    share = LANES // 8
    shares = owned.reshape(2, PAIRS, 8, share).transpose(0, 2, 1, 3).reshape(PLANE, 1, PAIRS * share)
    shares = lax.all_to_all(shares, ("zh", "zl", "core"), split_axis=0, concat_axis=0)
    summed = jnp.sum(shares, axis=(0, 1)).reshape(PAIRS, share)
    none = jnp.zeros_like(summed[0])
    real = [summed[0], summed[3], summed[5], summed[3], summed[1], summed[7], summed[5], summed[7], summed[2]]
    imag = [none, summed[4], summed[6], -summed[4], none, summed[8], -summed[6], -summed[8], none]
    return jnp.stack(real + imag).reshape(2, ORB, ORB, -1)


def solution(mesh):
    axes = ("y", "zh", "x", "zl", "core")
    finer = Mesh(mesh.devices.reshape(4, 2, 4, 4, 2), axes)
    mom, hist = axes[:3], axes[3:]
    return jax.shard_map(
        per_device,
        mesh=finer,
        in_specs=(P(None, None, None, None, hist, mom), P()),
        out_specs=P(None, None, None, axes),
        check_vma=False,
    )
```

```python
import functools
import math

import jax
import jax.numpy as jnp
import numpy as np
from jax import lax
from jax.experimental import pallas as pl
from jax.experimental.pallas import tpu as pltpu
from jax.sharding import Mesh
from jax.sharding import PartitionSpec as P

NKX = 64
NKY = 64
ORB = 3
PAIRS = ORB * ORB
ROWS = 32
PLANE = 16
SLOTS = 8
LANES = 128

delta_time = 0.01


def lane_tables():
    index = np.arange(64)
    angle = 2.0 * math.pi * (index[:, None] * index[None, :] % 64) / 64
    sign = np.array([[1.0, 1.0], [1.0, -1.0]])
    cosine = np.kron(sign, np.cos(angle)) / 64
    sine = np.kron(sign, np.sin(angle)) / 64
    table = np.block([[cosine, sine], [-sine, cosine]]).astype(np.float32)
    high = table.astype(jnp.bfloat16)
    low = (table - high.astype(np.float32)).astype(jnp.bfloat16)
    turn = 2.0 * math.pi * np.arange(ROWS)[:, None] * np.repeat([0, 1], 64)[None, :] / 64
    twiddle = np.stack([np.cos(turn), np.sin(turn)], 1).astype(np.float32)
    return high, low, twiddle


def turned(value, step, length):
    real, imag = value
    eighths = step * 8 / length
    if eighths == 0:
        return real, imag
    if eighths == 2:
        return -imag, real
    if eighths == 4:
        return -real, -imag
    if eighths == 6:
        return imag, -real
    root = math.sqrt(0.5)
    if eighths == 1:
        return root * (real - imag), root * (real + imag)
    if eighths == 3:
        return -root * (real + imag), root * (real - imag)
    if eighths == 5:
        return root * (imag - real), -root * (real + imag)
    if eighths == 7:
        return root * (real + imag), root * (imag - real)
    cosine, sine = math.cos(2 * math.pi * step / length), math.sin(2 * math.pi * step / length)
    return real * cosine - imag * sine, real * sine + imag * cosine


def plus(first, second):
    return first[0] + second[0], first[1] + second[1]


def minus(first, second):
    return first[0] - second[0], first[1] - second[1]


def fourier(values):
    length = len(values)
    if length == 1:
        return values
    if length == 2:
        return [plus(*values), minus(*values)]
    quarter = length // 4
    parts = [fourier(values[start::4]) for start in range(4)]
    out = [None] * length
    for m in range(quarter):
        first, second, third, fourth = (turned(parts[p][m], p * m, length) for p in range(4))
        even, odd = plus(first, third), minus(first, third)
        other, cross = plus(second, fourth), minus(second, fourth)
        cross = (-cross[1], cross[0])
        out[m], out[m + 2 * quarter] = plus(even, other), minus(even, other)
        out[m + quarter], out[m + 3 * quarter] = plus(odd, cross), minus(odd, cross)
    return out


def product(values, high, low):
    head = values.astype(jnp.bfloat16)
    tail = (values - head.astype(jnp.float32)).astype(jnp.bfloat16)

    def dot(left, right):
        return jnp.dot(left, right, preferred_element_type=jnp.float32)

    return dot(head, high) + (dot(tail, high) + dot(head, low))


def kernel(turn, *refs):
    *given_refs, weight, high_ref, low_ref, twiddle, before, out, field = refs
    straight = turn[0] == 0
    if len(given_refs) == 2:
        lower, upper = given_refs
    else:
        lower, upper = given_refs[0].at[:, 0], given_refs[0].at[:, 1]

    def green(m, at):
        plane, half = m // 8 * 4 + m % 4, m // 4 % 2
        one, two = lower[plane, at], upper[plane, at]
        return jnp.where(straight == (half == 0), one, two)

    def spot(part):
        return pl.ds(part * LANES, LANES)

    def twist(n):
        return twiddle[n, 0][None, :], twiddle[n, 1][None, :]

    def times(value, factor):
        return value[0] * factor[0] - value[1] * factor[1], value[0] * factor[1] + value[1] * factor[0]

    @pl.loop(0, 2 * ORB)
    def _(s):
        comp, pair = s // ORB, s % ORB
        at = comp * 2 * ORB + pair
        rows = pl.ds(pl.multiple_of(comp * SLOTS, SLOTS), SLOTS)
        values = [(green(m, at), green(m, at + ORB)) for m in range(ROWS)]
        for n, value in enumerate(fourier(values)):
            real, imag = times(value, twist(n)) if n else value
            field[n, pair, rows, spot(0)] = real
            field[n, pair, rows, spot(1)] = imag

    block = 8
    size = block * ORB * 2 * SLOTS

    @pl.loop(0, ROWS // block)
    def _(b):
        take = pl.ds(b * block, block)
        high, low = high_ref[...], low_ref[...]
        space = product(field[take].reshape(size, 2 * LANES), high, low)
        space = space.reshape(block * ORB, 2, SLOTS, 2 * LANES)
        less = space[:, 0, :, :LANES], space[:, 0, :, LANES:]
        great = space[:, 1, :, :LANES], space[:, 1, :, LANES:]

        def bubble(first, other):
            real = first[0] * first[0] - first[1] * first[1]
            imag = 2.0 * first[0] * first[1]
            return -(real * other[0] + imag * other[1]), imag * other[0] - real * other[1]

        sigma = jnp.stack(
            [jnp.concatenate(bubble(less, great), -1), jnp.concatenate(bubble(great, less), -1)], 1
        )
        back = product(sigma.reshape(size, 2 * LANES), high, low)
        field[take] = back.reshape(block, ORB, 2 * SLOTS, 2 * LANES)

    @pl.loop(0, 2 * ORB)
    def _(s):
        comp, pair = s // ORB, s % ORB
        rows = pl.ds(pl.multiple_of(comp * SLOTS, SLOTS), SLOTS)
        values = [(field[n, pair, rows, spot(0)], field[n, pair, rows, spot(1)]) for n in range(ROWS)]
        values = [times(value, twist(n)) if n else value for n, value in enumerate(values)]
        for m, (real, imag) in enumerate(fourier(values)):
            field[m, pair, rows, spot(0)] = real
            field[m, pair, rows, spot(1)] = imag

    scale = weight[...]

    @pl.loop(0, ROWS)
    def _(m):
        def sigma(comp, a):
            rows = pl.ds(comp * SLOTS, SLOTS)
            return field[m, a, rows, spot(0)], field[m, a, rows, spot(1)]

        def given(comp, b):
            at = comp * 2 * ORB + b
            return green(m, at), green(m, at + ORB)

        def memory(a, b):
            left, right = sigma(0, a), given(1, b)
            other, cross = sigma(1, a), given(0, b)
            real = left[0] * right[0] - left[1] * right[1] - other[0] * cross[0] + other[1] * cross[1]
            if a == b:
                return real, None
            imag = left[0] * right[1] + left[1] * right[0] - other[0] * cross[1] - other[1] * cross[0]
            return real, imag

        results = [2.0 * memory(a, a)[0] for a in range(ORB)]
        for a, b in ((0, 1), (0, 2), (1, 2)):
            one, two = memory(a, b), memory(b, a)
            results += [one[0] + two[0], two[1] - one[1]]
        for i, result in enumerate(results):
            spare, row = (m // 8 * 4 + m % 4) * 2 + m // 4 % 2, pl.ds(i, 1)
            out[spare, row, :] = before[spare, row, :] + jnp.sum(result * scale, axis=0, keepdims=True)


def collide(turn, fields, weights, high, low, twiddle, before):
    return pl.pallas_call(
        kernel,
        out_shape=jax.ShapeDtypeStruct((ROWS, PAIRS, LANES), jnp.float32),
        in_specs=[pl.BlockSpec(memory_space=pltpu.SMEM)] + [pl.BlockSpec(memory_space=pltpu.VMEM)] * (len(fields) + 5),
        out_specs=pl.BlockSpec(memory_space=pltpu.VMEM),
        scratch_shapes=[pltpu.VMEM((ROWS, ORB, 2 * SLOTS, 2 * LANES), jnp.float32)],
        compiler_params=pltpu.CompilerParams(vmem_limit_bytes=24 * 1024 * 1024),
        cost_estimate=pl.CostEstimate(flops=1000000000, bytes_accessed=0, transcendentals=0),
    )(turn, *fields, weights, high, low, twiddle, before)


def arrange_kernel(c, apart, first, parts, *refs):
    *outs, sems = refs
    copies = []
    for n in range(2):
        half = first[0] if n == 0 else 1 - first[0]
        for at in range(4 * ORB):
            target = outs[n].at[:, at] if apart else outs[0].at[:, n, at]
            copies.append(pltpu.make_async_copy(parts.at[at, c, half], target, sems.at[n, at]))
    for copy in copies:
        copy.start()
    for copy in copies:
        copy.wait()


def arrange(first, parts, c, apart):
    whole = (PLANE, 4 * ORB, SLOTS, LANES) if apart else (PLANE, 2, 4 * ORB, SLOTS, LANES)
    shape = jax.ShapeDtypeStruct(whole, jnp.float32)
    return pl.pallas_call(
        functools.partial(arrange_kernel, c, apart),
        out_shape=[shape] * (2 if apart else 1),
        in_specs=[pl.BlockSpec(memory_space=pltpu.SMEM), pl.BlockSpec(memory_space=pltpu.HBM)],
        out_specs=[pl.BlockSpec(memory_space=pltpu.VMEM)] * (2 if apart else 1),
        scratch_shapes=[pltpu.SemaphoreType.DMA((2, 4 * ORB))],
        compiler_params=pltpu.CompilerParams(vmem_limit_bytes=60 * 1024 * 1024),
        cost_estimate=pl.CostEstimate(flops=0, bytes_accessed=3_200_000, transcendentals=0),
    )(first, parts)


def settle(weights, fields, cost):
    def body(given, *refs):
        refs[-1][...] = given[...]

    return pl.pallas_call(
        body,
        out_shape=jax.ShapeDtypeStruct((SLOTS, LANES), jnp.float32),
        in_specs=[pl.BlockSpec(memory_space=pltpu.VMEM)] + [pl.BlockSpec(memory_space=pl.ANY)] * len(fields),
        out_specs=pl.BlockSpec(memory_space=pltpu.VMEM),
        compiler_params=pltpu.CompilerParams(vmem_limit_bytes=1024 * 1024),
        cost_estimate=pl.CostEstimate(flops=int(cost * 1e9), bytes_accessed=0, transcendentals=0),
    )(weights, *fields)


def shifted(step):
    return [(z, (z + step) % 8) for z in range(8)]


def per_device(green_row, time_step):
    slot_count = green_row.shape[4]
    history = slot_count * 8
    zh, zl, core = (lax.axis_index(axis) for axis in ("zh", "zl", "core"))
    plane = lax.axis_index("y") * 4 + lax.axis_index("x")
    turn = ((zh * 4 + zl + 2) // 4 + 1) % 2
    origin = (zl + 2) % 4 * 2 + core
    first = origin * slot_count + turn * (slot_count // 2) + plane * SLOTS
    slot_ids = first + jnp.arange(SLOTS, dtype=jnp.int32)
    slot_age = (time_step[0] - 1 - slot_ids) % history + 1
    decays = jnp.exp2(-(slot_age - 1).astype(jnp.float32) / history)
    weights = delta_time * decays * jnp.where(slot_age == history, 0.5, 1.0).astype(jnp.float32)
    weights = jnp.broadcast_to(weights[:, None], (SLOTS, LANES))
    high, low, twiddle = lane_tables()

    parts = green_row.reshape(4 * ORB, ORB, 2, PLANE, SLOTS, LANES)

    def spread(value):
        return lax.all_to_all(value, ("y", "x"), split_axis=0, concat_axis=0)

    def move(rising, falling):
        return (
            lax.ppermute(rising, ("zh", "zl"), shifted(2)),
            lax.ppermute(falling, ("zh", "zl"), shifted(-2)),
        )

    def work(fields, partial, weights):
        return collide(turn_flag, fields, weights, high, low, twiddle, partial)

    turn_flag = turn.reshape(1).astype(jnp.int32)
    partial = jnp.zeros((ROWS, PAIRS, LANES), jnp.float32)
    fence = lax.optimization_barrier
    side = zh.reshape(1).astype(jnp.int32)
    zero = arrange(side, parts, 0, True)
    zero, side = fence((zero, side))
    zero = tuple(move(*zero))
    (one,) = arrange(side, parts, 1, False)
    one, side = fence((spread(one), side))
    (two,) = arrange(side, parts, 2, False)
    two = spread(two)
    one, two = tuple(fence((one[:, 0], one[:, 1]))), tuple(fence((two[:, 0], two[:, 1])))
    zero, one, weights = fence((zero, one, settle(weights, zero + one, 6.0)))
    one = tuple(move(*one))
    zero, two = fence((jnp.stack(zero, 1), two))
    zero = spread(zero)
    one, two, weights = fence((one, two, settle(weights, one + two, 6.0)))
    two = move(*two)
    partial = work(one, partial, weights)
    partial = work([zero], partial, weights)
    partial, two = fence((partial, two))
    partial = work(two, partial, weights)

    blocks = partial.reshape(PLANE, 2, PAIRS, LANES)
    owned = jnp.sum(spread(blocks), axis=0)
    share = LANES // 8
    shares = owned.reshape(2, PAIRS, 8, share).transpose(0, 2, 1, 3).reshape(PLANE, 1, PAIRS * share)
    shares = lax.all_to_all(shares, ("zh", "zl", "core"), split_axis=0, concat_axis=0)
    summed = jnp.sum(shares, axis=(0, 1)).reshape(PAIRS, share)
    none = jnp.zeros_like(summed[0])
    real = [summed[0], summed[3], summed[5], summed[3], summed[1], summed[7], summed[5], summed[7], summed[2]]
    imag = [none, summed[4], summed[6], -summed[4], none, summed[8], -summed[6], -summed[8], none]
    return jnp.stack(real + imag).reshape(2, ORB, ORB, -1)


def solution(mesh):
    axes = ("y", "zh", "x", "zl", "core")
    finer = Mesh(mesh.devices.reshape(4, 2, 4, 4, 2), axes)
    mom, hist = axes[:3], axes[3:]
    return jax.shard_map(
        per_device,
        mesh=finer,
        in_specs=(P(None, None, None, None, hist, mom), P()),
        out_specs=P(None, None, None, axes),
        check_vma=False,
    )
```

```python
import functools
import math

import jax
import jax.numpy as jnp
import numpy as np
from jax import lax
from jax.experimental import pallas as pl
from jax.experimental.pallas import tpu as pltpu
from jax.sharding import Mesh
from jax.sharding import PartitionSpec as P

NKX = 64
NKY = 64
ORB = 3
PAIRS = ORB * ORB
ROWS = 32
PLANE = 16
SLOTS = 8
LANES = 128

delta_time = 0.01


def lane_tables():
    index = np.arange(64)
    angle = 2.0 * math.pi * (index[:, None] * index[None, :] % 64) / 64
    sign = np.array([[1.0, 1.0], [1.0, -1.0]])
    cosine = np.kron(sign, np.cos(angle)) / 64
    sine = np.kron(sign, np.sin(angle)) / 64
    table = np.block([[cosine, sine], [-sine, cosine]]).astype(np.float32)
    high = table.astype(jnp.bfloat16)
    low = (table - high.astype(np.float32)).astype(jnp.bfloat16)
    turn = 2.0 * math.pi * np.arange(ROWS)[:, None] * np.repeat([0, 1], 64)[None, :] / 64
    twiddle = np.stack([np.cos(turn), np.sin(turn)], 1).astype(np.float32)
    return high, low, twiddle


def turned(value, step, length):
    real, imag = value
    eighths = step * 8 / length
    if eighths == 0:
        return real, imag
    if eighths == 2:
        return -imag, real
    if eighths == 4:
        return -real, -imag
    if eighths == 6:
        return imag, -real
    root = math.sqrt(0.5)
    if eighths == 1:
        return root * (real - imag), root * (real + imag)
    if eighths == 3:
        return -root * (real + imag), root * (real - imag)
    if eighths == 5:
        return root * (imag - real), -root * (real + imag)
    if eighths == 7:
        return root * (real + imag), root * (imag - real)
    cosine, sine = math.cos(2 * math.pi * step / length), math.sin(2 * math.pi * step / length)
    return real * cosine - imag * sine, real * sine + imag * cosine


def plus(first, second):
    return first[0] + second[0], first[1] + second[1]


def minus(first, second):
    return first[0] - second[0], first[1] - second[1]


def fourier(values):
    length = len(values)
    if length == 1:
        return values
    if length == 2:
        return [plus(*values), minus(*values)]
    quarter = length // 4
    parts = [fourier(values[start::4]) for start in range(4)]
    out = [None] * length
    for m in range(quarter):
        first, second, third, fourth = (turned(parts[p][m], p * m, length) for p in range(4))
        even, odd = plus(first, third), minus(first, third)
        other, cross = plus(second, fourth), minus(second, fourth)
        cross = (-cross[1], cross[0])
        out[m], out[m + 2 * quarter] = plus(even, other), minus(even, other)
        out[m + quarter], out[m + 3 * quarter] = plus(odd, cross), minus(odd, cross)
    return out


def product(values, high, low):
    head = values.astype(jnp.bfloat16)
    tail = (values - head.astype(jnp.float32)).astype(jnp.bfloat16)

    def dot(left, right):
        return jnp.dot(left, right, preferred_element_type=jnp.float32)

    return dot(head, high) + (dot(tail, high) + dot(head, low))


def kernel(count, stacked, joined, spilled, turn, *refs):
    refs = list(refs)
    if stacked:
        whole = refs.pop(0)
        lower, upper = whole.at[:, 0], whole.at[:, 1]
    else:
        lower, upper = refs.pop(0), refs.pop(0)
    if joined:
        older, older_sigma = refs.pop(0), refs.pop(0)
    weight, high_ref, low_ref, twiddle, before, out = refs[:6]
    field = refs[-1]
    straight = turn[0] == 0

    def choose(one, two, m, at):
        plane, half = m // 8 * 4 + m % 4, m // 4 % 2
        return jnp.where(straight == (half == 0), one[plane, at], two[plane, at])

    def pair_of(one, two, pairs, m, comp, pair):
        at = comp * 2 * pairs + pair
        return choose(one, two, m, at), choose(one, two, m, at + pairs)

    def spot(part):
        return pl.ds(part * LANES, LANES)

    def twist(n):
        return twiddle[n, 0][None, :], twiddle[n, 1][None, :]

    def times(value, factor):
        return value[0] * factor[0] - value[1] * factor[1], value[0] * factor[1] + value[1] * factor[0]

    @pl.loop(0, 2 * count)
    def _(s):
        comp, pair = s // count, s % count
        rows = pl.ds(pl.multiple_of(comp * SLOTS, SLOTS), SLOTS)
        values = [pair_of(lower, upper, count, m, comp, pair) for m in range(ROWS)]
        for n, value in enumerate(fourier(values)):
            real, imag = times(value, twist(n)) if n else value
            field[n, pair, rows, spot(0)] = real
            field[n, pair, rows, spot(1)] = imag

    block = 8
    size = block * count * 2 * SLOTS

    @pl.loop(0, ROWS // block)
    def _(b):
        take = pl.ds(b * block, block)
        high, low = high_ref[...], low_ref[...]
        space = product(field[take].reshape(size, 2 * LANES), high, low)
        space = space.reshape(block * count, 2, SLOTS, 2 * LANES)
        less = space[:, 0, :, :LANES], space[:, 0, :, LANES:]
        great = space[:, 1, :, :LANES], space[:, 1, :, LANES:]

        def bubble(first, other):
            real = first[0] * first[0] - first[1] * first[1]
            imag = 2.0 * first[0] * first[1]
            return -(real * other[0] + imag * other[1]), imag * other[0] - real * other[1]

        sigma = jnp.stack(
            [jnp.concatenate(bubble(less, great), -1), jnp.concatenate(bubble(great, less), -1)], 1
        )
        back = product(sigma.reshape(size, 2 * LANES), high, low)
        field[take] = back.reshape(block, count, 2 * SLOTS, 2 * LANES)

    @pl.loop(0, 2 * count)
    def _(s):
        comp, pair = s // count, s % count
        rows = pl.ds(pl.multiple_of(comp * SLOTS, SLOTS), SLOTS)
        values = [(field[n, pair, rows, spot(0)], field[n, pair, rows, spot(1)]) for n in range(ROWS)]
        values = [times(value, twist(n)) if n else value for n, value in enumerate(values)]
        for m, (real, imag) in enumerate(fourier(values)):
            field[m, pair, rows, spot(0)] = real
            field[m, pair, rows, spot(1)] = imag

    scale = weight[...]

    @pl.loop(0, ROWS)
    def _(m):
        def sigma(comp, a):
            rows = pl.ds(comp * SLOTS, SLOTS)
            if joined and a == 0:
                return older_sigma[m, rows, spot(0)], older_sigma[m, rows, spot(1)]
            return field[m, a - joined, rows, spot(0)], field[m, a - joined, rows, spot(1)]

        def given(comp, b):
            if joined and b == 0:
                return pair_of(older.at[:, 0], older.at[:, 1], ORB + 1, m, comp, ORB)
            return pair_of(lower, upper, count, m, comp, b - joined)

        def memory(a, b):
            left, right = sigma(0, a), given(1, b)
            other, cross = sigma(1, a), given(0, b)
            real = left[0] * right[0] - left[1] * right[1] - other[0] * cross[0] + other[1] * cross[1]
            if a == b:
                return real, None
            imag = left[0] * right[1] + left[1] * right[0] - other[0] * cross[1] - other[1] * cross[0]
            return real, imag

        results = [2.0 * memory(a, a)[0] for a in range(ORB)]
        for a, b in ((0, 1), (0, 2), (1, 2)):
            one, two = memory(a, b), memory(b, a)
            results += [one[0] + two[0], two[1] - one[1]]
        for i, result in enumerate(results):
            spare, row = (m // 8 * 4 + m % 4) * 2 + m // 4 % 2, pl.ds(i, 1)
            out[spare, row, :] = before[spare, row, :] + jnp.sum(result * scale, axis=0, keepdims=True)
        if spilled:
            refs[6][m] = field[m, ORB]


def collide(turn, fields, weights, high, low, twiddle, before, older=(), spilled=False):
    stacked, joined = len(fields) == 1, int(len(older) > 0)
    count = ORB + 1 if stacked else ORB - joined
    shapes = [jax.ShapeDtypeStruct((ROWS, PAIRS, LANES), jnp.float32)]
    if spilled:
        shapes.append(jax.ShapeDtypeStruct((ROWS, 2 * SLOTS, 2 * LANES), jnp.float32))
    inputs = (*fields, *older, weights, high, low, twiddle, before)
    return pl.pallas_call(
        functools.partial(kernel, count, stacked, joined, spilled),
        out_shape=shapes,
        in_specs=[pl.BlockSpec(memory_space=pltpu.SMEM)]
        + [pl.BlockSpec(memory_space=pltpu.VMEM)] * len(inputs),
        out_specs=[pl.BlockSpec(memory_space=pltpu.VMEM)] * len(shapes),
        scratch_shapes=[pltpu.VMEM((ROWS, count, 2 * SLOTS, 2 * LANES), jnp.float32)],
        compiler_params=pltpu.CompilerParams(vmem_limit_bytes=24 * 1024 * 1024),
        cost_estimate=pl.CostEstimate(flops=1000000000, bytes_accessed=0, transcendentals=0),
    )(turn, *inputs)


def arrange_kernel(blocks, apart, first, parts, *refs):
    *outs, sems = refs
    copies, base = [], 0
    for pairs in blocks:
        for kind in range(4):
            for i, (a, c) in enumerate(pairs):
                at = base + kind * len(pairs) + i
                for n in range(2):
                    half = first[0] if n == 0 else 1 - first[0]
                    target = outs[n].at[:, at] if apart else outs[0].at[:, n, at]
                    source = parts.at[kind * ORB + a, c, half]
                    copies.append(pltpu.make_async_copy(source, target, sems.at[n, at]))
        base += 4 * len(pairs)
    for copy in copies:
        copy.start()
    for copy in copies:
        copy.wait()


def arrange(first, parts, blocks, apart):
    count = 4 * sum(len(pairs) for pairs in blocks)
    whole = (PLANE, count, SLOTS, LANES) if apart else (PLANE, 2, count, SLOTS, LANES)
    shape = jax.ShapeDtypeStruct(whole, jnp.float32)
    return pl.pallas_call(
        functools.partial(arrange_kernel, blocks, apart),
        out_shape=[shape] * (2 if apart else 1),
        in_specs=[pl.BlockSpec(memory_space=pltpu.SMEM), pl.BlockSpec(memory_space=pl.ANY)],
        out_specs=[pl.BlockSpec(memory_space=pltpu.VMEM)] * (2 if apart else 1),
        scratch_shapes=[pltpu.SemaphoreType.DMA((2, count))],
        compiler_params=pltpu.CompilerParams(vmem_limit_bytes=60 * 1024 * 1024),
        cost_estimate=pl.CostEstimate(flops=0, bytes_accessed=3_200_000, transcendentals=0),
    )(first, parts)


def settle(weights, fields, cost):
    def body(given, *refs):
        refs[-1][...] = given[...]

    return pl.pallas_call(
        body,
        out_shape=jax.ShapeDtypeStruct((SLOTS, LANES), jnp.float32),
        in_specs=[pl.BlockSpec(memory_space=pltpu.VMEM)] + [pl.BlockSpec(memory_space=pl.ANY)] * len(fields),
        out_specs=pl.BlockSpec(memory_space=pltpu.VMEM),
        compiler_params=pltpu.CompilerParams(vmem_limit_bytes=1024 * 1024),
        cost_estimate=pl.CostEstimate(flops=int(cost * 1e9), bytes_accessed=0, transcendentals=0),
    )(weights, *fields)


def shifted(step):
    return [(z, (z + step) % 8) for z in range(8)]


def per_device(green_row, time_step):
    slot_count = green_row.shape[4]
    history = slot_count * 8
    zh, zl, core = (lax.axis_index(axis) for axis in ("zh", "zl", "core"))
    plane = lax.axis_index("y") * 4 + lax.axis_index("x")
    turn = ((zh * 4 + zl + 2) // 4 + 1) % 2
    origin = (zl + 2) % 4 * 2 + core
    first = origin * slot_count + turn * (slot_count // 2) + plane * SLOTS
    slot_ids = first + jnp.arange(SLOTS, dtype=jnp.int32)
    slot_age = (time_step[0] - 1 - slot_ids) % history + 1
    decays = jnp.exp2(-(slot_age - 1).astype(jnp.float32) / history)
    weights = delta_time * decays * jnp.where(slot_age == history, 0.5, 1.0).astype(jnp.float32)
    weights = jnp.broadcast_to(weights[:, None], (SLOTS, LANES))
    high, low, twiddle = lane_tables()

    parts = green_row.reshape(4 * ORB, ORB, 2, PLANE, SLOTS, LANES)

    def spread(value):
        return lax.all_to_all(value, ("y", "x"), split_axis=0, concat_axis=0)

    def move(rising, falling):
        return (
            lax.ppermute(rising, ("zh", "zl"), shifted(2)),
            lax.ppermute(falling, ("zh", "zl"), shifted(-2)),
        )

    def work(fields, partial, weights, **more):
        return collide(turn_flag, fields, weights, high, low, twiddle, partial, **more)

    turn_flag = turn.reshape(1).astype(jnp.int32)
    partial = jnp.zeros((ROWS, PAIRS, LANES), jnp.float32)
    fence = lax.optimization_barrier
    early = [[(0, 0), (1, 0), (2, 0), (0, 1)]]
    late = [[(1, 1), (2, 1)], [(0, 2), (1, 2), (2, 2)]]
    cut = 4 * len(late[0])

    side = zh.reshape(1).astype(jnp.int32)
    zero = arrange(side, parts, early, True)
    zero, side = fence((zero, side))
    zero = tuple(move(*zero))
    (rest,) = arrange(side, parts, late, False)
    rest = spread(rest)
    zero, rest, weights = fence((zero, rest, settle(weights, zero, 50.0)))
    one, two = (rest[:, 0, :cut], rest[:, 1, :cut]), (rest[:, 0, cut:], rest[:, 1, cut:])
    one = tuple(move(*one))
    two = tuple(move(*two))
    zero = spread(jnp.stack(zero, 1))
    one, zero, weights = fence((one, zero, settle(weights, one, 50.0)))
    partial, sigma = work([zero], partial, weights, spilled=True)
    (partial,) = work(one, partial, weights, older=(zero, sigma))
    partial, two = fence((partial, two))
    (partial,) = work(two, partial, weights)
    blocks = partial.reshape(PLANE, 2, PAIRS, LANES)
    owned = jnp.sum(spread(blocks), axis=0)
    share = LANES // 8
    shares = owned.reshape(2, PAIRS, 8, share).transpose(0, 2, 1, 3).reshape(PLANE, 1, PAIRS * share)
    shares = lax.all_to_all(shares, ("zh", "zl", "core"), split_axis=0, concat_axis=0)
    summed = jnp.sum(shares, axis=(0, 1)).reshape(PAIRS, share)
    none = jnp.zeros_like(summed[0])
    real = [summed[0], summed[3], summed[5], summed[3], summed[1], summed[7], summed[5], summed[7], summed[2]]
    imag = [none, summed[4], summed[6], -summed[4], none, summed[8], -summed[6], -summed[8], none]
    return jnp.stack(real + imag).reshape(2, ORB, ORB, -1)


def solution(mesh):
    axes = ("y", "zh", "x", "zl", "core")
    finer = Mesh(mesh.devices.reshape(4, 2, 4, 4, 2), axes)
    mom, hist = axes[:3], axes[3:]
    return jax.shard_map(
        per_device,
        mesh=finer,
        in_specs=(P(None, None, None, None, hist, mom), P()),
        out_specs=P(None, None, None, axes),
        check_vma=False,
    )
```

```python
import functools
import math

import jax
import jax.numpy as jnp
import numpy as np
from jax import lax
from jax.experimental import pallas as pl
from jax.experimental.pallas import tpu as pltpu
from jax.sharding import Mesh
from jax.sharding import PartitionSpec as P

NKX = 64
NKY = 64
ORB = 3
PAIRS = ORB * ORB
ROWS = 32
PLANE = 16
SLOTS = 8
LANES = 128

delta_time = 0.01


def lane_tables():
    index = np.arange(64)
    angle = 2.0 * math.pi * (index[:, None] * index[None, :] % 64) / 64
    sign = np.array([[1.0, 1.0], [1.0, -1.0]])
    cosine = np.kron(sign, np.cos(angle)) / 64
    sine = np.kron(sign, np.sin(angle)) / 64
    table = np.block([[cosine, sine], [-sine, cosine]]).astype(np.float32)
    high = table.astype(jnp.bfloat16)
    low = (table - high.astype(np.float32)).astype(jnp.bfloat16)
    turn = 2.0 * math.pi * np.arange(ROWS)[:, None] * np.repeat([0, 1], 64)[None, :] / 64
    twiddle = np.stack([np.cos(turn), np.sin(turn)], 1).astype(np.float32)
    return high, low, twiddle


def turned(value, step, length):
    real, imag = value
    eighths = step * 8 / length
    if eighths == 0:
        return real, imag
    if eighths == 2:
        return -imag, real
    if eighths == 4:
        return -real, -imag
    if eighths == 6:
        return imag, -real
    root = math.sqrt(0.5)
    if eighths == 1:
        return root * (real - imag), root * (real + imag)
    if eighths == 3:
        return -root * (real + imag), root * (real - imag)
    if eighths == 5:
        return root * (imag - real), -root * (real + imag)
    if eighths == 7:
        return root * (real + imag), root * (imag - real)
    cosine, sine = math.cos(2 * math.pi * step / length), math.sin(2 * math.pi * step / length)
    return real * cosine - imag * sine, real * sine + imag * cosine


def plus(first, second):
    return first[0] + second[0], first[1] + second[1]


def minus(first, second):
    return first[0] - second[0], first[1] - second[1]


def fourier(values):
    length = len(values)
    if length == 1:
        return values
    if length == 2:
        return [plus(*values), minus(*values)]
    quarter = length // 4
    parts = [fourier(values[start::4]) for start in range(4)]
    out = [None] * length
    for m in range(quarter):
        first, second, third, fourth = (turned(parts[p][m], p * m, length) for p in range(4))
        even, odd = plus(first, third), minus(first, third)
        other, cross = plus(second, fourth), minus(second, fourth)
        cross = (-cross[1], cross[0])
        out[m], out[m + 2 * quarter] = plus(even, other), minus(even, other)
        out[m + quarter], out[m + 3 * quarter] = plus(odd, cross), minus(odd, cross)
    return out


def product(values, high, low):
    head = values.astype(jnp.bfloat16)
    tail = (values - head.astype(jnp.float32)).astype(jnp.bfloat16)

    def dot(left, right):
        return jnp.dot(left, right, preferred_element_type=jnp.float32)

    return dot(head, high) + (dot(tail, high) + dot(head, low))


def kernel(count, joined, spill, turn, *refs):
    *refs, field, green, sems = refs
    fields = [refs.pop(0)] if refs[0].ndim == 5 else [refs.pop(0), refs.pop(0)]
    if joined:
        older_green, older_sigma = refs.pop(0), refs.pop(0)
    weight, high_ref, low_ref, twiddle, before, out, *spilled = refs

    def fetch(n, at):
        source = fields[n].at[:, at] if len(fields) == 2 else fields[0].at[:, n, at]
        half = turn[0] if n == 0 else 1 - turn[0]
        return pltpu.make_async_copy(source, green.at[half, :, at], sems.at[n, at])

    kinds = [(comp, pair, part) for comp in range(2) for pair in range(count) for part in range(2)]
    for comp, pair, part in kinds:
        for n in range(2):
            fetch(n, (2 * comp + part) * count + pair).start()

    def pair_of(source, pairs, m, comp, pair):
        plane, half, at = m // 8 * 4 + m % 4, m // 4 % 2, comp * 2 * pairs + pair
        return source[half, plane, at], source[half, plane, at + pairs]

    def spot(part):
        return pl.ds(part * LANES, LANES)

    def twist(n):
        return twiddle[n, 0][None, :], twiddle[n, 1][None, :]

    def times(value, factor):
        return value[0] * factor[0] - value[1] * factor[1], value[0] * factor[1] + value[1] * factor[0]

    @pl.loop(0, 2 * count)
    def _(s):
        comp, pair = s // count, s % count
        rows = pl.ds(pl.multiple_of(comp * SLOTS, SLOTS), SLOTS)
        for part in range(2):
            for n in range(2):
                fetch(n, (2 * comp + part) * count + pair).wait()
        values = [pair_of(green, count, m, comp, pair) for m in range(ROWS)]
        for n, value in enumerate(fourier(values)):
            real, imag = times(value, twist(n)) if n else value
            field[n, pair, rows, spot(0)] = real
            field[n, pair, rows, spot(1)] = imag

    block = 8
    size = block * count * 2 * SLOTS

    @pl.loop(0, ROWS // block)
    def _(b):
        take = pl.ds(b * block, block)
        high, low = high_ref[...], low_ref[...]
        space = product(field[take].reshape(size, 2 * LANES), high, low)
        space = space.reshape(block * count, 2, SLOTS, 2 * LANES)
        less = space[:, 0, :, :LANES], space[:, 0, :, LANES:]
        great = space[:, 1, :, :LANES], space[:, 1, :, LANES:]

        def bubble(first, other):
            real = first[0] * first[0] - first[1] * first[1]
            imag = 2.0 * first[0] * first[1]
            return -(real * other[0] + imag * other[1]), imag * other[0] - real * other[1]

        sigma = jnp.stack(
            [jnp.concatenate(bubble(less, great), -1), jnp.concatenate(bubble(great, less), -1)], 1
        )
        back = product(sigma.reshape(size, 2 * LANES), high, low)
        field[take] = back.reshape(block, count, 2 * SLOTS, 2 * LANES)

    @pl.loop(0, 2 * count)
    def _(s):
        comp, pair = s // count, s % count
        rows = pl.ds(pl.multiple_of(comp * SLOTS, SLOTS), SLOTS)
        values = [(field[n, pair, rows, spot(0)], field[n, pair, rows, spot(1)]) for n in range(ROWS)]
        values = [times(value, twist(n)) if n else value for n, value in enumerate(values)]
        for m, (real, imag) in enumerate(fourier(values)):
            field[m, pair, rows, spot(0)] = real
            field[m, pair, rows, spot(1)] = imag

    scale = weight[...]

    @pl.loop(0, ROWS)
    def _(m):
        def sigma(comp, a):
            rows = pl.ds(comp * SLOTS, SLOTS)
            if joined and a == 0:
                return older_sigma[m, rows, spot(0)], older_sigma[m, rows, spot(1)]
            return field[m, a - joined, rows, spot(0)], field[m, a - joined, rows, spot(1)]

        def given(comp, b):
            if joined and b == 0:
                return pair_of(older_green, 1, m, comp, 0)
            return pair_of(green, count, m, comp, b - joined)

        def memory(a, b):
            left, right = sigma(0, a), given(1, b)
            other, cross = sigma(1, a), given(0, b)
            real = left[0] * right[0] - left[1] * right[1] - other[0] * cross[0] + other[1] * cross[1]
            if a == b:
                return real, None
            imag = left[0] * right[1] + left[1] * right[0] - other[0] * cross[1] - other[1] * cross[0]
            return real, imag

        results = [2.0 * memory(a, a)[0] for a in range(ORB)]
        for a, b in ((0, 1), (0, 2), (1, 2)):
            one, two = memory(a, b), memory(b, a)
            results += [one[0] + two[0], two[1] - one[1]]
        for i, result in enumerate(results):
            spare, row = (m // 8 * 4 + m % 4) * 2 + m // 4 % 2, pl.ds(i, 1)
            out[spare, row, :] = before[spare, row, :] + jnp.sum(result * scale, axis=0, keepdims=True)
        if spilled:
            spilled[1][m] = field[m, spill]

    if spilled:
        for kind in range(4):
            spilled[0][:, :, kind] = green[:, :, kind * count + spill]


def collide(turn, fields, weights, high, low, twiddle, before, older=(), spill=None):
    count = fields[0].shape[-3] // 4
    shapes = [(ROWS, PAIRS, LANES)]
    if spill is not None:
        shapes += [(2, PLANE, 4, SLOTS, LANES), (ROWS, 2 * SLOTS, 2 * LANES)]
    inputs = (*older, weights, high, low, twiddle, before)
    return pl.pallas_call(
        functools.partial(kernel, count, int(len(older) > 0), spill),
        out_shape=[jax.ShapeDtypeStruct(shape, jnp.float32) for shape in shapes],
        in_specs=[pl.BlockSpec(memory_space=pltpu.SMEM)]
        + [pl.BlockSpec(memory_space=pl.ANY)] * len(fields)
        + [pl.BlockSpec(memory_space=pltpu.VMEM)] * len(inputs),
        out_specs=[pl.BlockSpec(memory_space=pltpu.VMEM)] * len(shapes),
        scratch_shapes=[
            pltpu.VMEM((ROWS, count, 2 * SLOTS, 2 * LANES), jnp.float32),
            pltpu.VMEM((2, PLANE, 4 * count, SLOTS, LANES), jnp.float32),
            pltpu.SemaphoreType.DMA((2, 4 * count)),
        ],
        compiler_params=pltpu.CompilerParams(vmem_limit_bytes=24 * 1024 * 1024),
        cost_estimate=pl.CostEstimate(flops=1000000000, bytes_accessed=0, transcendentals=0),
    )(turn, *fields, *inputs)


def arrange_kernel(blocks, apart, first, parts, *refs):
    *outs, sems = refs
    copies, base = [], 0
    for pairs in blocks:
        for kind in range(4):
            for i, (a, c) in enumerate(pairs):
                at = base + kind * len(pairs) + i
                for n in range(2):
                    half = first[0] if n == 0 else 1 - first[0]
                    target = outs[n].at[:, at] if apart else outs[0].at[:, n, at]
                    source = parts.at[kind * ORB + a, c, half]
                    copies.append(pltpu.make_async_copy(source, target, sems.at[n, at]))
        base += 4 * len(pairs)
    for copy in copies:
        copy.start()
    for copy in copies:
        copy.wait()


def arrange(first, parts, blocks, apart):
    count = 4 * sum(len(pairs) for pairs in blocks)
    whole = (PLANE, count, SLOTS, LANES) if apart else (PLANE, 2, count, SLOTS, LANES)
    shape = jax.ShapeDtypeStruct(whole, jnp.float32)
    return pl.pallas_call(
        functools.partial(arrange_kernel, blocks, apart),
        out_shape=[shape] * (2 if apart else 1),
        in_specs=[pl.BlockSpec(memory_space=pltpu.SMEM), pl.BlockSpec(memory_space=pl.ANY)],
        out_specs=[pl.BlockSpec(memory_space=pltpu.VMEM)] * (2 if apart else 1),
        scratch_shapes=[pltpu.SemaphoreType.DMA((2, count))],
        compiler_params=pltpu.CompilerParams(vmem_limit_bytes=(57 if apart else 60) * 1024 * 1024),
        cost_estimate=pl.CostEstimate(flops=0, bytes_accessed=3_200_000, transcendentals=0),
    )(first, parts)


def settle(weights, fields, cost):
    def body(given, *refs):
        refs[-1][...] = given[...]

    return pl.pallas_call(
        body,
        out_shape=jax.ShapeDtypeStruct((SLOTS, LANES), jnp.float32),
        in_specs=[pl.BlockSpec(memory_space=pltpu.VMEM)] + [pl.BlockSpec(memory_space=pl.ANY)] * len(fields),
        out_specs=pl.BlockSpec(memory_space=pltpu.VMEM),
        compiler_params=pltpu.CompilerParams(vmem_limit_bytes=1024 * 1024),
        cost_estimate=pl.CostEstimate(flops=int(cost * 1e9), bytes_accessed=0, transcendentals=0),
    )(weights, *fields)


def shifted(step):
    return [(z, (z + step) % 8) for z in range(8)]


def per_device(green_row, time_step):
    slot_count = green_row.shape[4]
    history = slot_count * 8
    zh, zl, core = (lax.axis_index(axis) for axis in ("zh", "zl", "core"))
    plane = lax.axis_index("y") * 4 + lax.axis_index("x")
    turn = ((zh * 4 + zl + 2) // 4 + 1) % 2
    origin = (zl + 2) % 4 * 2 + core
    first = origin * slot_count + turn * (slot_count // 2) + plane * SLOTS
    slot_ids = first + jnp.arange(SLOTS, dtype=jnp.int32)
    slot_age = (time_step[0] - 1 - slot_ids) % history + 1
    decays = jnp.exp2(-(slot_age - 1).astype(jnp.float32) / history)
    weights = delta_time * decays * jnp.where(slot_age == history, 0.5, 1.0).astype(jnp.float32)
    weights = jnp.broadcast_to(weights[:, None], (SLOTS, LANES))
    high, low, twiddle = lane_tables()

    parts = green_row.reshape(4 * ORB, ORB, 2, PLANE, SLOTS, LANES)

    def spread(value):
        return lax.all_to_all(value, ("y", "x"), split_axis=0, concat_axis=0)

    def move(rising, falling):
        return (
            lax.ppermute(rising, ("zh", "zl"), shifted(2)),
            lax.ppermute(falling, ("zh", "zl"), shifted(-2)),
        )

    def work(fields, partial, weights, **more):
        return collide(turn_flag, fields, weights, high, low, twiddle, partial, **more)

    turn_flag = turn.reshape(1).astype(jnp.int32)
    partial = jnp.zeros((ROWS, PAIRS, LANES), jnp.float32)
    fence = lax.optimization_barrier
    early = [[(0, 0), (1, 0), (2, 0), (0, 1)]]
    late = [[(1, 1), (2, 1), (0, 2)], [(1, 2), (2, 2)]]
    cut = 4 * len(late[0])

    side = zh.reshape(1).astype(jnp.int32)
    zero = arrange(side, parts, early, True)
    zero, side = fence((zero, side))
    zero = tuple(move(*zero))
    (rest,) = arrange(side, parts, late, False)
    rest = spread(rest)
    zero, rest, weights = fence((zero, rest, settle(weights, zero, 50.0)))
    one, two = (rest[:, 0, :cut], rest[:, 1, :cut]), (rest[:, 0, cut:], rest[:, 1, cut:])
    one = tuple(move(*one))
    two = tuple(move(*two))
    zero = spread(jnp.stack(zero, 1))
    one, zero, weights = fence((one, zero, settle(weights, one, 50.0)))
    partial, *older = work([zero], partial, weights, spill=ORB)
    partial, *older = work(one, partial, weights, older=older, spill=ORB - 1)
    partial, two = fence((partial, two))
    (partial,) = work(two, partial, weights, older=older)
    blocks = partial.reshape(PLANE, 2, PAIRS, LANES)
    owned = jnp.sum(spread(blocks), axis=0)
    share = LANES // 8
    shares = owned.reshape(2, PAIRS, 8, share).transpose(0, 2, 1, 3).reshape(PLANE, 1, PAIRS * share)
    shares = lax.all_to_all(shares, ("zh", "zl", "core"), split_axis=0, concat_axis=0)
    summed = jnp.sum(shares, axis=(0, 1)).reshape(PAIRS, share)
    none = jnp.zeros_like(summed[0])
    real = [summed[0], summed[3], summed[5], summed[3], summed[1], summed[7], summed[5], summed[7], summed[2]]
    imag = [none, summed[4], summed[6], -summed[4], none, summed[8], -summed[6], -summed[8], none]
    return jnp.stack(real + imag).reshape(2, ORB, ORB, -1)


def solution(mesh):
    axes = ("y", "zh", "x", "zl", "core")
    finer = Mesh(mesh.devices.reshape(4, 2, 4, 4, 2), axes)
    mom, hist = axes[:3], axes[3:]
    return jax.shard_map(
        per_device,
        mesh=finer,
        in_specs=(P(None, None, None, None, hist, mom), P()),
        out_specs=P(None, None, None, axes),
        check_vma=False,
    )
```

```python
import functools
import math

import jax
import jax.numpy as jnp
import numpy as np
from jax import lax
from jax.experimental import pallas as pl
from jax.experimental.pallas import tpu as pltpu
from jax.sharding import Mesh
from jax.sharding import PartitionSpec as P

NKX = 64
NKY = 64
ORB = 3
PAIRS = ORB * ORB
ROWS = 32
PLANE = 16
SLOTS = 8
LANES = 128

delta_time = 0.01


def lane_tables():
    index = np.arange(64)
    angle = 2.0 * math.pi * (index[:, None] * index[None, :] % 64) / 64
    sign = np.array([[1.0, 1.0], [1.0, -1.0]])
    cosine = np.kron(sign, np.cos(angle)) / 64
    sine = np.kron(sign, np.sin(angle)) / 64
    table = np.block([[cosine, sine], [-sine, cosine]]).astype(np.float32)
    high = table.astype(jnp.bfloat16)
    low = (table - high.astype(np.float32)).astype(jnp.bfloat16)
    turn = 2.0 * math.pi * np.arange(ROWS)[:, None] * np.repeat([0, 1], 64)[None, :] / 64
    twiddle = np.stack([np.cos(turn), np.sin(turn)], 1).astype(np.float32)
    return high, low, twiddle


def turned(value, step, length):
    real, imag = value
    eighths = step * 8 / length
    if eighths == 0:
        return real, imag
    if eighths == 2:
        return -imag, real
    if eighths == 4:
        return -real, -imag
    if eighths == 6:
        return imag, -real
    root = math.sqrt(0.5)
    if eighths == 1:
        return root * (real - imag), root * (real + imag)
    if eighths == 3:
        return -root * (real + imag), root * (real - imag)
    if eighths == 5:
        return root * (imag - real), -root * (real + imag)
    if eighths == 7:
        return root * (real + imag), root * (imag - real)
    cosine, sine = math.cos(2 * math.pi * step / length), math.sin(2 * math.pi * step / length)
    return real * cosine - imag * sine, real * sine + imag * cosine


def plus(first, second):
    return first[0] + second[0], first[1] + second[1]


def minus(first, second):
    return first[0] - second[0], first[1] - second[1]


def fourier(values):
    length = len(values)
    if length == 1:
        return values
    if length == 2:
        return [plus(*values), minus(*values)]
    quarter = length // 4
    parts = [fourier(values[start::4]) for start in range(4)]
    out = [None] * length
    for m in range(quarter):
        first, second, third, fourth = (turned(parts[p][m], p * m, length) for p in range(4))
        even, odd = plus(first, third), minus(first, third)
        other, cross = plus(second, fourth), minus(second, fourth)
        cross = (-cross[1], cross[0])
        out[m], out[m + 2 * quarter] = plus(even, other), minus(even, other)
        out[m + quarter], out[m + 3 * quarter] = plus(odd, cross), minus(odd, cross)
    return out


def product(values, high, low):
    head = values.astype(jnp.bfloat16)
    tail = (values - head.astype(jnp.float32)).astype(jnp.bfloat16)

    left, right = jnp.concatenate([head, tail, head], 1), jnp.concatenate([high, high, low], 0)
    return jnp.dot(left, right, preferred_element_type=jnp.float32)


def kernel(count, stacked, joined, spilled, turn, *refs):
    refs = list(refs)
    if stacked:
        whole = refs.pop(0)
        lower, upper = whole.at[:, 0], whole.at[:, 1]
    else:
        lower, upper = refs.pop(0), refs.pop(0)
    if joined:
        older, older_sigma = refs.pop(0), refs.pop(0)
    weight, high_ref, low_ref, twiddle, before, out = refs[:6]
    field = refs[-1]

    def pair_of(source, plane, pairs, comp, pair):
        at = comp * 2 * pairs + pair
        return source[plane, at], source[plane, at + pairs]

    def either_way(act, *sides):
        pl.when(turn[0] == 0)(lambda: act(*sides))
        pl.when(turn[0] == 1)(lambda: act(*(side[::-1] for side in sides)))

    def spot(part):
        return pl.ds(part * LANES, LANES)

    def twist(n):
        return twiddle[n, 0][None, :], twiddle[n, 1][None, :]

    def times(value, factor):
        return value[0] * factor[0] - value[1] * factor[1], value[0] * factor[1] + value[1] * factor[0]

    def forward(halves):
        @pl.loop(0, 2 * count)
        def _(s):
            comp, pair = s // count, s % count
            rows = pl.ds(pl.multiple_of(comp * SLOTS, SLOTS), SLOTS)
            values = [
                pair_of(halves[m // 4 % 2], m // 8 * 4 + m % 4, count, comp, pair) for m in range(ROWS)
            ]
            for n, value in enumerate(fourier(values)):
                real, imag = times(value, twist(n)) if n else value
                field[n, pair, rows, spot(0)] = real
                field[n, pair, rows, spot(1)] = imag

    either_way(forward, (lower, upper))

    block = 32 if count <= ORB else 16
    size = block * count * 2 * SLOTS

    @pl.loop(0, ROWS // block)
    def _(b):
        take = pl.ds(b * block, block)
        high, low = high_ref[...], low_ref[...]
        space = product(field[take].reshape(size, 2 * LANES), high, low)
        space = space.reshape(block * count, 2, SLOTS, 2 * LANES)
        less = space[:, 0, :, :LANES], space[:, 0, :, LANES:]
        great = space[:, 1, :, :LANES], space[:, 1, :, LANES:]

        def bubble(first, other):
            real = first[0] * first[0] - first[1] * first[1]
            imag = 2.0 * first[0] * first[1]
            return -(real * other[0] + imag * other[1]), imag * other[0] - real * other[1]

        sigma = jnp.stack(
            [jnp.concatenate(bubble(less, great), -1), jnp.concatenate(bubble(great, less), -1)], 1
        )
        back = product(sigma.reshape(size, 2 * LANES), high, low)
        field[take] = back.reshape(block, count, 2 * SLOTS, 2 * LANES)

    @pl.loop(0, 2 * count)
    def _(s):
        comp, pair = s // count, s % count
        rows = pl.ds(pl.multiple_of(comp * SLOTS, SLOTS), SLOTS)
        values = [(field[n, pair, rows, spot(0)], field[n, pair, rows, spot(1)]) for n in range(ROWS)]
        values = [times(value, twist(n)) if n else value for n, value in enumerate(values)]
        for m, (real, imag) in enumerate(fourier(values)):
            field[m, pair, rows, spot(0)] = real
            field[m, pair, rows, spot(1)] = imag

    scale = weight[...]

    def contract(plane, half, halves, older_halves):
        m = plane // 4 * 8 + half * 4 + plane % 4

        def sigma(comp, a):
            rows = pl.ds(comp * SLOTS, SLOTS)
            if joined and a == 0:
                return older_sigma[m, rows, spot(0)], older_sigma[m, rows, spot(1)]
            return field[m, a - joined, rows, spot(0)], field[m, a - joined, rows, spot(1)]

        def given(comp, b):
            if joined and b == 0:
                return pair_of(older_halves[half], plane, ORB + 1, comp, ORB)
            return pair_of(halves[half], plane, count, comp, b - joined)

        def memory(a, b):
            left, right = sigma(0, a), given(1, b)
            other, cross = sigma(1, a), given(0, b)
            real = left[0] * right[0] - left[1] * right[1] - other[0] * cross[0] + other[1] * cross[1]
            if a == b:
                return real, None
            imag = left[0] * right[1] + left[1] * right[0] - other[0] * cross[1] - other[1] * cross[0]
            return real, imag

        results = [2.0 * memory(a, a)[0] for a in range(ORB)]
        for a, b in ((0, 1), (0, 2), (1, 2)):
            one, two = memory(a, b), memory(b, a)
            results += [one[0] + two[0], two[1] - one[1]]
        for i, result in enumerate(results):
            spot_out, row = plane * 2 + half, pl.ds(i, 1)
            out[spot_out, row, :] = before[spot_out, row, :] + jnp.sum(result * scale, axis=0, keepdims=True)
        if spilled:
            refs[6][m] = field[m, ORB]

    def contract_all(halves, older_halves):
        @pl.loop(0, PLANE, unroll=2)
        def _(plane):
            for half in range(2):
                contract(plane, half, halves, older_halves)

    olders = (older.at[:, 0], older.at[:, 1]) if joined else (None, None)
    either_way(contract_all, (lower, upper), olders)


def collide(turn, fields, weights, high, low, twiddle, before, older=(), spilled=False):
    stacked, joined = len(fields) == 1, int(len(older) > 0)
    count = ORB + 1 if stacked else ORB - joined
    shapes = [jax.ShapeDtypeStruct((ROWS, PAIRS, LANES), jnp.float32)]
    if spilled:
        shapes.append(jax.ShapeDtypeStruct((ROWS, 2 * SLOTS, 2 * LANES), jnp.float32))
    inputs = (*fields, *older, weights, high, low, twiddle, before)
    return pl.pallas_call(
        functools.partial(kernel, count, stacked, joined, spilled),
        out_shape=shapes,
        in_specs=[pl.BlockSpec(memory_space=pltpu.SMEM)]
        + [pl.BlockSpec(memory_space=pltpu.VMEM)] * len(inputs),
        out_specs=[pl.BlockSpec(memory_space=pltpu.VMEM)] * len(shapes),
        scratch_shapes=[pltpu.VMEM((ROWS, count, 2 * SLOTS, 2 * LANES), jnp.float32)],
        compiler_params=pltpu.CompilerParams(vmem_limit_bytes=24 * 1024 * 1024),
        cost_estimate=pl.CostEstimate(flops=1000000000, bytes_accessed=0, transcendentals=0),
    )(turn, *inputs)


def arrange_kernel(blocks, apart, first, parts, *refs):
    *outs, sems = refs
    copies, base = [], 0
    for pairs in blocks:
        for kind in range(4):
            for i, (a, c) in enumerate(pairs):
                at = base + kind * len(pairs) + i
                for n in range(2):
                    half = first[0] if n == 0 else 1 - first[0]
                    target = outs[n].at[:, at] if apart else outs[0].at[:, n, at]
                    source = parts.at[kind * ORB + a, c, half]
                    copies.append(pltpu.make_async_copy(source, target, sems.at[n, at]))
        base += 4 * len(pairs)
    for copy in copies:
        copy.start()
    for copy in copies:
        copy.wait()


def arrange(first, parts, blocks, apart):
    count = 4 * sum(len(pairs) for pairs in blocks)
    whole = (PLANE, count, SLOTS, LANES) if apart else (PLANE, 2, count, SLOTS, LANES)
    shape = jax.ShapeDtypeStruct(whole, jnp.float32)
    return pl.pallas_call(
        functools.partial(arrange_kernel, blocks, apart),
        out_shape=[shape] * (2 if apart else 1),
        in_specs=[pl.BlockSpec(memory_space=pltpu.SMEM), pl.BlockSpec(memory_space=pl.ANY)],
        out_specs=[pl.BlockSpec(memory_space=pltpu.VMEM)] * (2 if apart else 1),
        scratch_shapes=[pltpu.SemaphoreType.DMA((2, count))],
        compiler_params=pltpu.CompilerParams(vmem_limit_bytes=60 * 1024 * 1024),
        cost_estimate=pl.CostEstimate(flops=0, bytes_accessed=3_200_000, transcendentals=0),
    )(first, parts)


def settle(weights, fields, cost):
    def body(given, *refs):
        refs[-1][...] = given[...]

    return pl.pallas_call(
        body,
        out_shape=jax.ShapeDtypeStruct((SLOTS, LANES), jnp.float32),
        in_specs=[pl.BlockSpec(memory_space=pltpu.VMEM)] + [pl.BlockSpec(memory_space=pl.ANY)] * len(fields),
        out_specs=pl.BlockSpec(memory_space=pltpu.VMEM),
        compiler_params=pltpu.CompilerParams(vmem_limit_bytes=1024 * 1024),
        cost_estimate=pl.CostEstimate(flops=int(cost * 1e9), bytes_accessed=0, transcendentals=0),
    )(weights, *fields)


def shifted(step):
    return [(z, (z + step) % 8) for z in range(8)]


def per_device(green_row, time_step):
    slot_count = green_row.shape[4]
    history = slot_count * 8
    zh, zl, core = (lax.axis_index(axis) for axis in ("zh", "zl", "core"))
    plane = lax.axis_index("y") * 4 + lax.axis_index("x")
    turn = ((zh * 4 + zl + 2) // 4 + 1) % 2
    origin = (zl + 2) % 4 * 2 + core
    first = origin * slot_count + turn * (slot_count // 2) + plane * SLOTS
    slot_ids = first + jnp.arange(SLOTS, dtype=jnp.int32)
    slot_age = (time_step[0] - 1 - slot_ids) % history + 1
    decays = jnp.exp2(-(slot_age - 1).astype(jnp.float32) / history)
    weights = delta_time * decays * jnp.where(slot_age == history, 0.5, 1.0).astype(jnp.float32)
    weights = jnp.broadcast_to(weights[:, None], (SLOTS, LANES))
    high, low, twiddle = lane_tables()

    parts = green_row.reshape(4 * ORB, ORB, 2, PLANE, SLOTS, LANES)

    def spread(value):
        return lax.all_to_all(value, ("y", "x"), split_axis=0, concat_axis=0)

    def move(rising, falling):
        return (
            lax.ppermute(rising, ("zh", "zl"), shifted(2)),
            lax.ppermute(falling, ("zh", "zl"), shifted(-2)),
        )

    def work(fields, partial, weights, **more):
        return collide(turn_flag, fields, weights, high, low, twiddle, partial, **more)

    turn_flag = turn.reshape(1).astype(jnp.int32)
    partial = jnp.zeros((ROWS, PAIRS, LANES), jnp.float32)
    fence = lax.optimization_barrier
    early = [[(0, 0), (1, 0), (2, 0), (0, 1)]]
    late = [[(1, 1), (2, 1)], [(0, 2), (1, 2), (2, 2)]]
    cut = 4 * len(late[0])

    side = zh.reshape(1).astype(jnp.int32)
    zero = arrange(side, parts, early, True)
    zero, side = fence((zero, side))
    zero = tuple(move(*zero))
    (rest,) = arrange(side, parts, late, False)
    rest = spread(rest)
    zero, rest, weights = fence((zero, rest, settle(weights, zero, 50.0)))
    one, two = (rest[:, 0, :cut], rest[:, 1, :cut]), (rest[:, 0, cut:], rest[:, 1, cut:])
    one = tuple(move(*one))
    two = tuple(move(*two))
    zero = spread(jnp.stack(zero, 1))
    one, zero, weights = fence((one, zero, settle(weights, one, 50.0)))
    partial, sigma = work([zero], partial, weights, spilled=True)
    (partial,) = work(one, partial, weights, older=(zero, sigma))
    partial, two = fence((partial, two))
    (partial,) = work(two, partial, weights)
    blocks = partial.reshape(PLANE, 2, PAIRS, LANES)
    owned = jnp.sum(spread(blocks), axis=0)
    share = LANES // 8
    shares = owned.reshape(2, PAIRS, 8, share).transpose(0, 2, 1, 3).reshape(PLANE, 1, PAIRS * share)
    shares = lax.all_to_all(shares, ("zh", "zl", "core"), split_axis=0, concat_axis=0)
    summed = jnp.sum(shares, axis=(0, 1)).reshape(PAIRS, share)
    none = jnp.zeros_like(summed[0])
    real = [summed[0], summed[3], summed[5], summed[3], summed[1], summed[7], summed[5], summed[7], summed[2]]
    imag = [none, summed[4], summed[6], -summed[4], none, summed[8], -summed[6], -summed[8], none]
    return jnp.stack(real + imag).reshape(2, ORB, ORB, -1)


def solution(mesh):
    axes = ("y", "zh", "x", "zl", "core")
    finer = Mesh(mesh.devices.reshape(4, 2, 4, 4, 2), axes)
    mom, hist = axes[:3], axes[3:]
    return jax.shard_map(
        per_device,
        mesh=finer,
        in_specs=(P(None, None, None, None, hist, mom), P()),
        out_specs=P(None, None, None, axes),
        check_vma=False,
    )
```

```python
import functools
import math

import jax
import jax.numpy as jnp
import numpy as np
from jax import lax
from jax.experimental import pallas as pl
from jax.experimental.pallas import tpu as pltpu
from jax.sharding import Mesh
from jax.sharding import PartitionSpec as P

NKX = 64
NKY = 64
ORB = 3
PAIRS = ORB * ORB
ROWS = 32
PLANE = 16
SLOTS = 8
LANES = 128

delta_time = 0.01


def lane_tables():
    index = np.arange(64)
    angle = 2.0 * math.pi * (index[:, None] * index[None, :] % 64) / 64
    sign = np.array([[1.0, 1.0], [1.0, -1.0]])
    cosine = np.kron(sign, np.cos(angle)) / 64
    sine = np.kron(sign, np.sin(angle)) / 64
    table = np.block([[cosine, sine], [-sine, cosine]]).astype(np.float32)
    high = table.astype(jnp.bfloat16)
    low = (table - high.astype(np.float32)).astype(jnp.bfloat16)
    turn = 2.0 * math.pi * np.arange(ROWS)[:, None] * np.repeat([0, 1], 64)[None, :] / 64
    twiddle = np.stack([np.cos(turn), np.sin(turn)], 1).astype(np.float32)
    return high, low, twiddle


def turned(value, step, length):
    real, imag = value
    eighths = step * 8 / length
    if eighths == 0:
        return real, imag
    if eighths == 2:
        return -imag, real
    if eighths == 4:
        return -real, -imag
    if eighths == 6:
        return imag, -real
    root = math.sqrt(0.5)
    if eighths == 1:
        return root * (real - imag), root * (real + imag)
    if eighths == 3:
        return -root * (real + imag), root * (real - imag)
    if eighths == 5:
        return root * (imag - real), -root * (real + imag)
    if eighths == 7:
        return root * (real + imag), root * (imag - real)
    cosine, sine = math.cos(2 * math.pi * step / length), math.sin(2 * math.pi * step / length)
    return real * cosine - imag * sine, real * sine + imag * cosine


def plus(first, second):
    return first[0] + second[0], first[1] + second[1]


def minus(first, second):
    return first[0] - second[0], first[1] - second[1]


def fourier(values):
    length = len(values)
    if length == 1:
        return values
    if length == 2:
        return [plus(*values), minus(*values)]
    quarter = length // 4
    parts = [fourier(values[start::4]) for start in range(4)]
    out = [None] * length
    for m in range(quarter):
        first, second, third, fourth = (turned(parts[p][m], p * m, length) for p in range(4))
        even, odd = plus(first, third), minus(first, third)
        other, cross = plus(second, fourth), minus(second, fourth)
        cross = (-cross[1], cross[0])
        out[m], out[m + 2 * quarter] = plus(even, other), minus(even, other)
        out[m + quarter], out[m + 3 * quarter] = plus(odd, cross), minus(odd, cross)
    return out


def product(values, high, low):
    head = values.astype(jnp.bfloat16)
    tail = (values - head.astype(jnp.float32)).astype(jnp.bfloat16)

    left, right = jnp.concatenate([head, tail, head], 1), jnp.concatenate([high, high, low], 0)
    return jnp.dot(left, right, preferred_element_type=jnp.float32)


def kernel(count, olds, spills, turn, *refs):
    *refs, field = refs
    refs = list(refs)

    def halves_of():
        if len(refs[0].shape) == 5:
            whole = refs.pop(0)
            return whole.at[:, 0], whole.at[:, 1]
        return refs.pop(0), refs.pop(0)

    sides = halves_of()
    older_sides, older_sigma = (halves_of(), refs.pop(0)) if olds else ((None, None), None)
    weight, high_ref, low_ref, twiddle, before, out, *spilled = refs

    def pair_of(source, plane, pairs, comp, pair):
        at = comp * 2 * pairs + pair
        return source[plane, at], source[plane, at + pairs]

    def either_way(act, *sides):
        pl.when(turn[0] == 0)(lambda: act(*sides))
        pl.when(turn[0] == 1)(lambda: act(*(side[::-1] for side in sides)))

    def spot(part):
        return pl.ds(part * LANES, LANES)

    def twist(n):
        return twiddle[n, 0][None, :], twiddle[n, 1][None, :]

    def times(value, factor):
        return value[0] * factor[0] - value[1] * factor[1], value[0] * factor[1] + value[1] * factor[0]

    def forward(halves):
        @pl.loop(0, 2 * count)
        def _(s):
            comp, pair = s // count, s % count
            rows = pl.ds(pl.multiple_of(comp * SLOTS, SLOTS), SLOTS)
            values = [
                pair_of(halves[m // 4 % 2], m // 8 * 4 + m % 4, count, comp, pair) for m in range(ROWS)
            ]
            for n, value in enumerate(fourier(values)):
                real, imag = times(value, twist(n)) if n else value
                field[n, pair, rows, spot(0)] = real
                field[n, pair, rows, spot(1)] = imag

    either_way(forward, sides)

    block = 32 if count <= ORB else 16
    size = block * count * 2 * SLOTS

    @pl.loop(0, ROWS // block)
    def _(b):
        take = pl.ds(b * block, block)
        high, low = high_ref[...], low_ref[...]
        space = product(field[take].reshape(size, 2 * LANES), high, low)
        space = space.reshape(block * count, 2, SLOTS, 2 * LANES)
        less = space[:, 0, :, :LANES], space[:, 0, :, LANES:]
        great = space[:, 1, :, :LANES], space[:, 1, :, LANES:]

        def bubble(first, other):
            real = first[0] * first[0] - first[1] * first[1]
            imag = 2.0 * first[0] * first[1]
            return -(real * other[0] + imag * other[1]), imag * other[0] - real * other[1]

        sigma = jnp.stack(
            [jnp.concatenate(bubble(less, great), -1), jnp.concatenate(bubble(great, less), -1)], 1
        )
        back = product(sigma.reshape(size, 2 * LANES), high, low)
        field[take] = back.reshape(block, count, 2 * SLOTS, 2 * LANES)

    @pl.loop(0, 2 * count)
    def _(s):
        comp, pair = s // count, s % count
        rows = pl.ds(pl.multiple_of(comp * SLOTS, SLOTS), SLOTS)
        values = [(field[n, pair, rows, spot(0)], field[n, pair, rows, spot(1)]) for n in range(ROWS)]
        values = [times(value, twist(n)) if n else value for n, value in enumerate(values)]
        for m, (real, imag) in enumerate(fourier(values)):
            field[m, pair, rows, spot(0)] = real
            field[m, pair, rows, spot(1)] = imag

    scale = weight[...]

    def contract(plane, half, halves, older_halves):
        m = plane // 4 * 8 + half * 4 + plane % 4

        def sigma(comp, a):
            rows = pl.ds(comp * SLOTS, SLOTS)
            if a < len(olds):
                return older_sigma[a, m, rows, spot(0)], older_sigma[a, m, rows, spot(1)]
            return field[m, a - len(olds), rows, spot(0)], field[m, a - len(olds), rows, spot(1)]

        def given(comp, b):
            if b < len(olds):
                return pair_of(older_halves[half], plane, older_halves[half].shape[1] // 4, comp, olds[b])
            return pair_of(halves[half], plane, count, comp, b - len(olds))

        def memory(a, b):
            left, right = sigma(0, a), given(1, b)
            other, cross = sigma(1, a), given(0, b)
            real = left[0] * right[0] - left[1] * right[1] - other[0] * cross[0] + other[1] * cross[1]
            if a == b:
                return real, None
            imag = left[0] * right[1] + left[1] * right[0] - other[0] * cross[1] - other[1] * cross[0]
            return real, imag

        results = [2.0 * memory(a, a)[0] for a in range(ORB)]
        for a, b in ((0, 1), (0, 2), (1, 2)):
            one, two = memory(a, b), memory(b, a)
            results += [one[0] + two[0], two[1] - one[1]]
        for i, result in enumerate(results):
            spot_out, row = plane * 2 + half, pl.ds(i, 1)
            out[spot_out, row, :] = before[spot_out, row, :] + jnp.sum(result * scale, axis=0, keepdims=True)
        for i, pair in enumerate(spills):
            spilled[0][i, m] = field[m, pair]

    def contract_all(halves, older_halves):
        @pl.loop(0, PLANE, unroll=2)
        def _(plane):
            for half in range(2):
                contract(plane, half, halves, older_halves)

    either_way(contract_all, sides, older_sides)


def collide(turn, fields, weights, high, low, twiddle, before, older=None, spills=()):
    count = fields[0].shape[-3] // 4
    shapes = [(ROWS, PAIRS, LANES)]
    if spills:
        shapes.append((len(spills), ROWS, 2 * SLOTS, 2 * LANES))
    older_fields, older_sigma, olds = older or ((), None, ())
    given = (*older_fields, older_sigma) if older else ()
    inputs = (*fields, *given, weights, high, low, twiddle, before)
    return pl.pallas_call(
        functools.partial(kernel, count, olds, spills),
        out_shape=[jax.ShapeDtypeStruct(shape, jnp.float32) for shape in shapes],
        in_specs=[pl.BlockSpec(memory_space=pltpu.SMEM)]
        + [pl.BlockSpec(memory_space=pltpu.VMEM)] * len(inputs),
        out_specs=[pl.BlockSpec(memory_space=pltpu.VMEM)] * len(shapes),
        scratch_shapes=[pltpu.VMEM((ROWS, count, 2 * SLOTS, 2 * LANES), jnp.float32)],
        compiler_params=pltpu.CompilerParams(vmem_limit_bytes=24 * 1024 * 1024),
        cost_estimate=pl.CostEstimate(flops=1000000000, bytes_accessed=0, transcendentals=0),
    )(turn, *inputs)


def arrange_kernel(blocks, apart, first, parts, *refs):
    *outs, sems = refs
    copies, base = [], 0
    for block, pairs in enumerate(blocks):
        for kind in range(4):
            for i, (a, c) in enumerate(pairs):
                at = kind * len(pairs) + i
                for n in range(2):
                    half = first[0] if n == 0 else 1 - first[0]
                    target = outs[2 * block + n].at[:, at] if apart else outs[0].at[:, n, base + at]
                    source = parts.at[kind * ORB + a, c, half]
                    copies.append(pltpu.make_async_copy(source, target, sems.at[n, base + at]))
        base += 4 * len(pairs)
    for copy in copies:
        copy.start()
    for copy in copies:
        copy.wait()


def arrange(first, parts, blocks, apart):
    counts = [4 * len(pairs) for pairs in blocks]
    if apart:
        shapes = [(PLANE, count, SLOTS, LANES) for count in counts for _ in range(2)]
    else:
        shapes = [(PLANE, 2, sum(counts), SLOTS, LANES)]
    return pl.pallas_call(
        functools.partial(arrange_kernel, blocks, apart),
        out_shape=[jax.ShapeDtypeStruct(shape, jnp.float32) for shape in shapes],
        in_specs=[pl.BlockSpec(memory_space=pltpu.SMEM), pl.BlockSpec(memory_space=pl.ANY)],
        out_specs=[pl.BlockSpec(memory_space=pltpu.VMEM)] * len(shapes),
        scratch_shapes=[pltpu.SemaphoreType.DMA((2, sum(counts)))],
        compiler_params=pltpu.CompilerParams(vmem_limit_bytes=60 * 1024 * 1024),
        cost_estimate=pl.CostEstimate(flops=0, bytes_accessed=3_200_000, transcendentals=0),
    )(first, parts)


def settle(weights, fields, cost):
    def body(given, *refs):
        refs[-1][...] = given[...]

    return pl.pallas_call(
        body,
        out_shape=jax.ShapeDtypeStruct((SLOTS, LANES), jnp.float32),
        in_specs=[pl.BlockSpec(memory_space=pltpu.VMEM)] + [pl.BlockSpec(memory_space=pl.ANY)] * len(fields),
        out_specs=pl.BlockSpec(memory_space=pltpu.VMEM),
        compiler_params=pltpu.CompilerParams(vmem_limit_bytes=1024 * 1024),
        cost_estimate=pl.CostEstimate(flops=int(cost * 1e9), bytes_accessed=0, transcendentals=0),
    )(weights, *fields)


def shifted(step):
    return [(z, (z + step) % 8) for z in range(8)]


def per_device(green_row, time_step):
    slot_count = green_row.shape[4]
    history = slot_count * 8
    zh, zl, core = (lax.axis_index(axis) for axis in ("zh", "zl", "core"))
    plane = lax.axis_index("y") * 4 + lax.axis_index("x")
    turn = ((zh * 4 + zl + 2) // 4 + 1) % 2
    origin = (zl + 2) % 4 * 2 + core
    first = origin * slot_count + turn * (slot_count // 2) + plane * SLOTS
    slot_ids = first + jnp.arange(SLOTS, dtype=jnp.int32)
    slot_age = (time_step[0] - 1 - slot_ids) % history + 1
    decays = jnp.exp2(-(slot_age - 1).astype(jnp.float32) / history)
    weights = delta_time * decays * jnp.where(slot_age == history, 0.5, 1.0).astype(jnp.float32)
    weights = jnp.broadcast_to(weights[:, None], (SLOTS, LANES))
    high, low, twiddle = lane_tables()

    parts = green_row.reshape(4 * ORB, ORB, 2, PLANE, SLOTS, LANES)

    def spread(value):
        return lax.all_to_all(value, ("y", "x"), split_axis=0, concat_axis=0)

    def move(rising, falling):
        return (
            lax.ppermute(rising, ("zh", "zl"), shifted(2)),
            lax.ppermute(falling, ("zh", "zl"), shifted(-2)),
        )

    def work(fields, partial, weights, **more):
        return collide(turn_flag, fields, weights, high, low, twiddle, partial, **more)

    turn_flag = turn.reshape(1).astype(jnp.int32)
    partial = jnp.zeros((ROWS, PAIRS, LANES), jnp.float32)
    fence = lax.optimization_barrier
    early = [[(0, 0), (1, 0)], [(2, 0), (0, 1), (1, 1)]]
    late = [[(2, 1), (0, 2)], [(1, 2), (2, 2)]]
    cut = 4 * len(late[0])

    def joined(first, second):
        kinds = [part.reshape(PLANE, 4, -1, SLOTS, LANES) for part in (first, second)]
        return jnp.concatenate(kinds, 2).reshape(PLANE, -1, SLOTS, LANES)

    side = zh.reshape(1).astype(jnp.int32)
    zero = arrange(side, parts, early, True)
    zero, side = fence((zero, side))
    ahead, zero = tuple(move(*zero[:2])), tuple(move(*zero[2:]))
    (rest,) = arrange(side, parts, late, False)
    rest = spread(rest)
    ahead, rest, weights = fence((ahead, rest, settle(weights, ahead, 50.0)))
    one, two = (rest[:, 0, :cut], rest[:, 1, :cut]), (rest[:, 0, cut:], rest[:, 1, cut:])
    one = tuple(move(*one))
    two = tuple(move(*two))
    zero = spread(jnp.stack([joined(ahead[n], zero[n]) for n in range(2)], 1))
    one, zero, weights = fence((one, zero, settle(weights, one, 50.0)))
    partial, sigma = work([zero], partial, weights, spills=(3, 4))
    partial, sigma = work(one, partial, weights, older=([zero], sigma, (3, 4)), spills=(1,))
    partial, two = fence((partial, two))
    (partial,) = work(two, partial, weights, older=(one, sigma, (1,)))
    blocks = partial.reshape(PLANE, 2, PAIRS, LANES)
    owned = jnp.sum(spread(blocks), axis=0)
    share = LANES // 8
    shares = owned.reshape(2, PAIRS, 8, share).transpose(0, 2, 1, 3).reshape(PLANE, 1, PAIRS * share)
    shares = lax.all_to_all(shares, ("zh", "zl", "core"), split_axis=0, concat_axis=0)
    summed = jnp.sum(shares, axis=(0, 1)).reshape(PAIRS, share)
    none = jnp.zeros_like(summed[0])
    real = [summed[0], summed[3], summed[5], summed[3], summed[1], summed[7], summed[5], summed[7], summed[2]]
    imag = [none, summed[4], summed[6], -summed[4], none, summed[8], -summed[6], -summed[8], none]
    return jnp.stack(real + imag).reshape(2, ORB, ORB, -1)


def solution(mesh):
    axes = ("y", "zh", "x", "zl", "core")
    finer = Mesh(mesh.devices.reshape(4, 2, 4, 4, 2), axes)
    mom, hist = axes[:3], axes[3:]
    return jax.shard_map(
        per_device,
        mesh=finer,
        in_specs=(P(None, None, None, None, hist, mom), P()),
        out_specs=P(None, None, None, axes),
        check_vma=False,
    )
```

```python
import functools
import math

import jax
import jax.numpy as jnp
import numpy as np
from jax import lax
from jax.experimental import pallas as pl
from jax.experimental.pallas import tpu as pltpu
from jax.sharding import Mesh
from jax.sharding import PartitionSpec as P

NKX = 64
NKY = 64
ORB = 3
PAIRS = ORB * ORB
ROWS = 32
PLANE = 16
SLOTS = 8
LANES = 128

delta_time = 0.01


def lane_tables():
    index = np.arange(64)
    angle = 2.0 * math.pi * (index[:, None] * index[None, :] % 64) / 64
    sign = np.array([[1.0, 1.0], [1.0, -1.0]])
    cosine = np.kron(sign, np.cos(angle)) / 64
    sine = np.kron(sign, np.sin(angle)) / 64
    table = np.block([[cosine, sine], [-sine, cosine]]).astype(np.float32)
    high = table.astype(jnp.bfloat16)
    low = (table - high.astype(np.float32)).astype(jnp.bfloat16)
    turn = 2.0 * math.pi * np.arange(ROWS)[:, None] * np.repeat([0, 1], 64)[None, :] / 64
    twiddle = np.stack([np.cos(turn), np.sin(turn)], 1).astype(np.float32)
    return high, low, twiddle


def turned(value, step, length):
    real, imag = value
    eighths = step * 8 / length
    if eighths == 0:
        return real, imag
    if eighths == 2:
        return -imag, real
    if eighths == 4:
        return -real, -imag
    if eighths == 6:
        return imag, -real
    root = math.sqrt(0.5)
    if eighths == 1:
        return root * (real - imag), root * (real + imag)
    if eighths == 3:
        return -root * (real + imag), root * (real - imag)
    if eighths == 5:
        return root * (imag - real), -root * (real + imag)
    if eighths == 7:
        return root * (real + imag), root * (imag - real)
    cosine, sine = math.cos(2 * math.pi * step / length), math.sin(2 * math.pi * step / length)
    return real * cosine - imag * sine, real * sine + imag * cosine


def plus(first, second):
    return first[0] + second[0], first[1] + second[1]


def minus(first, second):
    return first[0] - second[0], first[1] - second[1]


def fourier(values):
    length = len(values)
    if length == 1:
        return values
    if length == 2:
        return [plus(*values), minus(*values)]
    quarter = length // 4
    parts = [fourier(values[start::4]) for start in range(4)]
    out = [None] * length
    for m in range(quarter):
        first, second, third, fourth = (turned(parts[p][m], p * m, length) for p in range(4))
        even, odd = plus(first, third), minus(first, third)
        other, cross = plus(second, fourth), minus(second, fourth)
        cross = (-cross[1], cross[0])
        out[m], out[m + 2 * quarter] = plus(even, other), minus(even, other)
        out[m + quarter], out[m + 3 * quarter] = plus(odd, cross), minus(odd, cross)
    return out


def product(values, high, low):
    head = values.astype(jnp.bfloat16)
    tail = (values - head.astype(jnp.float32)).astype(jnp.bfloat16)

    left, right = jnp.concatenate([head, tail, head], 1), jnp.concatenate([high, high, low], 0)
    return jnp.dot(left, right, preferred_element_type=jnp.float32)


def kernel(count, stacked, joined, spilled, turn, *refs):
    refs = list(refs)
    if stacked:
        whole = refs.pop(0)
        lower, upper = whole.at[:, 0], whole.at[:, 1]
    else:
        lower, upper = refs.pop(0), refs.pop(0)
    if joined:
        older, older_sigma = refs.pop(0), refs.pop(0)
    weight, high_ref, low_ref, twiddle, before, out = refs[:6]
    field = refs[-1]

    def pair_of(source, plane, pairs, comp, pair):
        at = comp * 2 * pairs + pair
        return source[plane, at], source[plane, at + pairs]

    def either_way(act, *sides):
        pl.when(turn[0] == 0)(lambda: act(*sides))
        pl.when(turn[0] == 1)(lambda: act(*(side[::-1] for side in sides)))

    def spot(part):
        return pl.ds(part * LANES, LANES)

    def twist(n):
        return twiddle[n, 0][None, :], twiddle[n, 1][None, :]

    def times(value, factor):
        return value[0] * factor[0] - value[1] * factor[1], value[0] * factor[1] + value[1] * factor[0]

    def forward(halves):
        @pl.loop(0, 2 * count)
        def _(s):
            comp, pair = s // count, s % count
            rows = pl.ds(pl.multiple_of(comp * SLOTS, SLOTS), SLOTS)
            values = [
                pair_of(halves[m // 4 % 2], m // 8 * 4 + m % 4, count, comp, pair) for m in range(ROWS)
            ]
            for n, value in enumerate(fourier(values)):
                real, imag = times(value, twist(n)) if n else value
                field[n, pair, rows, spot(0)] = real
                field[n, pair, rows, spot(1)] = imag

    either_way(forward, (lower, upper))

    block = 32 if count <= ORB else 16
    size = block * count * 2 * SLOTS

    @pl.loop(0, ROWS // block)
    def _(b):
        take = pl.ds(b * block, block)
        high, low = high_ref[...], low_ref[...]
        space = product(field[take].reshape(size, 2 * LANES), high, low)
        space = space.reshape(block * count, 2, SLOTS, 2 * LANES)
        less = space[:, 0, :, :LANES], space[:, 0, :, LANES:]
        great = space[:, 1, :, :LANES], space[:, 1, :, LANES:]

        def bubble(first, other):
            real = first[0] * first[0] - first[1] * first[1]
            imag = 2.0 * first[0] * first[1]
            return -(real * other[0] + imag * other[1]), imag * other[0] - real * other[1]

        sigma = jnp.stack(
            [jnp.concatenate(bubble(less, great), -1), jnp.concatenate(bubble(great, less), -1)], 1
        )
        back = product(sigma.reshape(size, 2 * LANES), high, low)
        field[take] = back.reshape(block, count, 2 * SLOTS, 2 * LANES)

    @pl.loop(0, 2 * count)
    def _(s):
        comp, pair = s // count, s % count
        rows = pl.ds(pl.multiple_of(comp * SLOTS, SLOTS), SLOTS)
        values = [(field[n, pair, rows, spot(0)], field[n, pair, rows, spot(1)]) for n in range(ROWS)]
        values = [times(value, twist(n)) if n else value for n, value in enumerate(values)]
        for m, (real, imag) in enumerate(fourier(values)):
            field[m, pair, rows, spot(0)] = real
            field[m, pair, rows, spot(1)] = imag

    scale = weight[...]

    def contract(plane, half, halves, older_halves):
        m = plane // 4 * 8 + half * 4 + plane % 4

        def sigma(comp, a):
            rows = pl.ds(comp * SLOTS, SLOTS)
            if joined and a == 0:
                return older_sigma[m, rows, spot(0)], older_sigma[m, rows, spot(1)]
            return field[m, a - joined, rows, spot(0)], field[m, a - joined, rows, spot(1)]

        def given(comp, b):
            if joined and b == 0:
                return pair_of(older_halves[half], plane, ORB + 1, comp, ORB)
            return pair_of(halves[half], plane, count, comp, b - joined)

        def memory(a, b):
            left, right = sigma(0, a), given(1, b)
            other, cross = sigma(1, a), given(0, b)
            real = left[0] * right[0] - left[1] * right[1] - other[0] * cross[0] + other[1] * cross[1]
            if a == b:
                return real, None
            imag = left[0] * right[1] + left[1] * right[0] - other[0] * cross[1] - other[1] * cross[0]
            return real, imag

        results = [2.0 * memory(a, a)[0] for a in range(ORB)]
        for a, b in ((0, 1), (0, 2), (1, 2)):
            one, two = memory(a, b), memory(b, a)
            results += [one[0] + two[0], two[1] - one[1]]
        for i, result in enumerate(results):
            spot_out, row = plane * 2 + half, pl.ds(i, 1)
            out[spot_out, row, :] = before[spot_out, row, :] + jnp.sum(result * scale, axis=0, keepdims=True)
        if spilled:
            refs[6][m] = field[m, ORB]

    def contract_all(halves, older_halves):
        @pl.loop(0, PLANE, unroll=2)
        def _(plane):
            for half in range(2):
                contract(plane, half, halves, older_halves)

    olders = (older.at[:, 0], older.at[:, 1]) if joined else (None, None)
    either_way(contract_all, (lower, upper), olders)


def collide(turn, fields, weights, high, low, twiddle, before, older=(), spilled=False):
    stacked, joined = len(fields) == 1, int(len(older) > 0)
    count = ORB + 1 if stacked else ORB - joined
    shapes = [jax.ShapeDtypeStruct((ROWS, PAIRS, LANES), jnp.float32)]
    if spilled:
        shapes.append(jax.ShapeDtypeStruct((ROWS, 2 * SLOTS, 2 * LANES), jnp.float32))
    inputs = (*fields, *older, weights, high, low, twiddle, before)
    return pl.pallas_call(
        functools.partial(kernel, count, stacked, joined, spilled),
        out_shape=shapes,
        in_specs=[pl.BlockSpec(memory_space=pltpu.SMEM)]
        + [pl.BlockSpec(memory_space=pltpu.VMEM)] * len(inputs),
        out_specs=[pl.BlockSpec(memory_space=pltpu.VMEM)] * len(shapes),
        scratch_shapes=[pltpu.VMEM((ROWS, count, 2 * SLOTS, 2 * LANES), jnp.float32)],
        compiler_params=pltpu.CompilerParams(vmem_limit_bytes=24 * 1024 * 1024),
        cost_estimate=pl.CostEstimate(flops=1000000000, bytes_accessed=0, transcendentals=0),
    )(turn, *inputs)


def arrange_kernel(blocks, apart, first, parts, *refs):
    *outs, sems = refs
    copies, base = [], 0
    for pairs in blocks:
        for kind in range(4):
            for i, (a, c) in enumerate(pairs):
                at = base + kind * len(pairs) + i
                for n in range(2):
                    half = first[0] if n == 0 else 1 - first[0]
                    target = outs[n].at[:, at] if apart else outs[0].at[:, n, at]
                    source = parts.at[kind * ORB + a, c, half]
                    copies.append(pltpu.make_async_copy(source, target, sems.at[n, at]))
        base += 4 * len(pairs)
    for copy in copies:
        copy.start()
    for copy in copies:
        copy.wait()


def arrange(first, parts, blocks, apart):
    count = 4 * sum(len(pairs) for pairs in blocks)
    whole = (PLANE, count, SLOTS, LANES) if apart else (PLANE, 2, count, SLOTS, LANES)
    shape = jax.ShapeDtypeStruct(whole, jnp.float32)
    return pl.pallas_call(
        functools.partial(arrange_kernel, blocks, apart),
        out_shape=[shape] * (2 if apart else 1),
        in_specs=[pl.BlockSpec(memory_space=pltpu.SMEM), pl.BlockSpec(memory_space=pl.ANY)],
        out_specs=[pl.BlockSpec(memory_space=pltpu.VMEM)] * (2 if apart else 1),
        scratch_shapes=[pltpu.SemaphoreType.DMA((2, count))],
        compiler_params=pltpu.CompilerParams(vmem_limit_bytes=8 * 1024 * 1024),
        cost_estimate=pl.CostEstimate(flops=0, bytes_accessed=3_200_000, transcendentals=0),
    )(first, parts)


def cut_kernel(base, whole, *refs):
    *outs, sems = refs
    copies = []
    for n, out in enumerate(outs):
        source = whole.at[:, n, pl.ds(base, out.shape[1])]
        copies.append(pltpu.make_async_copy(source, out, sems.at[n]))
    for copy in copies:
        copy.start()
    for copy in copies:
        copy.wait()


def cut(whole, base, size):
    return pl.pallas_call(
        functools.partial(cut_kernel, base),
        out_shape=[jax.ShapeDtypeStruct((PLANE, size, SLOTS, LANES), jnp.float32)] * 2,
        in_specs=[pl.BlockSpec(memory_space=pl.ANY)],
        out_specs=[pl.BlockSpec(memory_space=pltpu.VMEM)] * 2,
        scratch_shapes=[pltpu.SemaphoreType.DMA((2,))],
        compiler_params=pltpu.CompilerParams(vmem_limit_bytes=8 * 1024 * 1024),
        cost_estimate=pl.CostEstimate(flops=0, bytes_accessed=3_200_000, transcendentals=0),
    )(whole)


def settle(weights, fields, cost):
    def body(given, *refs):
        refs[-1][...] = given[...]

    return pl.pallas_call(
        body,
        out_shape=jax.ShapeDtypeStruct((SLOTS, LANES), jnp.float32),
        in_specs=[pl.BlockSpec(memory_space=pltpu.VMEM)] + [pl.BlockSpec(memory_space=pl.ANY)] * len(fields),
        out_specs=pl.BlockSpec(memory_space=pltpu.VMEM),
        compiler_params=pltpu.CompilerParams(vmem_limit_bytes=1024 * 1024),
        cost_estimate=pl.CostEstimate(flops=int(cost * 1e9), bytes_accessed=0, transcendentals=0),
    )(weights, *fields)


def shifted(step):
    return [(z, (z + step) % 8) for z in range(8)]


def per_device(green_row, time_step):
    slot_count = green_row.shape[4]
    history = slot_count * 8
    zh, zl, core = (lax.axis_index(axis) for axis in ("zh", "zl", "core"))
    plane = lax.axis_index("y") * 4 + lax.axis_index("x")
    turn = ((zh * 4 + zl + 2) // 4 + 1) % 2
    origin = (zl + 2) % 4 * 2 + core
    first = origin * slot_count + turn * (slot_count // 2) + plane * SLOTS
    slot_ids = first + jnp.arange(SLOTS, dtype=jnp.int32)
    slot_age = (time_step[0] - 1 - slot_ids) % history + 1
    decays = jnp.exp2(-(slot_age - 1).astype(jnp.float32) / history)
    weights = delta_time * decays * jnp.where(slot_age == history, 0.5, 1.0).astype(jnp.float32)
    weights = jnp.broadcast_to(weights[:, None], (SLOTS, LANES))
    high, low, twiddle = lane_tables()

    parts = green_row.reshape(4 * ORB, ORB, 2, PLANE, SLOTS, LANES)

    def spread(value):
        return lax.all_to_all(value, ("y", "x"), split_axis=0, concat_axis=0)

    def move(rising, falling):
        return (
            lax.ppermute(rising, ("zh", "zl"), shifted(2)),
            lax.ppermute(falling, ("zh", "zl"), shifted(-2)),
        )

    def work(fields, partial, weights, **more):
        return collide(turn_flag, fields, weights, high, low, twiddle, partial, **more)

    turn_flag = turn.reshape(1).astype(jnp.int32)
    partial = jnp.zeros((ROWS, PAIRS, LANES), jnp.float32)
    fence = lax.optimization_barrier
    early = [[(0, 0), (1, 0), (2, 0), (0, 1)]]
    late = [[(1, 1), (2, 1)], [(0, 2), (1, 2), (2, 2)]]

    side = zh.reshape(1).astype(jnp.int32)
    zero = arrange(side, parts, early, True)
    zero, side = fence((zero, side))
    zero = tuple(move(*zero))
    (rest,) = arrange(side, parts, late, False)
    rest = spread(rest)
    zero, rest, weights = fence((zero, rest, settle(weights, zero, 50.0)))
    one = cut(rest, 0, 4 * len(late[0]))
    two = cut(rest, 4 * len(late[0]), 4 * len(late[1]))
    one = tuple(move(*one))
    two = tuple(move(*two))
    zero = spread(jnp.stack(zero, 1))
    one, zero, weights = fence((one, zero, settle(weights, one, 50.0)))
    partial, sigma = work([zero], partial, weights, spilled=True)
    (partial,) = work(one, partial, weights, older=(zero, sigma))
    partial, two = fence((partial, two))
    (partial,) = work(two, partial, weights)
    blocks = partial.reshape(PLANE, 2, PAIRS, LANES)
    owned = jnp.sum(spread(blocks), axis=0)
    share = LANES // 8
    shares = owned.reshape(2, PAIRS, 8, share).transpose(0, 2, 1, 3).reshape(PLANE, 1, PAIRS * share)
    shares = lax.all_to_all(shares, ("zh", "zl", "core"), split_axis=0, concat_axis=0)
    summed = jnp.sum(shares, axis=(0, 1)).reshape(PAIRS, share)
    none = jnp.zeros_like(summed[0])
    real = [summed[0], summed[3], summed[5], summed[3], summed[1], summed[7], summed[5], summed[7], summed[2]]
    imag = [none, summed[4], summed[6], -summed[4], none, summed[8], -summed[6], -summed[8], none]
    return jnp.stack(real + imag).reshape(2, ORB, ORB, -1)


def solution(mesh):
    axes = ("y", "zh", "x", "zl", "core")
    finer = Mesh(mesh.devices.reshape(4, 2, 4, 4, 2), axes)
    mom, hist = axes[:3], axes[3:]
    return jax.shard_map(
        per_device,
        mesh=finer,
        in_specs=(P(None, None, None, None, hist, mom), P()),
        out_specs=P(None, None, None, axes),
        check_vma=False,
    )
```

```python
import functools
import math

import jax
import jax.numpy as jnp
import numpy as np
from jax import lax
from jax.experimental import pallas as pl
from jax.experimental.pallas import tpu as pltpu
from jax.sharding import Mesh
from jax.sharding import PartitionSpec as P

NKX = 64
NKY = 64
ORB = 3
PAIRS = ORB * ORB
ROWS = 32
PLANE = 16
SLOTS = 8
LANES = 128

delta_time = 0.01


def lane_tables():
    index = np.arange(64)
    angle = 2.0 * math.pi * (index[:, None] * index[None, :] % 64) / 64
    sign = np.array([[1.0, 1.0], [1.0, -1.0]])
    cosine = np.kron(sign, np.cos(angle)) / 64
    sine = np.kron(sign, np.sin(angle)) / 64
    table = np.block([[cosine, sine], [-sine, cosine]]).astype(np.float32)
    high = table.astype(jnp.bfloat16)
    low = (table - high.astype(np.float32)).astype(jnp.bfloat16)
    turn = 2.0 * math.pi * np.arange(ROWS)[:, None] * np.repeat([0, 1], 64)[None, :] / 64
    twiddle = np.stack([np.cos(turn), np.sin(turn)], 1).astype(np.float32)
    return high, low, twiddle


def turned(value, step, length):
    real, imag = value
    eighths = step * 8 / length
    if eighths == 0:
        return real, imag
    if eighths == 2:
        return -imag, real
    if eighths == 4:
        return -real, -imag
    if eighths == 6:
        return imag, -real
    root = math.sqrt(0.5)
    if eighths == 1:
        return root * (real - imag), root * (real + imag)
    if eighths == 3:
        return -root * (real + imag), root * (real - imag)
    if eighths == 5:
        return root * (imag - real), -root * (real + imag)
    if eighths == 7:
        return root * (real + imag), root * (imag - real)
    cosine, sine = math.cos(2 * math.pi * step / length), math.sin(2 * math.pi * step / length)
    return real * cosine - imag * sine, real * sine + imag * cosine


def plus(first, second):
    return first[0] + second[0], first[1] + second[1]


def minus(first, second):
    return first[0] - second[0], first[1] - second[1]


def fourier(values):
    length = len(values)
    if length == 1:
        return values
    if length == 2:
        return [plus(*values), minus(*values)]
    quarter = length // 4
    parts = [fourier(values[start::4]) for start in range(4)]
    out = [None] * length
    for m in range(quarter):
        first, second, third, fourth = (turned(parts[p][m], p * m, length) for p in range(4))
        even, odd = plus(first, third), minus(first, third)
        other, cross = plus(second, fourth), minus(second, fourth)
        cross = (-cross[1], cross[0])
        out[m], out[m + 2 * quarter] = plus(even, other), minus(even, other)
        out[m + quarter], out[m + 3 * quarter] = plus(odd, cross), minus(odd, cross)
    return out


def product(values, high, low):
    head = values.astype(jnp.bfloat16)
    tail = (values - head.astype(jnp.float32)).astype(jnp.bfloat16)

    left, right = jnp.concatenate([head, tail, head], 1), jnp.concatenate([high, high, low], 0)
    return jnp.dot(left, right, preferred_element_type=jnp.float32)


def kernel(count, stacked, joined, spilled, turn, *refs):
    refs = list(refs)
    if stacked:
        whole = refs.pop(0)
        lower, upper = whole.at[:, 0], whole.at[:, 1]
    else:
        lower, upper = refs.pop(0), refs.pop(0)
    if joined:
        older, older_sigma = refs.pop(0), refs.pop(0)
    weight, high_ref, low_ref, twiddle, before, out = refs[:6]
    field = refs[-1]

    def pair_of(source, plane, pairs, comp, pair):
        at = comp * 2 * pairs + pair
        return source[plane, at], source[plane, at + pairs]

    def either_way(act, *sides):
        pl.when(turn[0] == 0)(lambda: act(*sides))
        pl.when(turn[0] == 1)(lambda: act(*(side[::-1] for side in sides)))

    def spot(part):
        return pl.ds(part * LANES, LANES)

    def twist(n):
        return twiddle[n, 0][None, :], twiddle[n, 1][None, :]

    def times(value, factor):
        return value[0] * factor[0] - value[1] * factor[1], value[0] * factor[1] + value[1] * factor[0]

    def forward(halves):
        @pl.loop(0, 2 * count)
        def _(s):
            comp, pair = s // count, s % count
            rows = pl.ds(pl.multiple_of(comp * SLOTS, SLOTS), SLOTS)
            values = [
                pair_of(halves[m // 4 % 2], m // 8 * 4 + m % 4, count, comp, pair) for m in range(ROWS)
            ]
            for n, value in enumerate(fourier(values)):
                real, imag = times(value, twist(n)) if n else value
                field[n, pair, rows, spot(0)] = real
                field[n, pair, rows, spot(1)] = imag

    either_way(forward, (lower, upper))

    block = 32 if count <= ORB else 16
    size = block * count * 2 * SLOTS

    @pl.loop(0, ROWS // block)
    def _(b):
        take = pl.ds(b * block, block)
        high, low = high_ref[...], low_ref[...]
        space = product(field[take].reshape(size, 2 * LANES), high, low)
        space = space.reshape(block * count, 2, SLOTS, 2 * LANES)
        less = space[:, 0, :, :LANES], space[:, 0, :, LANES:]
        great = space[:, 1, :, :LANES], space[:, 1, :, LANES:]

        def bubble(first, other):
            real = first[0] * first[0] - first[1] * first[1]
            imag = 2.0 * first[0] * first[1]
            return -(real * other[0] + imag * other[1]), imag * other[0] - real * other[1]

        sigma = jnp.stack(
            [jnp.concatenate(bubble(less, great), -1), jnp.concatenate(bubble(great, less), -1)], 1
        )
        back = product(sigma.reshape(size, 2 * LANES), high, low)
        field[take] = back.reshape(block, count, 2 * SLOTS, 2 * LANES)

    @pl.loop(0, 2 * count)
    def _(s):
        comp, pair = s // count, s % count
        rows = pl.ds(pl.multiple_of(comp * SLOTS, SLOTS), SLOTS)
        values = [(field[n, pair, rows, spot(0)], field[n, pair, rows, spot(1)]) for n in range(ROWS)]
        values = [times(value, twist(n)) if n else value for n, value in enumerate(values)]
        for m, (real, imag) in enumerate(fourier(values)):
            field[m, pair, rows, spot(0)] = real
            field[m, pair, rows, spot(1)] = imag

    scale = weight[...]

    def contract(plane, half, halves, older_halves):
        m = plane // 4 * 8 + half * 4 + plane % 4

        def sigma(comp, a):
            rows = pl.ds(comp * SLOTS, SLOTS)
            if joined and a == 0:
                return older_sigma[m, rows, spot(0)], older_sigma[m, rows, spot(1)]
            return field[m, a - joined, rows, spot(0)], field[m, a - joined, rows, spot(1)]

        def given(comp, b):
            if joined and b == 0:
                return pair_of(older_halves[half], plane, ORB + 1, comp, ORB)
            return pair_of(halves[half], plane, count, comp, b - joined)

        def memory(a, b):
            left, right = sigma(0, a), given(1, b)
            other, cross = sigma(1, a), given(0, b)
            real = left[0] * right[0] - left[1] * right[1] - other[0] * cross[0] + other[1] * cross[1]
            if a == b:
                return real, None
            imag = left[0] * right[1] + left[1] * right[0] - other[0] * cross[1] - other[1] * cross[0]
            return real, imag

        results = [2.0 * memory(a, a)[0] for a in range(ORB)]
        for a, b in ((0, 1), (0, 2), (1, 2)):
            one, two = memory(a, b), memory(b, a)
            results += [one[0] + two[0], two[1] - one[1]]
        for i, result in enumerate(results):
            spot_out, row = plane * 2 + half, pl.ds(i, 1)
            out[spot_out, row, :] = before[spot_out, row, :] + jnp.sum(result * scale, axis=0, keepdims=True)
        if spilled:
            refs[6][m] = field[m, ORB]

    def contract_all(halves, older_halves):
        @pl.loop(0, PLANE, unroll=2)
        def _(plane):
            for half in range(2):
                contract(plane, half, halves, older_halves)

    olders = (older.at[:, 0], older.at[:, 1]) if joined else (None, None)
    either_way(contract_all, (lower, upper), olders)


def collide(turn, fields, weights, high, low, twiddle, before, older=(), spilled=False):
    stacked, joined = len(fields) == 1, int(len(older) > 0)
    count = ORB + 1 if stacked else ORB - joined
    shapes = [jax.ShapeDtypeStruct((ROWS, PAIRS, LANES), jnp.float32)]
    if spilled:
        shapes.append(jax.ShapeDtypeStruct((ROWS, 2 * SLOTS, 2 * LANES), jnp.float32))
    inputs = (*fields, *older, weights, high, low, twiddle, before)
    return pl.pallas_call(
        functools.partial(kernel, count, stacked, joined, spilled),
        out_shape=shapes,
        in_specs=[pl.BlockSpec(memory_space=pltpu.SMEM)]
        + [pl.BlockSpec(memory_space=pltpu.VMEM)] * len(inputs),
        out_specs=[pl.BlockSpec(memory_space=pltpu.VMEM)] * len(shapes),
        scratch_shapes=[pltpu.VMEM((ROWS, count, 2 * SLOTS, 2 * LANES), jnp.float32)],
        compiler_params=pltpu.CompilerParams(vmem_limit_bytes=24 * 1024 * 1024),
        cost_estimate=pl.CostEstimate(flops=1000000000, bytes_accessed=0, transcendentals=0),
    )(turn, *inputs)


def arrange_kernel(blocks, apart, first, parts, *refs):
    *outs, sems = refs
    copies, base = [], 0
    for pairs in blocks:
        for kind in range(4):
            for i, (a, c) in enumerate(pairs):
                at = base + kind * len(pairs) + i
                for n in range(2):
                    half = first[0] if n == 0 else 1 - first[0]
                    target = outs[n].at[:, at] if apart else outs[0].at[:, n, at]
                    source = parts.at[kind * ORB + a, c, half]
                    copies.append(pltpu.make_async_copy(source, target, sems.at[n, at]))
        base += 4 * len(pairs)
    for copy in copies:
        copy.start()
    for copy in copies:
        copy.wait()


def arrange(first, parts, blocks, apart):
    count = 4 * sum(len(pairs) for pairs in blocks)
    whole = (PLANE, count, SLOTS, LANES) if apart else (PLANE, 2, count, SLOTS, LANES)
    shape = jax.ShapeDtypeStruct(whole, jnp.float32)
    return pl.pallas_call(
        functools.partial(arrange_kernel, blocks, apart),
        out_shape=[shape] * (2 if apart else 1),
        in_specs=[pl.BlockSpec(memory_space=pltpu.SMEM), pl.BlockSpec(memory_space=pl.ANY)],
        out_specs=[pl.BlockSpec(memory_space=pltpu.VMEM)] * (2 if apart else 1),
        scratch_shapes=[pltpu.SemaphoreType.DMA((2, count))],
        compiler_params=pltpu.CompilerParams(vmem_limit_bytes=8 * 1024 * 1024),
        cost_estimate=pl.CostEstimate(flops=0, bytes_accessed=3_200_000, transcendentals=0),
    )(first, parts)


def cut_kernel(base, whole, *refs):
    *outs, sems = refs
    copies = []
    for n, out in enumerate(outs):
        source = whole.at[:, n, pl.ds(base, out.shape[1])]
        copies.append(pltpu.make_async_copy(source, out, sems.at[n]))
    for copy in copies:
        copy.start()
    for copy in copies:
        copy.wait()


def cut(whole, base, size):
    return pl.pallas_call(
        functools.partial(cut_kernel, base),
        out_shape=[jax.ShapeDtypeStruct((PLANE, size, SLOTS, LANES), jnp.float32)] * 2,
        in_specs=[pl.BlockSpec(memory_space=pl.ANY)],
        out_specs=[pl.BlockSpec(memory_space=pltpu.VMEM)] * 2,
        scratch_shapes=[pltpu.SemaphoreType.DMA((2,))],
        compiler_params=pltpu.CompilerParams(vmem_limit_bytes=8 * 1024 * 1024),
        cost_estimate=pl.CostEstimate(flops=0, bytes_accessed=3_200_000, transcendentals=0),
    )(whole)


def settle(weights, fields, cost):
    def body(given, *refs):
        refs[-1][...] = given[...]

    return pl.pallas_call(
        body,
        out_shape=jax.ShapeDtypeStruct((SLOTS, LANES), jnp.float32),
        in_specs=[pl.BlockSpec(memory_space=pltpu.VMEM)] + [pl.BlockSpec(memory_space=pl.ANY)] * len(fields),
        out_specs=pl.BlockSpec(memory_space=pltpu.VMEM),
        compiler_params=pltpu.CompilerParams(vmem_limit_bytes=1024 * 1024),
        cost_estimate=pl.CostEstimate(flops=int(cost * 1e9), bytes_accessed=0, transcendentals=0),
    )(weights, *fields)


def per_device(green_row, time_step):
    slot_count = green_row.shape[4]
    history = slot_count * 8
    zh, zl, core = (lax.axis_index(axis) for axis in ("zh", "zl", "core"))
    plane = lax.axis_index("y") * 4 + lax.axis_index("x")
    first = (zl * 2 + core) * slot_count + zh * (slot_count // 2) + plane * SLOTS
    slot_ids = first + jnp.arange(SLOTS, dtype=jnp.int32)
    slot_age = (time_step[0] - 1 - slot_ids) % history + 1
    decays = jnp.exp2(-(slot_age - 1).astype(jnp.float32) / history)
    weights = delta_time * decays * jnp.where(slot_age == history, 0.5, 1.0).astype(jnp.float32)
    weights = jnp.broadcast_to(weights[:, None], (SLOTS, LANES))
    high, low, twiddle = lane_tables()

    parts = green_row.reshape(4 * ORB, ORB, 2, PLANE, SLOTS, LANES)

    def spread(value):
        return lax.all_to_all(value, ("y", "x"), split_axis=0, concat_axis=0)

    def move(kept, sent):
        return kept, lax.ppermute(sent, "zh", [(0, 1), (1, 0)])

    def work(fields, partial, weights, **more):
        return collide(turn_flag, fields, weights, high, low, twiddle, partial, **more)

    turn_flag = zh.reshape(1).astype(jnp.int32)
    partial = jnp.zeros((ROWS, PAIRS, LANES), jnp.float32)
    fence = lax.optimization_barrier
    early = [[(0, 0), (1, 0), (2, 0), (0, 1)]]
    late = [[(1, 1), (2, 1)], [(0, 2), (1, 2), (2, 2)]]

    side = zh.reshape(1).astype(jnp.int32)
    zero = arrange(side, parts, early, True)
    zero, side = fence((zero, side))
    zero = tuple(move(*zero))
    (rest,) = arrange(side, parts, late, False)
    rest = spread(rest)
    zero, rest, weights = fence((zero, rest, settle(weights, zero[1:], 50.0)))
    one = cut(rest, 0, 4 * len(late[0]))
    two = cut(rest, 4 * len(late[0]), 4 * len(late[1]))
    one = tuple(move(*one))
    two = tuple(move(*two))
    zero = spread(jnp.stack(zero, 1))
    one, zero, weights = fence((one, zero, settle(weights, one[1:], 50.0)))
    partial, sigma = work([zero], partial, weights, spilled=True)
    (partial,) = work(one, partial, weights, older=(zero, sigma))
    partial, two = fence((partial, two))
    (partial,) = work(two, partial, weights)
    blocks = partial.reshape(PLANE, 2, PAIRS, LANES)
    owned = jnp.sum(spread(blocks), axis=0)
    share = LANES // 8
    shares = owned.reshape(2, PAIRS, 8, share).transpose(0, 2, 1, 3).reshape(PLANE, 1, PAIRS * share)
    shares = lax.all_to_all(shares, ("zh", "zl", "core"), split_axis=0, concat_axis=0)
    summed = jnp.sum(shares, axis=(0, 1)).reshape(PAIRS, share)
    none = jnp.zeros_like(summed[0])
    real = [summed[0], summed[3], summed[5], summed[3], summed[1], summed[7], summed[5], summed[7], summed[2]]
    imag = [none, summed[4], summed[6], -summed[4], none, summed[8], -summed[6], -summed[8], none]
    return jnp.stack(real + imag).reshape(2, ORB, ORB, -1)


def solution(mesh):
    axes = ("y", "zh", "x", "zl", "core")
    finer = Mesh(mesh.devices.reshape(4, 2, 4, 4, 2), axes)
    mom, hist = axes[:3], axes[3:]
    return jax.shard_map(
        per_device,
        mesh=finer,
        in_specs=(P(None, None, None, None, hist, mom), P()),
        out_specs=P(None, None, None, axes),
        check_vma=False,
    )
```

```python
import functools
import math

import jax
import jax.numpy as jnp
import numpy as np
from jax import lax
from jax.experimental import pallas as pl
from jax.experimental.pallas import tpu as pltpu
from jax.sharding import Mesh
from jax.sharding import PartitionSpec as P

NKX = 64
NKY = 64
ORB = 3
PAIRS = ORB * ORB
ROWS = 32
PLANE = 16
SLOTS = 8
LANES = 128

delta_time = 0.01


def lane_tables():
    index = np.arange(64)
    angle = 2.0 * math.pi * (index[:, None] * index[None, :] % 64) / 64
    sign = np.array([[1.0, 1.0], [1.0, -1.0]])
    cosine = np.kron(sign, np.cos(angle)) / 64
    sine = np.kron(sign, np.sin(angle)) / 64
    table = np.block([[cosine, sine], [-sine, cosine]]).astype(np.float32)
    high = table.astype(jnp.bfloat16)
    low = (table - high.astype(np.float32)).astype(jnp.bfloat16)
    turn = 2.0 * math.pi * np.arange(ROWS)[:, None] * np.repeat([0, 1], 64)[None, :] / 64
    twiddle = np.stack([np.cos(turn), np.sin(turn)], 1).astype(np.float32)
    return high, low, twiddle


def turned(value, step, length):
    real, imag = value
    eighths = step * 8 / length
    if eighths == 0:
        return real, imag
    if eighths == 2:
        return -imag, real
    if eighths == 4:
        return -real, -imag
    if eighths == 6:
        return imag, -real
    root = math.sqrt(0.5)
    if eighths == 1:
        return root * (real - imag), root * (real + imag)
    if eighths == 3:
        return -root * (real + imag), root * (real - imag)
    if eighths == 5:
        return root * (imag - real), -root * (real + imag)
    if eighths == 7:
        return root * (real + imag), root * (imag - real)
    cosine, sine = math.cos(2 * math.pi * step / length), math.sin(2 * math.pi * step / length)
    return real * cosine - imag * sine, real * sine + imag * cosine


def plus(first, second):
    return first[0] + second[0], first[1] + second[1]


def minus(first, second):
    return first[0] - second[0], first[1] - second[1]


def fourier(values):
    length = len(values)
    if length == 1:
        return values
    if length == 2:
        return [plus(*values), minus(*values)]
    quarter = length // 4
    parts = [fourier(values[start::4]) for start in range(4)]
    out = [None] * length
    for m in range(quarter):
        first, second, third, fourth = (turned(parts[p][m], p * m, length) for p in range(4))
        even, odd = plus(first, third), minus(first, third)
        other, cross = plus(second, fourth), minus(second, fourth)
        cross = (-cross[1], cross[0])
        out[m], out[m + 2 * quarter] = plus(even, other), minus(even, other)
        out[m + quarter], out[m + 3 * quarter] = plus(odd, cross), minus(odd, cross)
    return out


def product(values, high, low):
    head = values.astype(jnp.bfloat16)
    tail = (values - head.astype(jnp.float32)).astype(jnp.bfloat16)

    left, right = jnp.concatenate([head, tail, head], 1), jnp.concatenate([high, high, low], 0)
    return jnp.dot(left, right, preferred_element_type=jnp.float32)


def kernel(count, stacked, joined, spilled, turn, *refs):
    refs = list(refs)
    if stacked:
        whole = refs.pop(0)
        lower, upper = whole.at[:, 0], whole.at[:, 1]
    else:
        lower, upper = refs.pop(0), refs.pop(0)
    if joined:
        older, older_sigma = refs.pop(0), refs.pop(0)
    weight, high_ref, low_ref, twiddle, before, out = refs[:6]
    field = refs[-1]

    def pair_of(source, plane, pairs, comp, pair):
        at = comp * 2 * pairs + pair
        return source[plane, at], source[plane, at + pairs]

    def either_way(act, *sides):
        pl.when(turn[0] == 0)(lambda: act(*sides))
        pl.when(turn[0] == 1)(lambda: act(*(side[::-1] for side in sides)))

    def spot(part):
        return pl.ds(part * LANES, LANES)

    def twist(n):
        return twiddle[n, 0][None, :], twiddle[n, 1][None, :]

    def times(value, factor):
        return value[0] * factor[0] - value[1] * factor[1], value[0] * factor[1] + value[1] * factor[0]

    def forward(halves):
        @pl.loop(0, 2 * count)
        def _(s):
            comp, pair = s // count, s % count
            rows = pl.ds(pl.multiple_of(comp * SLOTS, SLOTS), SLOTS)
            values = [
                pair_of(halves[m // 4 % 2], m // 8 * 4 + m % 4, count, comp, pair) for m in range(ROWS)
            ]
            for n, value in enumerate(fourier(values)):
                real, imag = times(value, twist(n)) if n else value
                field[n, pair, rows, spot(0)] = real
                field[n, pair, rows, spot(1)] = imag

    either_way(forward, (lower, upper))

    block = 32 if count <= ORB else 16
    size = block * count * 2 * SLOTS

    @pl.loop(0, ROWS // block)
    def _(b):
        take = pl.ds(b * block, block)
        high, low = high_ref[...], low_ref[...]
        space = product(field[take].reshape(size, 2 * LANES), high, low)
        space = space.reshape(block * count, 2, SLOTS, 2 * LANES)
        less = space[:, 0, :, :LANES], space[:, 0, :, LANES:]
        great = space[:, 1, :, :LANES], space[:, 1, :, LANES:]

        def bubble(first, other):
            real = first[0] * first[0] - first[1] * first[1]
            imag = 2.0 * first[0] * first[1]
            return -(real * other[0] + imag * other[1]), imag * other[0] - real * other[1]

        sigma = jnp.stack(
            [jnp.concatenate(bubble(less, great), -1), jnp.concatenate(bubble(great, less), -1)], 1
        )
        back = product(sigma.reshape(size, 2 * LANES), high, low)
        field[take] = back.reshape(block, count, 2 * SLOTS, 2 * LANES)

    @pl.loop(0, 2 * count)
    def _(s):
        comp, pair = s // count, s % count
        rows = pl.ds(pl.multiple_of(comp * SLOTS, SLOTS), SLOTS)
        values = [(field[n, pair, rows, spot(0)], field[n, pair, rows, spot(1)]) for n in range(ROWS)]
        values = [times(value, twist(n)) if n else value for n, value in enumerate(values)]
        for m, (real, imag) in enumerate(fourier(values)):
            field[m, pair, rows, spot(0)] = real
            field[m, pair, rows, spot(1)] = imag

    scale = weight[...]

    def contract(plane, half, halves, older_halves):
        m = plane // 4 * 8 + half * 4 + plane % 4

        def sigma(comp, a):
            rows = pl.ds(comp * SLOTS, SLOTS)
            if joined and a == 0:
                return older_sigma[m, rows, spot(0)], older_sigma[m, rows, spot(1)]
            return field[m, a - joined, rows, spot(0)], field[m, a - joined, rows, spot(1)]

        def given(comp, b):
            if joined and b == 0:
                return pair_of(older_halves[half], plane, ORB + 1, comp, ORB)
            return pair_of(halves[half], plane, count, comp, b - joined)

        def memory(a, b):
            left, right = sigma(0, a), given(1, b)
            other, cross = sigma(1, a), given(0, b)
            real = left[0] * right[0] - left[1] * right[1] - other[0] * cross[0] + other[1] * cross[1]
            if a == b:
                return real, None
            imag = left[0] * right[1] + left[1] * right[0] - other[0] * cross[1] - other[1] * cross[0]
            return real, imag

        results = [2.0 * memory(a, a)[0] for a in range(ORB)]
        for a, b in ((0, 1), (0, 2), (1, 2)):
            one, two = memory(a, b), memory(b, a)
            results += [one[0] + two[0], two[1] - one[1]]
        for i, result in enumerate(results):
            spot_out, row = plane * 2 + half, pl.ds(i, 1)
            out[spot_out, row, :] = before[spot_out, row, :] + jnp.sum(result * scale, axis=0, keepdims=True)
        if spilled:
            refs[6][m] = field[m, ORB]

    def contract_all(halves, older_halves):
        @pl.loop(0, PLANE, unroll=2)
        def _(plane):
            for half in range(2):
                contract(plane, half, halves, older_halves)

    olders = (older.at[:, 0], older.at[:, 1]) if joined else (None, None)
    either_way(contract_all, (lower, upper), olders)


def collide(turn, fields, weights, high, low, twiddle, before, older=(), spilled=False):
    stacked, joined = len(fields) == 1, int(len(older) > 0)
    count = ORB + 1 if stacked else ORB - joined
    shapes = [jax.ShapeDtypeStruct((ROWS, PAIRS, LANES), jnp.float32)]
    if spilled:
        shapes.append(jax.ShapeDtypeStruct((ROWS, 2 * SLOTS, 2 * LANES), jnp.float32))
    inputs = (*fields, *older, weights, high, low, twiddle, before)
    return pl.pallas_call(
        functools.partial(kernel, count, stacked, joined, spilled),
        out_shape=shapes,
        in_specs=[pl.BlockSpec(memory_space=pltpu.SMEM)]
        + [pl.BlockSpec(memory_space=pltpu.VMEM)] * len(inputs),
        out_specs=[pl.BlockSpec(memory_space=pltpu.VMEM)] * len(shapes),
        scratch_shapes=[pltpu.VMEM((ROWS, count, 2 * SLOTS, 2 * LANES), jnp.float32)],
        compiler_params=pltpu.CompilerParams(vmem_limit_bytes=24 * 1024 * 1024),
        cost_estimate=pl.CostEstimate(flops=1000000000, bytes_accessed=0, transcendentals=0),
    )(turn, *inputs)


def arrange_kernel(blocks, ways, first, parts, out, sems):
    copies, base = [], 0
    for pairs in blocks:
        for kind in range(4):
            for i, (a, c) in enumerate(pairs):
                at = base + kind * len(pairs) + i
                for n, way in enumerate(ways):
                    half = first[0] if way == 0 else 1 - first[0]
                    target = out.at[:, n, at] if len(ways) > 1 else out.at[:, at]
                    source = parts.at[kind * ORB + a, c, half]
                    copies.append(pltpu.make_async_copy(source, target, sems.at[n, at]))
        base += 4 * len(pairs)
    for copy in copies:
        copy.start()
    for copy in copies:
        copy.wait()


def arrange(first, parts, blocks, ways):
    count = 4 * sum(len(pairs) for pairs in blocks)
    shape = (PLANE, *((len(ways),) if len(ways) > 1 else ()), count, SLOTS, LANES)
    return pl.pallas_call(
        functools.partial(arrange_kernel, blocks, ways),
        out_shape=jax.ShapeDtypeStruct(shape, jnp.float32),
        in_specs=[pl.BlockSpec(memory_space=pltpu.SMEM), pl.BlockSpec(memory_space=pl.ANY)],
        out_specs=pl.BlockSpec(memory_space=pltpu.VMEM),
        scratch_shapes=[pltpu.SemaphoreType.DMA((len(ways), count))],
        compiler_params=pltpu.CompilerParams(vmem_limit_bytes=60 * 1024 * 1024),
        cost_estimate=pl.CostEstimate(flops=0, bytes_accessed=3_200_000, transcendentals=0),
    )(first, parts)


def cut_kernel(base, whole, *refs):
    *outs, sems = refs
    copies = []
    for n, out in enumerate(outs):
        source = whole.at[:, n, pl.ds(base, out.shape[1])]
        copies.append(pltpu.make_async_copy(source, out, sems.at[n]))
    for copy in copies:
        copy.start()
    for copy in copies:
        copy.wait()


def cut(whole, base, size):
    return pl.pallas_call(
        functools.partial(cut_kernel, base),
        out_shape=[jax.ShapeDtypeStruct((PLANE, size, SLOTS, LANES), jnp.float32)] * 2,
        in_specs=[pl.BlockSpec(memory_space=pl.ANY)],
        out_specs=[pl.BlockSpec(memory_space=pltpu.VMEM)] * 2,
        scratch_shapes=[pltpu.SemaphoreType.DMA((2,))],
        compiler_params=pltpu.CompilerParams(vmem_limit_bytes=8 * 1024 * 1024),
        cost_estimate=pl.CostEstimate(flops=0, bytes_accessed=3_200_000, transcendentals=0),
    )(whole)


def settle(weights, fields, cost):
    def body(given, *refs):
        refs[-1][...] = given[...]

    return pl.pallas_call(
        body,
        out_shape=jax.ShapeDtypeStruct((SLOTS, LANES), jnp.float32),
        in_specs=[pl.BlockSpec(memory_space=pltpu.VMEM)] + [pl.BlockSpec(memory_space=pl.ANY)] * len(fields),
        out_specs=pl.BlockSpec(memory_space=pltpu.VMEM),
        compiler_params=pltpu.CompilerParams(vmem_limit_bytes=1024 * 1024),
        cost_estimate=pl.CostEstimate(flops=int(cost * 1e9), bytes_accessed=0, transcendentals=0),
    )(weights, *fields)


def per_device(green_row, time_step):
    slot_count = green_row.shape[4]
    history = slot_count * 8
    zh, zl, core = (lax.axis_index(axis) for axis in ("zh", "zl", "core"))
    plane = lax.axis_index("y") * 4 + lax.axis_index("x")
    first = (zl * 2 + core) * slot_count + zh * (slot_count // 2) + plane * SLOTS
    slot_ids = first + jnp.arange(SLOTS, dtype=jnp.int32)
    slot_age = (time_step[0] - 1 - slot_ids) % history + 1
    decays = jnp.exp2(-(slot_age - 1).astype(jnp.float32) / history)
    weights = delta_time * decays * jnp.where(slot_age == history, 0.5, 1.0).astype(jnp.float32)
    weights = jnp.broadcast_to(weights[:, None], (SLOTS, LANES))
    high, low, twiddle = lane_tables()

    parts = green_row.reshape(4 * ORB, ORB, 2, PLANE, SLOTS, LANES)

    def spread(value):
        return lax.all_to_all(value, ("y", "x"), split_axis=0, concat_axis=0)

    def move(value):
        return lax.ppermute(value, "zh", [(0, 1), (1, 0)])

    def work(fields, partial, weights, **more):
        return collide(turn_flag, fields, weights, high, low, twiddle, partial, **more)

    turn_flag = zh.reshape(1).astype(jnp.int32)
    partial = jnp.zeros((ROWS, PAIRS, LANES), jnp.float32)
    fence = lax.optimization_barrier
    early = [[(0, 0), (1, 0), (2, 0), (0, 1)]]
    late = [[(1, 1), (2, 1)], [(0, 2), (1, 2), (2, 2)]]

    side = zh.reshape(1).astype(jnp.int32)
    sent = arrange(side, parts, early, (1,))
    sent, side = fence((sent, side))
    landed = move(sent)
    rest = arrange(side, parts, late, (0, 1))
    rest = spread(rest)
    kept = arrange(side, parts, early, (0,))
    kept, weights = fence((kept, weights))
    landed, rest, weights = fence((landed, rest, settle(weights, [landed], 50.0)))
    one = cut(rest, 0, 4 * len(late[0]))
    two = cut(rest, 4 * len(late[0]), 4 * len(late[1]))
    one, two = (one[0], move(one[1])), (two[0], move(two[1]))
    zero = spread(jnp.stack([kept, landed], 1))
    one, zero, weights = fence((one, zero, settle(weights, one[1:], 50.0)))
    partial, sigma = work([zero], partial, weights, spilled=True)
    (partial,) = work(one, partial, weights, older=(zero, sigma))
    partial, two = fence((partial, two))
    (partial,) = work(two, partial, weights)
    blocks = partial.reshape(PLANE, 2, PAIRS, LANES)
    owned = jnp.sum(spread(blocks), axis=0)
    share = LANES // 8
    shares = owned.reshape(2, PAIRS, 8, share).transpose(0, 2, 1, 3).reshape(PLANE, 1, PAIRS * share)
    shares = lax.all_to_all(shares, ("zh", "zl", "core"), split_axis=0, concat_axis=0)
    summed = jnp.sum(shares, axis=(0, 1)).reshape(PAIRS, share)
    none = jnp.zeros_like(summed[0])
    real = [summed[0], summed[3], summed[5], summed[3], summed[1], summed[7], summed[5], summed[7], summed[2]]
    imag = [none, summed[4], summed[6], -summed[4], none, summed[8], -summed[6], -summed[8], none]
    return jnp.stack(real + imag).reshape(2, ORB, ORB, -1)


def solution(mesh):
    axes = ("y", "zh", "x", "zl", "core")
    finer = Mesh(mesh.devices.reshape(4, 2, 4, 4, 2), axes)
    mom, hist = axes[:3], axes[3:]
    return jax.shard_map(
        per_device,
        mesh=finer,
        in_specs=(P(None, None, None, None, hist, mom), P()),
        out_specs=P(None, None, None, axes),
        check_vma=False,
    )
```

```python
import functools
import math

import jax
import jax.numpy as jnp
import numpy as np
from jax import lax
from jax.experimental import pallas as pl
from jax.experimental.pallas import tpu as pltpu
from jax.sharding import Mesh
from jax.sharding import PartitionSpec as P

NKX = 64
NKY = 64
ORB = 3
PAIRS = ORB * ORB
ROWS = 32
PLANE = 16
SLOTS = 8
LANES = 128

delta_time = 0.01


def lane_tables():
    index = np.arange(64)
    angle = 2.0 * math.pi * (index[:, None] * index[None, :] % 64) / 64
    sign = np.array([[1.0, 1.0], [1.0, -1.0]])
    cosine = np.kron(sign, np.cos(angle)) / 64
    sine = np.kron(sign, np.sin(angle)) / 64
    table = np.block([[cosine, sine], [-sine, cosine]]).astype(np.float32)
    high = table.astype(jnp.bfloat16)
    low = (table - high.astype(np.float32)).astype(jnp.bfloat16)
    turn = 2.0 * math.pi * np.arange(ROWS)[:, None] * np.repeat([0, 1], 64)[None, :] / 64
    twiddle = np.stack([np.cos(turn), np.sin(turn)], 1).astype(np.float32)
    return high, low, twiddle


def turned(value, step, length):
    real, imag = value
    eighths = step * 8 / length
    if eighths == 0:
        return real, imag
    if eighths == 2:
        return -imag, real
    if eighths == 4:
        return -real, -imag
    if eighths == 6:
        return imag, -real
    root = math.sqrt(0.5)
    if eighths == 1:
        return root * (real - imag), root * (real + imag)
    if eighths == 3:
        return -root * (real + imag), root * (real - imag)
    if eighths == 5:
        return root * (imag - real), -root * (real + imag)
    if eighths == 7:
        return root * (real + imag), root * (imag - real)
    cosine, sine = math.cos(2 * math.pi * step / length), math.sin(2 * math.pi * step / length)
    return real * cosine - imag * sine, real * sine + imag * cosine


def plus(first, second):
    return first[0] + second[0], first[1] + second[1]


def minus(first, second):
    return first[0] - second[0], first[1] - second[1]


def fourier(values):
    length = len(values)
    if length == 1:
        return values
    if length == 2:
        return [plus(*values), minus(*values)]
    quarter = length // 4
    parts = [fourier(values[start::4]) for start in range(4)]
    out = [None] * length
    for m in range(quarter):
        first, second, third, fourth = (turned(parts[p][m], p * m, length) for p in range(4))
        even, odd = plus(first, third), minus(first, third)
        other, cross = plus(second, fourth), minus(second, fourth)
        cross = (-cross[1], cross[0])
        out[m], out[m + 2 * quarter] = plus(even, other), minus(even, other)
        out[m + quarter], out[m + 3 * quarter] = plus(odd, cross), minus(odd, cross)
    return out


def product(values, high, low):
    head = values.astype(jnp.bfloat16)
    tail = (values - head.astype(jnp.float32)).astype(jnp.bfloat16)

    left, right = jnp.concatenate([head, tail, head], 1), jnp.concatenate([high, high, low], 0)
    return jnp.dot(left, right, preferred_element_type=jnp.float32)


def kernel(count, stacked, joined, spilled, turn, *refs):
    refs = list(refs)
    if stacked:
        whole = refs.pop(0)
        lower, upper = whole.at[:, 0], whole.at[:, 1]
    else:
        lower, upper = refs.pop(0), refs.pop(0)
    if joined:
        older, older_sigma = refs.pop(0), refs.pop(0)
    weight, high_ref, low_ref, twiddle, before, out = refs[:6]
    field = refs[-1]

    def pair_of(source, plane, pairs, comp, pair):
        size = 2 if pairs == ORB + 1 else pairs
        at = pair // size * 4 * size + 2 * comp * size + pair % size
        return source[plane, at], source[plane, at + size]

    def either_way(act, *sides):
        pl.when(turn[0] == 0)(lambda: act(*sides))
        pl.when(turn[0] == 1)(lambda: act(*(side[::-1] for side in sides)))

    def spot(part):
        return pl.ds(part * LANES, LANES)

    def twist(n):
        return twiddle[n, 0][None, :], twiddle[n, 1][None, :]

    def times(value, factor):
        return value[0] * factor[0] - value[1] * factor[1], value[0] * factor[1] + value[1] * factor[0]

    def forward(halves):
        @pl.loop(0, 2 * count)
        def _(s):
            comp, pair = s // count, s % count
            rows = pl.ds(pl.multiple_of(comp * SLOTS, SLOTS), SLOTS)
            values = [
                pair_of(halves[m // 4 % 2], m // 8 * 4 + m % 4, count, comp, pair) for m in range(ROWS)
            ]
            for n, value in enumerate(fourier(values)):
                real, imag = times(value, twist(n)) if n else value
                field[n, pair, rows, spot(0)] = real
                field[n, pair, rows, spot(1)] = imag

    either_way(forward, (lower, upper))

    block = 32 if count <= ORB else 16
    size = block * count * 2 * SLOTS

    @pl.loop(0, ROWS // block)
    def _(b):
        take = pl.ds(b * block, block)
        high, low = high_ref[...], low_ref[...]
        space = product(field[take].reshape(size, 2 * LANES), high, low)
        space = space.reshape(block * count, 2, SLOTS, 2 * LANES)
        less = space[:, 0, :, :LANES], space[:, 0, :, LANES:]
        great = space[:, 1, :, :LANES], space[:, 1, :, LANES:]

        def bubble(first, other):
            real = first[0] * first[0] - first[1] * first[1]
            imag = 2.0 * first[0] * first[1]
            return -(real * other[0] + imag * other[1]), imag * other[0] - real * other[1]

        sigma = jnp.stack(
            [jnp.concatenate(bubble(less, great), -1), jnp.concatenate(bubble(great, less), -1)], 1
        )
        back = product(sigma.reshape(size, 2 * LANES), high, low)
        field[take] = back.reshape(block, count, 2 * SLOTS, 2 * LANES)

    @pl.loop(0, 2 * count)
    def _(s):
        comp, pair = s // count, s % count
        rows = pl.ds(pl.multiple_of(comp * SLOTS, SLOTS), SLOTS)
        values = [(field[n, pair, rows, spot(0)], field[n, pair, rows, spot(1)]) for n in range(ROWS)]
        values = [times(value, twist(n)) if n else value for n, value in enumerate(values)]
        for m, (real, imag) in enumerate(fourier(values)):
            field[m, pair, rows, spot(0)] = real
            field[m, pair, rows, spot(1)] = imag

    scale = weight[...]

    def contract(plane, half, halves, older_halves):
        m = plane // 4 * 8 + half * 4 + plane % 4

        def sigma(comp, a):
            rows = pl.ds(comp * SLOTS, SLOTS)
            if joined and a == 0:
                return older_sigma[m, rows, spot(0)], older_sigma[m, rows, spot(1)]
            return field[m, a - joined, rows, spot(0)], field[m, a - joined, rows, spot(1)]

        def given(comp, b):
            if joined and b == 0:
                return pair_of(older_halves[half], plane, ORB + 1, comp, ORB)
            return pair_of(halves[half], plane, count, comp, b - joined)

        def memory(a, b):
            left, right = sigma(0, a), given(1, b)
            other, cross = sigma(1, a), given(0, b)
            real = left[0] * right[0] - left[1] * right[1] - other[0] * cross[0] + other[1] * cross[1]
            if a == b:
                return real, None
            imag = left[0] * right[1] + left[1] * right[0] - other[0] * cross[1] - other[1] * cross[0]
            return real, imag

        results = [2.0 * memory(a, a)[0] for a in range(ORB)]
        for a, b in ((0, 1), (0, 2), (1, 2)):
            one, two = memory(a, b), memory(b, a)
            results += [one[0] + two[0], two[1] - one[1]]
        for i, result in enumerate(results):
            spot_out, row = plane * 2 + half, pl.ds(i, 1)
            out[spot_out, row, :] = before[spot_out, row, :] + jnp.sum(result * scale, axis=0, keepdims=True)
        if spilled:
            refs[6][m] = field[m, ORB]

    def contract_all(halves, older_halves):
        @pl.loop(0, PLANE, unroll=2)
        def _(plane):
            for half in range(2):
                contract(plane, half, halves, older_halves)

    olders = (older.at[:, 0], older.at[:, 1]) if joined else (None, None)
    either_way(contract_all, (lower, upper), olders)


def collide(turn, fields, weights, high, low, twiddle, before, older=(), spilled=False):
    stacked, joined = len(fields) == 1, int(len(older) > 0)
    count = ORB + 1 if stacked else ORB - joined
    shapes = [jax.ShapeDtypeStruct((ROWS, PAIRS, LANES), jnp.float32)]
    if spilled:
        shapes.append(jax.ShapeDtypeStruct((ROWS, 2 * SLOTS, 2 * LANES), jnp.float32))
    inputs = (*fields, *older, weights, high, low, twiddle, before)
    return pl.pallas_call(
        functools.partial(kernel, count, stacked, joined, spilled),
        out_shape=shapes,
        in_specs=[pl.BlockSpec(memory_space=pltpu.SMEM)]
        + [pl.BlockSpec(memory_space=pltpu.VMEM)] * len(inputs),
        out_specs=[pl.BlockSpec(memory_space=pltpu.VMEM)] * len(shapes),
        scratch_shapes=[pltpu.VMEM((ROWS, count, 2 * SLOTS, 2 * LANES), jnp.float32)],
        compiler_params=pltpu.CompilerParams(vmem_limit_bytes=24 * 1024 * 1024),
        cost_estimate=pl.CostEstimate(flops=1000000000, bytes_accessed=0, transcendentals=0),
    )(turn, *inputs)


def arrange_kernel(blocks, ways, first, parts, out, sems):
    copies, base = [], 0
    for pairs in blocks:
        for kind in range(4):
            for i, (a, c) in enumerate(pairs):
                at = base + kind * len(pairs) + i
                for n, way in enumerate(ways):
                    half = first[0] if way == 0 else 1 - first[0]
                    target = out.at[:, n, at] if len(ways) > 1 else out.at[:, at]
                    source = parts.at[kind * ORB + a, c, half]
                    copies.append(pltpu.make_async_copy(source, target, sems.at[n, at]))
        base += 4 * len(pairs)
    for copy in copies:
        copy.start()
    for copy in copies:
        copy.wait()


def arrange(first, parts, blocks, ways):
    count = 4 * sum(len(pairs) for pairs in blocks)
    shape = (PLANE, *((len(ways),) if len(ways) > 1 else ()), count, SLOTS, LANES)
    return pl.pallas_call(
        functools.partial(arrange_kernel, blocks, ways),
        out_shape=jax.ShapeDtypeStruct(shape, jnp.float32),
        in_specs=[pl.BlockSpec(memory_space=pltpu.SMEM), pl.BlockSpec(memory_space=pl.ANY)],
        out_specs=pl.BlockSpec(memory_space=pltpu.VMEM),
        scratch_shapes=[pltpu.SemaphoreType.DMA((len(ways), count))],
        compiler_params=pltpu.CompilerParams(vmem_limit_bytes=60 * 1024 * 1024),
        cost_estimate=pl.CostEstimate(flops=0, bytes_accessed=3_200_000, transcendentals=0),
    )(first, parts)


def join_kernel(kept, ahead, landed, out, sems):
    first = ahead.shape[1]
    copies = [
        pltpu.make_async_copy(kept, out.at[:, 0], sems.at[0]),
        pltpu.make_async_copy(ahead, out.at[:, 1, pl.ds(0, first)], sems.at[1]),
        pltpu.make_async_copy(landed, out.at[:, 1, pl.ds(first, landed.shape[1])], sems.at[2]),
    ]
    for copy in copies:
        copy.start()
    for copy in copies:
        copy.wait()


def join(kept, ahead, landed):
    return pl.pallas_call(
        join_kernel,
        out_shape=jax.ShapeDtypeStruct((PLANE, 2, *kept.shape[1:]), jnp.float32),
        in_specs=[pl.BlockSpec(memory_space=pl.ANY)] * 3,
        out_specs=pl.BlockSpec(memory_space=pltpu.VMEM),
        scratch_shapes=[pltpu.SemaphoreType.DMA((3,))],
        compiler_params=pltpu.CompilerParams(vmem_limit_bytes=8 * 1024 * 1024),
        cost_estimate=pl.CostEstimate(flops=0, bytes_accessed=3_200_000, transcendentals=0),
    )(kept, ahead, landed)


def cut_kernel(base, whole, *refs):
    *outs, sems = refs
    copies = []
    for n, out in enumerate(outs):
        source = whole.at[:, n, pl.ds(base, out.shape[1])]
        copies.append(pltpu.make_async_copy(source, out, sems.at[n]))
    for copy in copies:
        copy.start()
    for copy in copies:
        copy.wait()


def cut(whole, base, size):
    return pl.pallas_call(
        functools.partial(cut_kernel, base),
        out_shape=[jax.ShapeDtypeStruct((PLANE, size, SLOTS, LANES), jnp.float32)] * 2,
        in_specs=[pl.BlockSpec(memory_space=pl.ANY)],
        out_specs=[pl.BlockSpec(memory_space=pltpu.VMEM)] * 2,
        scratch_shapes=[pltpu.SemaphoreType.DMA((2,))],
        compiler_params=pltpu.CompilerParams(vmem_limit_bytes=8 * 1024 * 1024),
        cost_estimate=pl.CostEstimate(flops=0, bytes_accessed=3_200_000, transcendentals=0),
    )(whole)


def settle(weights, fields, cost):
    def body(given, *refs):
        refs[-1][...] = given[...]

    return pl.pallas_call(
        body,
        out_shape=jax.ShapeDtypeStruct((SLOTS, LANES), jnp.float32),
        in_specs=[pl.BlockSpec(memory_space=pltpu.VMEM)] + [pl.BlockSpec(memory_space=pl.ANY)] * len(fields),
        out_specs=pl.BlockSpec(memory_space=pltpu.VMEM),
        compiler_params=pltpu.CompilerParams(vmem_limit_bytes=1024 * 1024),
        cost_estimate=pl.CostEstimate(flops=int(cost * 1e9), bytes_accessed=0, transcendentals=0),
    )(weights, *fields)


def per_device(green_row, time_step):
    slot_count = green_row.shape[4]
    history = slot_count * 8
    zh, zl, core = (lax.axis_index(axis) for axis in ("zh", "zl", "core"))
    plane = lax.axis_index("y") * 4 + lax.axis_index("x")
    first = (zl * 2 + core) * slot_count + zh * (slot_count // 2) + plane * SLOTS
    slot_ids = first + jnp.arange(SLOTS, dtype=jnp.int32)
    slot_age = (time_step[0] - 1 - slot_ids) % history + 1
    decays = jnp.exp2(-(slot_age - 1).astype(jnp.float32) / history)
    weights = delta_time * decays * jnp.where(slot_age == history, 0.5, 1.0).astype(jnp.float32)
    weights = jnp.broadcast_to(weights[:, None], (SLOTS, LANES))
    high, low, twiddle = lane_tables()

    parts = green_row.reshape(4 * ORB, ORB, 2, PLANE, SLOTS, LANES)

    def spread(value):
        return lax.all_to_all(value, ("y", "x"), split_axis=0, concat_axis=0)

    def move(value):
        return lax.ppermute(value, "zh", [(0, 1), (1, 0)])

    def work(fields, partial, weights, **more):
        return collide(turn_flag, fields, weights, high, low, twiddle, partial, **more)

    turn_flag = zh.reshape(1).astype(jnp.int32)
    partial = jnp.zeros((ROWS, PAIRS, LANES), jnp.float32)
    fence = lax.optimization_barrier
    early = [[(0, 0), (1, 0)], [(2, 0), (0, 1)]]
    late = [[(1, 1), (2, 1)], [(0, 2), (1, 2), (2, 2)]]

    side = zh.reshape(1).astype(jnp.int32)
    ahead = arrange(side, parts, early[:1], (1,))
    ahead, side = fence((ahead, side))
    sent = arrange(side, parts, early[1:], (1,))
    sent, side = fence((sent, side))
    ahead, landed = move(ahead), move(sent)
    rest = arrange(side, parts, late, (0, 1))
    rest = spread(rest)
    kept = arrange(side, parts, early, (0,))
    kept, weights = fence((kept, weights))
    ahead, rest, weights = fence((ahead, rest, settle(weights, [ahead], 50.0)))
    one = cut(rest, 0, 4 * len(late[0]))
    two = cut(rest, 4 * len(late[0]), 4 * len(late[1]))
    one, two = (one[0], move(one[1])), (two[0], move(two[1]))
    zero = spread(join(kept, ahead, landed))
    one, zero, weights = fence((one, zero, settle(weights, one[1:], 50.0)))
    partial, sigma = work([zero], partial, weights, spilled=True)
    (partial,) = work(one, partial, weights, older=(zero, sigma))
    partial, two = fence((partial, two))
    (partial,) = work(two, partial, weights)
    blocks = partial.reshape(PLANE, 2, PAIRS, LANES)
    owned = jnp.sum(spread(blocks), axis=0)
    share = LANES // 8
    shares = owned.reshape(2, PAIRS, 8, share).transpose(0, 2, 1, 3).reshape(PLANE, 1, PAIRS * share)
    shares = lax.all_to_all(shares, ("zh", "zl", "core"), split_axis=0, concat_axis=0)
    summed = jnp.sum(shares, axis=(0, 1)).reshape(PAIRS, share)
    none = jnp.zeros_like(summed[0])
    real = [summed[0], summed[3], summed[5], summed[3], summed[1], summed[7], summed[5], summed[7], summed[2]]
    imag = [none, summed[4], summed[6], -summed[4], none, summed[8], -summed[6], -summed[8], none]
    return jnp.stack(real + imag).reshape(2, ORB, ORB, -1)


def solution(mesh):
    axes = ("y", "zh", "x", "zl", "core")
    finer = Mesh(mesh.devices.reshape(4, 2, 4, 4, 2), axes)
    mom, hist = axes[:3], axes[3:]
    return jax.shard_map(
        per_device,
        mesh=finer,
        in_specs=(P(None, None, None, None, hist, mom), P()),
        out_specs=P(None, None, None, axes),
        check_vma=False,
    )
```

```python
import functools
import math

import jax
import jax.numpy as jnp
import numpy as np
from jax import lax
from jax.experimental import pallas as pl
from jax.experimental.pallas import tpu as pltpu
from jax.sharding import Mesh
from jax.sharding import PartitionSpec as P

NKX = 64
NKY = 64
ORB = 3
PAIRS = ORB * ORB
ROWS = 32
PLANE = 16
SLOTS = 8
LANES = 128

delta_time = 0.01


def lane_tables():
    index = np.arange(64)
    angle = 2.0 * math.pi * (index[:, None] * index[None, :] % 64) / 64
    sign = np.array([[1.0, 1.0], [1.0, -1.0]])
    cosine = np.kron(sign, np.cos(angle)) / 64
    sine = np.kron(sign, np.sin(angle)) / 64
    table = np.block([[cosine, sine], [-sine, cosine]]).astype(np.float32)
    high = table.astype(jnp.bfloat16)
    low = (table - high.astype(np.float32)).astype(jnp.bfloat16)
    turn = 2.0 * math.pi * np.arange(ROWS)[:, None] * np.repeat([0, 1], 64)[None, :] / 64
    twiddle = np.stack([np.cos(turn), np.sin(turn)], 1).astype(np.float32)
    return high, low, twiddle


def turned(value, step, length):
    real, imag = value
    eighths = step * 8 / length
    if eighths == 0:
        return real, imag
    if eighths == 2:
        return -imag, real
    if eighths == 4:
        return -real, -imag
    if eighths == 6:
        return imag, -real
    root = math.sqrt(0.5)
    if eighths == 1:
        return root * (real - imag), root * (real + imag)
    if eighths == 3:
        return -root * (real + imag), root * (real - imag)
    if eighths == 5:
        return root * (imag - real), -root * (real + imag)
    if eighths == 7:
        return root * (real + imag), root * (imag - real)
    cosine, sine = math.cos(2 * math.pi * step / length), math.sin(2 * math.pi * step / length)
    return real * cosine - imag * sine, real * sine + imag * cosine


def plus(first, second):
    return first[0] + second[0], first[1] + second[1]


def minus(first, second):
    return first[0] - second[0], first[1] - second[1]


def fourier(values):
    length = len(values)
    if length == 1:
        return values
    if length == 2:
        return [plus(*values), minus(*values)]
    quarter = length // 4
    parts = [fourier(values[start::4]) for start in range(4)]
    out = [None] * length
    for m in range(quarter):
        first, second, third, fourth = (turned(parts[p][m], p * m, length) for p in range(4))
        even, odd = plus(first, third), minus(first, third)
        other, cross = plus(second, fourth), minus(second, fourth)
        cross = (-cross[1], cross[0])
        out[m], out[m + 2 * quarter] = plus(even, other), minus(even, other)
        out[m + quarter], out[m + 3 * quarter] = plus(odd, cross), minus(odd, cross)
    return out


def product(values, high, low):
    head = values.astype(jnp.bfloat16)
    tail = (values - head.astype(jnp.float32)).astype(jnp.bfloat16)

    left, right = jnp.concatenate([head, tail, head], 1), jnp.concatenate([high, high, low], 0)
    return jnp.dot(left, right, preferred_element_type=jnp.float32)


def kernel(count, stacked, joined, spilled, turn, *refs):
    refs = list(refs)
    if stacked:
        whole = refs.pop(0)
        lower, upper = whole.at[:, 0], whole.at[:, 1]
    else:
        lower, upper = refs.pop(0), refs.pop(0)
    if joined:
        older, older_sigma = refs.pop(0), refs.pop(0)
    weight, high_ref, low_ref, twiddle, before, out = refs[:6]
    field = refs[-1]

    def pair_of(source, plane, pairs, comp, pair):
        size = 2 if pairs == ORB + 1 else pairs
        at = pair // size * 4 * size + 2 * comp * size + pair % size
        return source[plane, at], source[plane, at + size]

    def either_way(act, *sides):
        pl.when(turn[0] == 0)(lambda: act(*sides))
        pl.when(turn[0] == 1)(lambda: act(*(side[::-1] for side in sides)))

    def spot(part):
        return pl.ds(part * LANES, LANES)

    def twist(n):
        return twiddle[n, 0][None, :], twiddle[n, 1][None, :]

    def times(value, factor):
        return value[0] * factor[0] - value[1] * factor[1], value[0] * factor[1] + value[1] * factor[0]

    def forward(halves):
        @pl.loop(0, 2 * count)
        def _(s):
            comp, pair = s // count, s % count
            rows = pl.ds(pl.multiple_of(comp * SLOTS, SLOTS), SLOTS)
            values = [
                pair_of(halves[m // 4 % 2], m // 8 * 4 + m % 4, count, comp, pair) for m in range(ROWS)
            ]
            for n, value in enumerate(fourier(values)):
                real, imag = times(value, twist(n)) if n else value
                field[n, pair, rows, spot(0)] = real
                field[n, pair, rows, spot(1)] = imag

    either_way(forward, (lower, upper))

    block = 32 if count <= ORB else 16
    size = block * count * 2 * SLOTS

    @pl.loop(0, ROWS // block)
    def _(b):
        take = pl.ds(b * block, block)
        high, low = high_ref[...], low_ref[...]
        space = product(field[take].reshape(size, 2 * LANES), high, low)
        space = space.reshape(block * count, 2, SLOTS, 2 * LANES)
        less = space[:, 0, :, :LANES], space[:, 0, :, LANES:]
        great = space[:, 1, :, :LANES], space[:, 1, :, LANES:]

        def bubble(first, other):
            real = first[0] * first[0] - first[1] * first[1]
            imag = 2.0 * first[0] * first[1]
            return -(real * other[0] + imag * other[1]), imag * other[0] - real * other[1]

        sigma = jnp.stack(
            [jnp.concatenate(bubble(less, great), -1), jnp.concatenate(bubble(great, less), -1)], 1
        )
        back = product(sigma.reshape(size, 2 * LANES), high, low)
        field[take] = back.reshape(block, count, 2 * SLOTS, 2 * LANES)

    @pl.loop(0, 2 * count)
    def _(s):
        comp, pair = s // count, s % count
        rows = pl.ds(pl.multiple_of(comp * SLOTS, SLOTS), SLOTS)
        values = [(field[n, pair, rows, spot(0)], field[n, pair, rows, spot(1)]) for n in range(ROWS)]
        values = [times(value, twist(n)) if n else value for n, value in enumerate(values)]
        for m, (real, imag) in enumerate(fourier(values)):
            field[m, pair, rows, spot(0)] = real
            field[m, pair, rows, spot(1)] = imag

    scale = weight[...]

    def contract(plane, half, halves, older_halves):
        m = plane // 4 * 8 + half * 4 + plane % 4

        def sigma(comp, a):
            rows = pl.ds(comp * SLOTS, SLOTS)
            if joined and a == 0:
                return older_sigma[m, rows, spot(0)], older_sigma[m, rows, spot(1)]
            return field[m, a - joined, rows, spot(0)], field[m, a - joined, rows, spot(1)]

        def given(comp, b):
            if joined and b == 0:
                return pair_of(older_halves[half], plane, ORB + 1, comp, ORB)
            return pair_of(halves[half], plane, count, comp, b - joined)

        def memory(a, b):
            left, right = sigma(0, a), given(1, b)
            other, cross = sigma(1, a), given(0, b)
            real = left[0] * right[0] - left[1] * right[1] - other[0] * cross[0] + other[1] * cross[1]
            if a == b:
                return real, None
            imag = left[0] * right[1] + left[1] * right[0] - other[0] * cross[1] - other[1] * cross[0]
            return real, imag

        results = [2.0 * memory(a, a)[0] for a in range(ORB)]
        for a, b in ((0, 1), (0, 2), (1, 2)):
            one, two = memory(a, b), memory(b, a)
            results += [one[0] + two[0], two[1] - one[1]]
        for i, result in enumerate(results):
            spot_out, row = plane * 2 + half, pl.ds(i, 1)
            out[spot_out, row, :] = before[spot_out, row, :] + jnp.sum(result * scale, axis=0, keepdims=True)
        if spilled:
            refs[6][m] = field[m, ORB]

    def contract_all(halves, older_halves):
        @pl.loop(0, PLANE, unroll=2)
        def _(plane):
            for half in range(2):
                contract(plane, half, halves, older_halves)

    olders = (older.at[:, 0], older.at[:, 1]) if joined else (None, None)
    either_way(contract_all, (lower, upper), olders)


def collide(turn, fields, weights, high, low, twiddle, before, older=(), spilled=False):
    stacked, joined = len(fields) == 1, int(len(older) > 0)
    count = ORB + 1 if stacked else ORB - joined
    shapes = [jax.ShapeDtypeStruct((ROWS, PAIRS, LANES), jnp.float32)]
    if spilled:
        shapes.append(jax.ShapeDtypeStruct((ROWS, 2 * SLOTS, 2 * LANES), jnp.float32))
    inputs = (*fields, *older, weights, high, low, twiddle, before)
    return pl.pallas_call(
        functools.partial(kernel, count, stacked, joined, spilled),
        out_shape=shapes,
        in_specs=[pl.BlockSpec(memory_space=pltpu.SMEM)]
        + [pl.BlockSpec(memory_space=pltpu.VMEM)] * len(inputs),
        out_specs=[pl.BlockSpec(memory_space=pltpu.VMEM)] * len(shapes),
        scratch_shapes=[pltpu.VMEM((ROWS, count, 2 * SLOTS, 2 * LANES), jnp.float32)],
        compiler_params=pltpu.CompilerParams(vmem_limit_bytes=24 * 1024 * 1024),
        cost_estimate=pl.CostEstimate(flops=1000000000, bytes_accessed=0, transcendentals=0),
    )(turn, *inputs)


def arrange_kernel(blocks, ways, first, parts, out, sems):
    copies, base = [], 0
    for pairs in blocks:
        for kind in range(4):
            for i, (a, c) in enumerate(pairs):
                at = base + kind * len(pairs) + i
                for n, way in enumerate(ways):
                    half = first[0] if way == 0 else 1 - first[0]
                    target = out.at[:, n, at] if len(ways) > 1 else out.at[:, at]
                    source = parts.at[kind * ORB + a, c, half]
                    copies.append(pltpu.make_async_copy(source, target, sems.at[n, at]))
        base += 4 * len(pairs)
    for copy in copies:
        copy.start()
    for copy in copies:
        copy.wait()


def arrange(first, parts, blocks, ways):
    count = 4 * sum(len(pairs) for pairs in blocks)
    shape = (PLANE, *((len(ways),) if len(ways) > 1 else ()), count, SLOTS, LANES)
    return pl.pallas_call(
        functools.partial(arrange_kernel, blocks, ways),
        out_shape=jax.ShapeDtypeStruct(shape, jnp.float32),
        in_specs=[pl.BlockSpec(memory_space=pltpu.SMEM), pl.BlockSpec(memory_space=pl.ANY)],
        out_specs=pl.BlockSpec(memory_space=pltpu.VMEM),
        scratch_shapes=[pltpu.SemaphoreType.DMA((len(ways), count))],
        compiler_params=pltpu.CompilerParams(vmem_limit_bytes=60 * 1024 * 1024),
        cost_estimate=pl.CostEstimate(flops=0, bytes_accessed=3_200_000, transcendentals=0),
    )(first, parts)


def join_kernel(kept, ahead, landed, out, sems):
    first = ahead.shape[1]
    copies = [
        pltpu.make_async_copy(kept, out.at[:, 0], sems.at[0]),
        pltpu.make_async_copy(ahead, out.at[:, 1, pl.ds(0, first)], sems.at[1]),
        pltpu.make_async_copy(landed, out.at[:, 1, pl.ds(first, landed.shape[1])], sems.at[2]),
    ]
    for copy in copies:
        copy.start()
    for copy in copies:
        copy.wait()


def join(kept, ahead, landed):
    return pl.pallas_call(
        join_kernel,
        out_shape=jax.ShapeDtypeStruct((PLANE, 2, *kept.shape[1:]), jnp.float32),
        in_specs=[pl.BlockSpec(memory_space=pl.ANY)] * 3,
        out_specs=pl.BlockSpec(memory_space=pltpu.VMEM),
        scratch_shapes=[pltpu.SemaphoreType.DMA((3,))],
        compiler_params=pltpu.CompilerParams(vmem_limit_bytes=8 * 1024 * 1024),
        cost_estimate=pl.CostEstimate(flops=0, bytes_accessed=3_200_000, transcendentals=0),
    )(kept, ahead, landed)


def cut_kernel(base, whole, *refs):
    *outs, sems = refs
    copies = []
    for n, out in enumerate(outs):
        source = whole.at[:, n, pl.ds(base, out.shape[1])]
        copies.append(pltpu.make_async_copy(source, out, sems.at[n]))
    for copy in copies:
        copy.start()
    for copy in copies:
        copy.wait()


def cut(whole, base, size):
    return pl.pallas_call(
        functools.partial(cut_kernel, base),
        out_shape=[jax.ShapeDtypeStruct((PLANE, size, SLOTS, LANES), jnp.float32)] * 2,
        in_specs=[pl.BlockSpec(memory_space=pl.ANY)],
        out_specs=[pl.BlockSpec(memory_space=pltpu.VMEM)] * 2,
        scratch_shapes=[pltpu.SemaphoreType.DMA((2,))],
        compiler_params=pltpu.CompilerParams(vmem_limit_bytes=8 * 1024 * 1024),
        cost_estimate=pl.CostEstimate(flops=0, bytes_accessed=3_200_000, transcendentals=0),
    )(whole)


def settle(weights, fields, cost):
    def body(given, *refs):
        refs[-1][...] = given[...]

    return pl.pallas_call(
        body,
        out_shape=jax.ShapeDtypeStruct((SLOTS, LANES), jnp.float32),
        in_specs=[pl.BlockSpec(memory_space=pltpu.VMEM)] + [pl.BlockSpec(memory_space=pl.ANY)] * len(fields),
        out_specs=pl.BlockSpec(memory_space=pltpu.VMEM),
        compiler_params=pltpu.CompilerParams(vmem_limit_bytes=1024 * 1024),
        cost_estimate=pl.CostEstimate(flops=int(cost * 1e9), bytes_accessed=0, transcendentals=0),
    )(weights, *fields)


def per_device(green_row, time_step):
    slot_count = green_row.shape[4]
    history = slot_count * 8
    zh, zl, core = (lax.axis_index(axis) for axis in ("zh", "zl", "core"))
    plane = lax.axis_index("y") * 4 + lax.axis_index("x")
    first = (zl * 2 + core) * slot_count + zh * (slot_count // 2) + plane * SLOTS
    slot_ids = first + jnp.arange(SLOTS, dtype=jnp.int32)
    slot_age = (time_step[0] - 1 - slot_ids) % history + 1
    decays = jnp.exp2(-(slot_age - 1).astype(jnp.float32) / history)
    weights = delta_time * decays * jnp.where(slot_age == history, 0.5, 1.0).astype(jnp.float32)
    weights = jnp.broadcast_to(weights[:, None], (SLOTS, LANES))
    high, low, twiddle = lane_tables()

    parts = green_row.reshape(4 * ORB, ORB, 2, PLANE, SLOTS, LANES)

    def spread(value):
        return lax.all_to_all(value, ("y", "x"), split_axis=0, concat_axis=0)

    def move(value):
        return lax.ppermute(value, "zh", [(0, 1), (1, 0)])

    def work(fields, partial, weights, **more):
        return collide(turn_flag, fields, weights, high, low, twiddle, partial, **more)

    turn_flag = zh.reshape(1).astype(jnp.int32)
    partial = jnp.zeros((ROWS, PAIRS, LANES), jnp.float32)
    fence = lax.optimization_barrier
    early = [[(0, 0), (1, 0)], [(2, 0), (0, 1)]]
    late = [[(1, 1), (2, 1)], [(0, 2), (1, 2), (2, 2)]]

    side = zh.reshape(1).astype(jnp.int32)
    ahead = arrange(side, parts, early[:1], (1,))
    ahead, side = fence((ahead, side))
    ahead = move(ahead)
    rest = arrange(side, parts, late, (0, 1))
    rest, side = fence((rest, side))
    sent = arrange(side, parts, early[1:], (1,))
    rest, sent = spread(rest), fence(sent)
    landed = move(sent)
    kept = arrange(side, parts, early, (0,))
    kept, weights = fence((kept, weights))
    ahead, rest, weights = fence((ahead, rest, settle(weights, [ahead], 50.0)))
    one = cut(rest, 0, 4 * len(late[0]))
    two = cut(rest, 4 * len(late[0]), 4 * len(late[1]))
    one, two = (one[0], move(one[1])), (two[0], move(two[1]))
    zero = spread(join(kept, ahead, landed))
    one, zero, weights = fence((one, zero, settle(weights, one[1:], 50.0)))
    partial, sigma = work([zero], partial, weights, spilled=True)
    (partial,) = work(one, partial, weights, older=(zero, sigma))
    partial, two = fence((partial, two))
    (partial,) = work(two, partial, weights)
    blocks = partial.reshape(PLANE, 2, PAIRS, LANES)
    owned = jnp.sum(spread(blocks), axis=0)
    share = LANES // 8
    shares = owned.reshape(2, PAIRS, 8, share).transpose(0, 2, 1, 3).reshape(PLANE, 1, PAIRS * share)
    shares = lax.all_to_all(shares, ("zh", "zl", "core"), split_axis=0, concat_axis=0)
    summed = jnp.sum(shares, axis=(0, 1)).reshape(PAIRS, share)
    none = jnp.zeros_like(summed[0])
    real = [summed[0], summed[3], summed[5], summed[3], summed[1], summed[7], summed[5], summed[7], summed[2]]
    imag = [none, summed[4], summed[6], -summed[4], none, summed[8], -summed[6], -summed[8], none]
    return jnp.stack(real + imag).reshape(2, ORB, ORB, -1)


def solution(mesh):
    axes = ("y", "zh", "x", "zl", "core")
    finer = Mesh(mesh.devices.reshape(4, 2, 4, 4, 2), axes)
    mom, hist = axes[:3], axes[3:]
    return jax.shard_map(
        per_device,
        mesh=finer,
        in_specs=(P(None, None, None, None, hist, mom), P()),
        out_specs=P(None, None, None, axes),
        check_vma=False,
    )
```

```python
import functools
import math

import jax
import jax.numpy as jnp
import numpy as np
from jax import lax
from jax.experimental import pallas as pl
from jax.experimental.pallas import tpu as pltpu
from jax.sharding import Mesh
from jax.sharding import PartitionSpec as P

NKX = 64
NKY = 64
ORB = 3
PAIRS = ORB * ORB
ROWS = 32
PLANE = 16
SLOTS = 8
LANES = 128

delta_time = 0.01


def lane_tables():
    index = np.arange(64)
    angle = 2.0 * math.pi * (index[:, None] * index[None, :] % 64) / 64
    sign = np.array([[1.0, 1.0], [1.0, -1.0]])
    cosine = np.kron(sign, np.cos(angle)) / 64
    sine = np.kron(sign, np.sin(angle)) / 64
    table = np.block([[cosine, sine], [-sine, cosine]]).astype(np.float32)
    high = table.astype(jnp.bfloat16)
    low = (table - high.astype(np.float32)).astype(jnp.bfloat16)
    turn = 2.0 * math.pi * np.arange(ROWS)[:, None] * np.repeat([0, 1], 64)[None, :] / 64
    twiddle = np.stack([np.cos(turn), np.sin(turn)], 1).astype(np.float32)
    return high, low, twiddle


def turned(value, step, length):
    real, imag = value
    eighths = step * 8 / length
    if eighths == 0:
        return real, imag
    if eighths == 2:
        return -imag, real
    if eighths == 4:
        return -real, -imag
    if eighths == 6:
        return imag, -real
    root = math.sqrt(0.5)
    if eighths == 1:
        return root * (real - imag), root * (real + imag)
    if eighths == 3:
        return -root * (real + imag), root * (real - imag)
    if eighths == 5:
        return root * (imag - real), -root * (real + imag)
    if eighths == 7:
        return root * (real + imag), root * (imag - real)
    cosine, sine = math.cos(2 * math.pi * step / length), math.sin(2 * math.pi * step / length)
    return real * cosine - imag * sine, real * sine + imag * cosine


def plus(first, second):
    return first[0] + second[0], first[1] + second[1]


def minus(first, second):
    return first[0] - second[0], first[1] - second[1]


def fourier(values):
    length = len(values)
    if length == 1:
        return values
    if length == 2:
        return [plus(*values), minus(*values)]
    quarter = length // 4
    parts = [fourier(values[start::4]) for start in range(4)]
    out = [None] * length
    for m in range(quarter):
        first, second, third, fourth = (turned(parts[p][m], p * m, length) for p in range(4))
        even, odd = plus(first, third), minus(first, third)
        other, cross = plus(second, fourth), minus(second, fourth)
        cross = (-cross[1], cross[0])
        out[m], out[m + 2 * quarter] = plus(even, other), minus(even, other)
        out[m + quarter], out[m + 3 * quarter] = plus(odd, cross), minus(odd, cross)
    return out


def product(values, high, low):
    head = values.astype(jnp.bfloat16)
    tail = (values - head.astype(jnp.float32)).astype(jnp.bfloat16)

    left, right = jnp.concatenate([head, tail, head], 1), jnp.concatenate([high, high, low], 0)
    return jnp.dot(left, right, preferred_element_type=jnp.float32)


def kernel(count, stacked, joined, spilled, turn, *refs):
    refs = list(refs)
    if stacked:
        whole = refs.pop(0)
        lower, upper = whole.at[:, 0], whole.at[:, 1]
    else:
        lower, upper = refs.pop(0), refs.pop(0)
    if joined:
        older, older_sigma = refs.pop(0), refs.pop(0)
    weight, high_ref, low_ref, twiddle, before, out = refs[:6]
    field = refs[-1]

    def pair_of(source, plane, pairs, comp, pair):
        size = 2 if pairs == ORB + 1 else pairs
        at = pair // size * 4 * size + 2 * comp * size + pair % size
        return source[plane, at], source[plane, at + size]

    def either_way(act, *sides):
        pl.when(turn[0] == 0)(lambda: act(*sides))
        pl.when(turn[0] == 1)(lambda: act(*(side[::-1] for side in sides)))

    def spot(part):
        return pl.ds(part * LANES, LANES)

    def twist(n):
        return twiddle[n, 0][None, :], twiddle[n, 1][None, :]

    def times(value, factor):
        return value[0] * factor[0] - value[1] * factor[1], value[0] * factor[1] + value[1] * factor[0]

    def forward(halves):
        @pl.loop(0, 2 * count)
        def _(s):
            comp, pair = s // count, s % count
            rows = pl.ds(pl.multiple_of(comp * SLOTS, SLOTS), SLOTS)
            values = [
                pair_of(halves[m // 4 % 2], m // 8 * 4 + m % 4, count, comp, pair) for m in range(ROWS)
            ]
            for n, value in enumerate(fourier(values)):
                real, imag = times(value, twist(n)) if n else value
                field[n, pair, rows, spot(0)] = real
                field[n, pair, rows, spot(1)] = imag

    either_way(forward, (lower, upper))

    block = 32 if count <= ORB else 16
    size = block * count * 2 * SLOTS

    @pl.loop(0, ROWS // block)
    def _(b):
        take = pl.ds(b * block, block)
        high, low = high_ref[...], low_ref[...]
        space = product(field[take].reshape(size, 2 * LANES), high, low)
        space = space.reshape(block * count, 2, SLOTS, 2 * LANES)
        less = space[:, 0, :, :LANES], space[:, 0, :, LANES:]
        great = space[:, 1, :, :LANES], space[:, 1, :, LANES:]

        def bubble(first, other):
            real = first[0] * first[0] - first[1] * first[1]
            imag = 2.0 * first[0] * first[1]
            return -(real * other[0] + imag * other[1]), imag * other[0] - real * other[1]

        sigma = jnp.stack(
            [jnp.concatenate(bubble(less, great), -1), jnp.concatenate(bubble(great, less), -1)], 1
        )
        back = product(sigma.reshape(size, 2 * LANES), high, low)
        field[take] = back.reshape(block, count, 2 * SLOTS, 2 * LANES)

    @pl.loop(0, 2 * count)
    def _(s):
        comp, pair = s // count, s % count
        rows = pl.ds(pl.multiple_of(comp * SLOTS, SLOTS), SLOTS)
        values = [(field[n, pair, rows, spot(0)], field[n, pair, rows, spot(1)]) for n in range(ROWS)]
        values = [times(value, twist(n)) if n else value for n, value in enumerate(values)]
        for m, (real, imag) in enumerate(fourier(values)):
            field[m, pair, rows, spot(0)] = real
            field[m, pair, rows, spot(1)] = imag

    scale = weight[...]

    def contract(plane, half, halves, older_halves):
        m = plane // 4 * 8 + half * 4 + plane % 4

        def sigma(comp, a):
            rows = pl.ds(comp * SLOTS, SLOTS)
            if joined and a == 0:
                return older_sigma[m, rows, spot(0)], older_sigma[m, rows, spot(1)]
            return field[m, a - joined, rows, spot(0)], field[m, a - joined, rows, spot(1)]

        def given(comp, b):
            if joined and b == 0:
                return pair_of(older_halves[half], plane, ORB + 1, comp, ORB)
            return pair_of(halves[half], plane, count, comp, b - joined)

        def memory(a, b):
            left, right = sigma(0, a), given(1, b)
            other, cross = sigma(1, a), given(0, b)
            real = left[0] * right[0] - left[1] * right[1] - other[0] * cross[0] + other[1] * cross[1]
            if a == b:
                return real, None
            imag = left[0] * right[1] + left[1] * right[0] - other[0] * cross[1] - other[1] * cross[0]
            return real, imag

        results = [2.0 * memory(a, a)[0] for a in range(ORB)]
        for a, b in ((0, 1), (0, 2), (1, 2)):
            one, two = memory(a, b), memory(b, a)
            results += [one[0] + two[0], two[1] - one[1]]
        for i, result in enumerate(results):
            spot_out, row = plane * 2 + half, pl.ds(i, 1)
            out[spot_out, row, :] = before[spot_out, row, :] + jnp.sum(result * scale, axis=0, keepdims=True)
        if spilled:
            refs[6][m] = field[m, ORB]

    def contract_all(halves, older_halves):
        @pl.loop(0, PLANE, unroll=2)
        def _(plane):
            for half in range(2):
                contract(plane, half, halves, older_halves)

    olders = (older.at[:, 0], older.at[:, 1]) if joined else (None, None)
    either_way(contract_all, (lower, upper), olders)


def collide(turn, fields, weights, high, low, twiddle, before, older=(), spilled=False):
    stacked, joined = len(fields) == 1, int(len(older) > 0)
    count = ORB + 1 if stacked else ORB - joined
    shapes = [jax.ShapeDtypeStruct((ROWS, PAIRS, LANES), jnp.float32)]
    if spilled:
        shapes.append(jax.ShapeDtypeStruct((ROWS, 2 * SLOTS, 2 * LANES), jnp.float32))
    inputs = (*fields, *older, weights, high, low, twiddle, before)
    return pl.pallas_call(
        functools.partial(kernel, count, stacked, joined, spilled),
        out_shape=shapes,
        in_specs=[pl.BlockSpec(memory_space=pltpu.SMEM)]
        + [pl.BlockSpec(memory_space=pltpu.VMEM)] * len(inputs),
        out_specs=[pl.BlockSpec(memory_space=pltpu.VMEM)] * len(shapes),
        scratch_shapes=[pltpu.VMEM((ROWS, count, 2 * SLOTS, 2 * LANES), jnp.float32)],
        compiler_params=pltpu.CompilerParams(vmem_limit_bytes=24 * 1024 * 1024),
        cost_estimate=pl.CostEstimate(flops=1000000000, bytes_accessed=0, transcendentals=0),
    )(turn, *inputs)


def arrange_kernel(blocks, ways, first, parts, out, sems):
    copies, base = [], 0
    for pairs in blocks:
        for kind in range(4):
            for i, (a, c) in enumerate(pairs):
                at = base + kind * len(pairs) + i
                for n, way in enumerate(ways):
                    half = first[0] if way == 0 else 1 - first[0]
                    target = out.at[:, n, at] if len(ways) > 1 else out.at[:, at]
                    source = parts.at[kind * ORB + a, c, half]
                    copies.append(pltpu.make_async_copy(source, target, sems.at[n, at]))
        base += 4 * len(pairs)
    for copy in copies:
        copy.start()
    for copy in copies:
        copy.wait()


def arrange(first, parts, blocks, ways):
    count = 4 * sum(len(pairs) for pairs in blocks)
    shape = (PLANE, *((len(ways),) if len(ways) > 1 else ()), count, SLOTS, LANES)
    return pl.pallas_call(
        functools.partial(arrange_kernel, blocks, ways),
        out_shape=jax.ShapeDtypeStruct(shape, jnp.float32),
        in_specs=[pl.BlockSpec(memory_space=pltpu.SMEM), pl.BlockSpec(memory_space=pl.ANY)],
        out_specs=pl.BlockSpec(memory_space=pltpu.VMEM),
        scratch_shapes=[pltpu.SemaphoreType.DMA((len(ways), count))],
        compiler_params=pltpu.CompilerParams(vmem_limit_bytes=60 * 1024 * 1024),
        cost_estimate=pl.CostEstimate(flops=0, bytes_accessed=3_200_000, transcendentals=0),
    )(first, parts)


def join_kernel(kept, ahead, landed, out, sems):
    first = ahead.shape[1]
    copies = [
        pltpu.make_async_copy(kept, out.at[:, 0], sems.at[0]),
        pltpu.make_async_copy(ahead, out.at[:, 1, pl.ds(0, first)], sems.at[1]),
        pltpu.make_async_copy(landed, out.at[:, 1, pl.ds(first, landed.shape[1])], sems.at[2]),
    ]
    for copy in copies:
        copy.start()
    for copy in copies:
        copy.wait()


def join(kept, ahead, landed):
    return pl.pallas_call(
        join_kernel,
        out_shape=jax.ShapeDtypeStruct((PLANE, 2, *kept.shape[1:]), jnp.float32),
        in_specs=[pl.BlockSpec(memory_space=pl.ANY)] * 3,
        out_specs=pl.BlockSpec(memory_space=pltpu.VMEM),
        scratch_shapes=[pltpu.SemaphoreType.DMA((3,))],
        compiler_params=pltpu.CompilerParams(vmem_limit_bytes=8 * 1024 * 1024),
        cost_estimate=pl.CostEstimate(flops=0, bytes_accessed=3_200_000, transcendentals=0),
    )(kept, ahead, landed)


def cut_kernel(base, way, whole, out, sem):
    copy = pltpu.make_async_copy(whole.at[:, way, pl.ds(base, out.shape[1])], out, sem)
    copy.start()
    copy.wait()


def cut(whole, base, size, way):
    return pl.pallas_call(
        functools.partial(cut_kernel, base, way),
        out_shape=jax.ShapeDtypeStruct((PLANE, size, SLOTS, LANES), jnp.float32),
        in_specs=[pl.BlockSpec(memory_space=pl.ANY)],
        out_specs=pl.BlockSpec(memory_space=pltpu.VMEM),
        scratch_shapes=[pltpu.SemaphoreType.DMA],
        compiler_params=pltpu.CompilerParams(vmem_limit_bytes=8 * 1024 * 1024),
        cost_estimate=pl.CostEstimate(flops=0, bytes_accessed=1_600_000, transcendentals=0),
    )(whole)


def settle(weights, fields, cost):
    def body(given, *refs):
        refs[-1][...] = given[...]

    return pl.pallas_call(
        body,
        out_shape=jax.ShapeDtypeStruct((SLOTS, LANES), jnp.float32),
        in_specs=[pl.BlockSpec(memory_space=pltpu.VMEM)] + [pl.BlockSpec(memory_space=pl.ANY)] * len(fields),
        out_specs=pl.BlockSpec(memory_space=pltpu.VMEM),
        compiler_params=pltpu.CompilerParams(vmem_limit_bytes=1024 * 1024),
        cost_estimate=pl.CostEstimate(flops=int(cost * 1e9), bytes_accessed=0, transcendentals=0),
    )(weights, *fields)


def per_device(green_row, time_step):
    slot_count = green_row.shape[4]
    history = slot_count * 8
    zh, zl, core = (lax.axis_index(axis) for axis in ("zh", "zl", "core"))
    plane = lax.axis_index("y") * 4 + lax.axis_index("x")
    first = (zl * 2 + core) * slot_count + zh * (slot_count // 2) + plane * SLOTS
    slot_ids = first + jnp.arange(SLOTS, dtype=jnp.int32)
    slot_age = (time_step[0] - 1 - slot_ids) % history + 1
    decays = jnp.exp2(-(slot_age - 1).astype(jnp.float32) / history)
    weights = delta_time * decays * jnp.where(slot_age == history, 0.5, 1.0).astype(jnp.float32)
    weights = jnp.broadcast_to(weights[:, None], (SLOTS, LANES))
    high, low, twiddle = lane_tables()

    parts = green_row.reshape(4 * ORB, ORB, 2, PLANE, SLOTS, LANES)

    def spread(value):
        return lax.all_to_all(value, ("y", "x"), split_axis=0, concat_axis=0)

    def move(value):
        return lax.ppermute(value, "zh", [(0, 1), (1, 0)])

    def work(fields, partial, weights, **more):
        return collide(turn_flag, fields, weights, high, low, twiddle, partial, **more)

    turn_flag = zh.reshape(1).astype(jnp.int32)
    partial = jnp.zeros((ROWS, PAIRS, LANES), jnp.float32)
    fence = lax.optimization_barrier
    early = [[(0, 0), (1, 0)], [(2, 0), (0, 1)]]
    late = [[(1, 1), (2, 1)], [(0, 2), (1, 2), (2, 2)]]

    side = zh.reshape(1).astype(jnp.int32)
    ahead = arrange(side, parts, early[:1], (1,))
    ahead, side = fence((ahead, side))
    ahead = move(ahead)
    rest = arrange(side, parts, late, (0, 1))
    rest, side = fence((rest, side))
    sent = arrange(side, parts, early[1:], (1,))
    rest, sent = spread(rest), fence(sent)
    landed = move(sent)
    kept = arrange(side, parts, early, (0,))
    kept, weights = fence((kept, weights))
    ahead, rest, weights = fence((ahead, rest, settle(weights, [ahead], 50.0)))
    place, sizes = (0, 4 * len(late[0])), [4 * len(pairs) for pairs in late]
    one, two = (move(cut(rest, base, size, 1)) for base, size in zip(place, sizes))
    one, two = ((cut(rest, base, size, 0), part) for base, size, part in zip(place, sizes, (one, two)))
    zero = spread(join(kept, ahead, landed))
    one, zero, weights = fence((one, zero, settle(weights, one[1:], 50.0)))
    partial, sigma = work([zero], partial, weights, spilled=True)
    (partial,) = work(one, partial, weights, older=(zero, sigma))
    partial, two = fence((partial, two))
    (partial,) = work(two, partial, weights)
    blocks = partial.reshape(PLANE, 2, PAIRS, LANES)
    owned = jnp.sum(spread(blocks), axis=0)
    share = LANES // 8
    shares = owned.reshape(2, PAIRS, 8, share).transpose(0, 2, 1, 3).reshape(PLANE, 1, PAIRS * share)
    shares = lax.all_to_all(shares, ("zh", "zl", "core"), split_axis=0, concat_axis=0)
    summed = jnp.sum(shares, axis=(0, 1)).reshape(PAIRS, share)
    none = jnp.zeros_like(summed[0])
    real = [summed[0], summed[3], summed[5], summed[3], summed[1], summed[7], summed[5], summed[7], summed[2]]
    imag = [none, summed[4], summed[6], -summed[4], none, summed[8], -summed[6], -summed[8], none]
    return jnp.stack(real + imag).reshape(2, ORB, ORB, -1)


def solution(mesh):
    axes = ("y", "zh", "x", "zl", "core")
    finer = Mesh(mesh.devices.reshape(4, 2, 4, 4, 2), axes)
    mom, hist = axes[:3], axes[3:]
    return jax.shard_map(
        per_device,
        mesh=finer,
        in_specs=(P(None, None, None, None, hist, mom), P()),
        out_specs=P(None, None, None, axes),
        check_vma=False,
    )
```

```python
import functools
import math

import jax
import jax.numpy as jnp
import numpy as np
from jax import lax
from jax.experimental import pallas as pl
from jax.experimental.pallas import tpu as pltpu
from jax.sharding import Mesh
from jax.sharding import PartitionSpec as P

NKX = 64
NKY = 64
ORB = 3
PAIRS = ORB * ORB
ROWS = 32
PLANE = 16
SLOTS = 8
LANES = 128

delta_time = 0.01


def lane_tables():
    index = np.arange(64)
    angle = 2.0 * math.pi * (index[:, None] * index[None, :] % 64) / 64
    sign = np.array([[1.0, 1.0], [1.0, -1.0]])
    cosine = np.kron(sign, np.cos(angle)) / 64
    sine = np.kron(sign, np.sin(angle)) / 64
    table = np.block([[cosine, sine], [-sine, cosine]]).astype(np.float32)
    high = table.astype(jnp.bfloat16)
    low = (table - high.astype(np.float32)).astype(jnp.bfloat16)
    turn = 2.0 * math.pi * np.arange(ROWS)[:, None] * np.repeat([0, 1], 64)[None, :] / 64
    twiddle = np.stack([np.cos(turn), np.sin(turn)], 1).astype(np.float32)
    return high, low, twiddle


def turned(value, step, length):
    real, imag = value
    eighths = step * 8 / length
    if eighths == 0:
        return real, imag
    if eighths == 2:
        return -imag, real
    if eighths == 4:
        return -real, -imag
    if eighths == 6:
        return imag, -real
    root = math.sqrt(0.5)
    if eighths == 1:
        return root * (real - imag), root * (real + imag)
    if eighths == 3:
        return -root * (real + imag), root * (real - imag)
    if eighths == 5:
        return root * (imag - real), -root * (real + imag)
    if eighths == 7:
        return root * (real + imag), root * (imag - real)
    cosine, sine = math.cos(2 * math.pi * step / length), math.sin(2 * math.pi * step / length)
    return real * cosine - imag * sine, real * sine + imag * cosine


def plus(first, second):
    return first[0] + second[0], first[1] + second[1]


def minus(first, second):
    return first[0] - second[0], first[1] - second[1]


def fourier(values):
    length = len(values)
    if length == 1:
        return values
    if length == 2:
        return [plus(*values), minus(*values)]
    quarter = length // 4
    parts = [fourier(values[start::4]) for start in range(4)]
    out = [None] * length
    for m in range(quarter):
        first, second, third, fourth = (turned(parts[p][m], p * m, length) for p in range(4))
        even, odd = plus(first, third), minus(first, third)
        other, cross = plus(second, fourth), minus(second, fourth)
        cross = (-cross[1], cross[0])
        out[m], out[m + 2 * quarter] = plus(even, other), minus(even, other)
        out[m + quarter], out[m + 3 * quarter] = plus(odd, cross), minus(odd, cross)
    return out


def product(values, high, low):
    head = values.astype(jnp.bfloat16)
    tail = (values - head.astype(jnp.float32)).astype(jnp.bfloat16)

    left, right = jnp.concatenate([head, tail, head], 1), jnp.concatenate([high, high, low], 0)
    return jnp.dot(left, right, preferred_element_type=jnp.float32)


def kernel(count, stacked, joined, spilled, turn, *refs):
    refs = list(refs)
    if stacked:
        whole = refs.pop(0)
        lower, upper = whole.at[:, 0], whole.at[:, 1]
    else:
        lower, upper = refs.pop(0), refs.pop(0)
    if joined:
        older, older_sigma = refs.pop(0), refs.pop(0)
    weight, high_ref, low_ref, twiddle, before, out = refs[:6]
    field = refs[-1]

    def pair_of(source, plane, pairs, comp, pair):
        size = 2 if pairs == ORB + 1 else pairs
        at = pair // size * 4 * size + 2 * comp * size + pair % size
        return source[plane, at], source[plane, at + size]

    def either_way(act, *sides):
        pl.when(turn[0] == 0)(lambda: act(*sides))
        pl.when(turn[0] == 1)(lambda: act(*(side[::-1] for side in sides)))

    def spot(part):
        return pl.ds(part * LANES, LANES)

    def twist(n):
        return twiddle[n, 0][None, :], twiddle[n, 1][None, :]

    def times(value, factor):
        return value[0] * factor[0] - value[1] * factor[1], value[0] * factor[1] + value[1] * factor[0]

    def forward(halves):
        @pl.loop(0, 2 * count)
        def _(s):
            comp, pair = s // count, s % count
            rows = pl.ds(pl.multiple_of(comp * SLOTS, SLOTS), SLOTS)
            values = [
                pair_of(halves[m // 4 % 2], m // 8 * 4 + m % 4, count, comp, pair) for m in range(ROWS)
            ]
            for n, value in enumerate(fourier(values)):
                real, imag = times(value, twist(n)) if n else value
                field[n, pair, rows, spot(0)] = real
                field[n, pair, rows, spot(1)] = imag

    either_way(forward, (lower, upper))

    block = 32 if count <= ORB else 16
    size = block * count * 2 * SLOTS

    @pl.loop(0, ROWS // block)
    def _(b):
        take = pl.ds(b * block, block)
        high, low = high_ref[...], low_ref[...]
        space = product(field[take].reshape(size, 2 * LANES), high, low)
        space = space.reshape(block * count, 2, SLOTS, 2 * LANES)
        less = space[:, 0, :, :LANES], space[:, 0, :, LANES:]
        great = space[:, 1, :, :LANES], space[:, 1, :, LANES:]

        def bubble(first, other):
            real = first[0] * first[0] - first[1] * first[1]
            imag = 2.0 * first[0] * first[1]
            return -(real * other[0] + imag * other[1]), imag * other[0] - real * other[1]

        sigma = jnp.stack(
            [jnp.concatenate(bubble(less, great), -1), jnp.concatenate(bubble(great, less), -1)], 1
        )
        back = product(sigma.reshape(size, 2 * LANES), high, low)
        field[take] = back.reshape(block, count, 2 * SLOTS, 2 * LANES)

    @pl.loop(0, 2 * count)
    def _(s):
        comp, pair = s // count, s % count
        rows = pl.ds(pl.multiple_of(comp * SLOTS, SLOTS), SLOTS)
        values = [(field[n, pair, rows, spot(0)], field[n, pair, rows, spot(1)]) for n in range(ROWS)]
        values = [times(value, twist(n)) if n else value for n, value in enumerate(values)]
        for m, (real, imag) in enumerate(fourier(values)):
            field[m, pair, rows, spot(0)] = real
            field[m, pair, rows, spot(1)] = imag

    scale = weight[...]

    def contract(plane, half, halves, older_halves):
        m = plane // 4 * 8 + half * 4 + plane % 4

        def sigma(comp, a):
            rows = pl.ds(comp * SLOTS, SLOTS)
            if joined and a == 0:
                return older_sigma[m, rows, spot(0)], older_sigma[m, rows, spot(1)]
            return field[m, a - joined, rows, spot(0)], field[m, a - joined, rows, spot(1)]

        def given(comp, b):
            if joined and b == 0:
                return pair_of(older_halves[half], plane, ORB + 1, comp, ORB)
            return pair_of(halves[half], plane, count, comp, b - joined)

        def memory(a, b):
            left, right = sigma(0, a), given(1, b)
            other, cross = sigma(1, a), given(0, b)
            real = left[0] * right[0] - left[1] * right[1] - other[0] * cross[0] + other[1] * cross[1]
            if a == b:
                return real, None
            imag = left[0] * right[1] + left[1] * right[0] - other[0] * cross[1] - other[1] * cross[0]
            return real, imag

        results = [2.0 * memory(a, a)[0] for a in range(ORB)]
        for a, b in ((0, 1), (0, 2), (1, 2)):
            one, two = memory(a, b), memory(b, a)
            results += [one[0] + two[0], two[1] - one[1]]
        for i, result in enumerate(results):
            row = pl.ds(half * PAIRS + i, 1)
            out[plane, row, :] = before[plane, row, :] + jnp.sum(result * scale, axis=0, keepdims=True)
        if spilled:
            refs[6][m] = field[m, ORB]

    def contract_all(halves, older_halves):
        @pl.loop(0, PLANE, unroll=2)
        def _(plane):
            for half in range(2):
                contract(plane, half, halves, older_halves)

    olders = (older.at[:, 0], older.at[:, 1]) if joined else (None, None)
    either_way(contract_all, (lower, upper), olders)


def collide(turn, fields, weights, high, low, twiddle, before, older=(), spilled=False):
    stacked, joined = len(fields) == 1, int(len(older) > 0)
    count = ORB + 1 if stacked else ORB - joined
    shapes = [jax.ShapeDtypeStruct((PLANE, 2 * PAIRS, LANES), jnp.float32)]
    if spilled:
        shapes.append(jax.ShapeDtypeStruct((ROWS, 2 * SLOTS, 2 * LANES), jnp.float32))
    inputs = (*fields, *older, weights, high, low, twiddle, before)
    return pl.pallas_call(
        functools.partial(kernel, count, stacked, joined, spilled),
        out_shape=shapes,
        in_specs=[pl.BlockSpec(memory_space=pltpu.SMEM)]
        + [pl.BlockSpec(memory_space=pltpu.VMEM)] * len(inputs),
        out_specs=[pl.BlockSpec(memory_space=pltpu.VMEM)] * len(shapes),
        scratch_shapes=[pltpu.VMEM((ROWS, count, 2 * SLOTS, 2 * LANES), jnp.float32)],
        compiler_params=pltpu.CompilerParams(vmem_limit_bytes=24 * 1024 * 1024),
        cost_estimate=pl.CostEstimate(flops=1000000000, bytes_accessed=0, transcendentals=0),
    )(turn, *inputs)


def arrange_kernel(blocks, ways, first, parts, out, sems):
    copies, base = [], 0
    for pairs in blocks:
        for kind in range(4):
            for i, (a, c) in enumerate(pairs):
                at = base + kind * len(pairs) + i
                for n, way in enumerate(ways):
                    half = first[0] if way == 0 else 1 - first[0]
                    target = out.at[:, n, at] if len(ways) > 1 else out.at[:, at]
                    source = parts.at[kind * ORB + a, c, half]
                    copies.append(pltpu.make_async_copy(source, target, sems.at[n, at]))
        base += 4 * len(pairs)
    for copy in copies:
        copy.start()
    for copy in copies:
        copy.wait()


def arrange(first, parts, blocks, ways):
    count = 4 * sum(len(pairs) for pairs in blocks)
    shape = (PLANE, *((len(ways),) if len(ways) > 1 else ()), count, SLOTS, LANES)
    return pl.pallas_call(
        functools.partial(arrange_kernel, blocks, ways),
        out_shape=jax.ShapeDtypeStruct(shape, jnp.float32),
        in_specs=[pl.BlockSpec(memory_space=pltpu.SMEM), pl.BlockSpec(memory_space=pl.ANY)],
        out_specs=pl.BlockSpec(memory_space=pltpu.VMEM),
        scratch_shapes=[pltpu.SemaphoreType.DMA((len(ways), count))],
        compiler_params=pltpu.CompilerParams(vmem_limit_bytes=60 * 1024 * 1024),
        cost_estimate=pl.CostEstimate(flops=0, bytes_accessed=3_200_000, transcendentals=0),
    )(first, parts)


def join_kernel(kept, ahead, landed, out, sems):
    first = ahead.shape[1]
    copies = [
        pltpu.make_async_copy(kept, out.at[:, 0], sems.at[0]),
        pltpu.make_async_copy(ahead, out.at[:, 1, pl.ds(0, first)], sems.at[1]),
        pltpu.make_async_copy(landed, out.at[:, 1, pl.ds(first, landed.shape[1])], sems.at[2]),
    ]
    for copy in copies:
        copy.start()
    for copy in copies:
        copy.wait()


def join(kept, ahead, landed):
    return pl.pallas_call(
        join_kernel,
        out_shape=jax.ShapeDtypeStruct((PLANE, 2, *kept.shape[1:]), jnp.float32),
        in_specs=[pl.BlockSpec(memory_space=pl.ANY)] * 3,
        out_specs=pl.BlockSpec(memory_space=pltpu.VMEM),
        scratch_shapes=[pltpu.SemaphoreType.DMA((3,))],
        compiler_params=pltpu.CompilerParams(vmem_limit_bytes=8 * 1024 * 1024),
        cost_estimate=pl.CostEstimate(flops=0, bytes_accessed=3_200_000, transcendentals=0),
    )(kept, ahead, landed)


def cut_kernel(base, way, whole, out, sem):
    copy = pltpu.make_async_copy(whole.at[:, way, pl.ds(base, out.shape[1])], out, sem)
    copy.start()
    copy.wait()


def cut(whole, base, size, way):
    return pl.pallas_call(
        functools.partial(cut_kernel, base, way),
        out_shape=jax.ShapeDtypeStruct((PLANE, size, SLOTS, LANES), jnp.float32),
        in_specs=[pl.BlockSpec(memory_space=pl.ANY)],
        out_specs=pl.BlockSpec(memory_space=pltpu.VMEM),
        scratch_shapes=[pltpu.SemaphoreType.DMA],
        compiler_params=pltpu.CompilerParams(vmem_limit_bytes=8 * 1024 * 1024),
        cost_estimate=pl.CostEstimate(flops=0, bytes_accessed=1_600_000, transcendentals=0),
    )(whole)


def settle(weights, fields, cost):
    def body(given, *refs):
        refs[-1][...] = given[...]

    return pl.pallas_call(
        body,
        out_shape=jax.ShapeDtypeStruct((SLOTS, LANES), jnp.float32),
        in_specs=[pl.BlockSpec(memory_space=pltpu.VMEM)] + [pl.BlockSpec(memory_space=pl.ANY)] * len(fields),
        out_specs=pl.BlockSpec(memory_space=pltpu.VMEM),
        compiler_params=pltpu.CompilerParams(vmem_limit_bytes=1024 * 1024),
        cost_estimate=pl.CostEstimate(flops=int(cost * 1e9), bytes_accessed=0, transcendentals=0),
    )(weights, *fields)


def per_device(green_row, time_step):
    slot_count = green_row.shape[4]
    history = slot_count * 8
    zh, zl, core = (lax.axis_index(axis) for axis in ("zh", "zl", "core"))
    plane = lax.axis_index("y") * 4 + lax.axis_index("x")
    first = (zl * 2 + core) * slot_count + zh * (slot_count // 2) + plane * SLOTS
    slot_ids = first + jnp.arange(SLOTS, dtype=jnp.int32)
    slot_age = (time_step[0] - 1 - slot_ids) % history + 1
    decays = jnp.exp2(-(slot_age - 1).astype(jnp.float32) / history)
    weights = delta_time * decays * jnp.where(slot_age == history, 0.5, 1.0).astype(jnp.float32)
    weights = jnp.broadcast_to(weights[:, None], (SLOTS, LANES))
    high, low, twiddle = lane_tables()

    parts = green_row.reshape(4 * ORB, ORB, 2, PLANE, SLOTS, LANES)

    def spread(value):
        return lax.all_to_all(value, ("y", "x"), split_axis=0, concat_axis=0)

    def move(value):
        return lax.ppermute(value, "zh", [(0, 1), (1, 0)])

    def work(fields, partial, weights, **more):
        return collide(turn_flag, fields, weights, high, low, twiddle, partial, **more)

    turn_flag = zh.reshape(1).astype(jnp.int32)
    partial = jnp.zeros((PLANE, 2 * PAIRS, LANES), jnp.float32)
    fence = lax.optimization_barrier
    early = [[(0, 0), (1, 0)], [(2, 0), (0, 1)]]
    late = [[(1, 1), (2, 1)], [(0, 2), (1, 2), (2, 2)]]

    side = zh.reshape(1).astype(jnp.int32)
    ahead = arrange(side, parts, early[:1], (1,))
    ahead, side = fence((ahead, side))
    ahead = move(ahead)
    rest = arrange(side, parts, late, (0, 1))
    rest, side = fence((rest, side))
    sent = arrange(side, parts, early[1:], (1,))
    rest, sent = spread(rest), fence(sent)
    landed = move(sent)
    kept = arrange(side, parts, early, (0,))
    kept, weights = fence((kept, weights))
    ahead, rest, weights = fence((ahead, rest, settle(weights, [ahead], 50.0)))
    place, sizes = (0, 4 * len(late[0])), [4 * len(pairs) for pairs in late]
    one, two = (move(cut(rest, base, size, 1)) for base, size in zip(place, sizes))
    one, two = ((cut(rest, base, size, 0), part) for base, size, part in zip(place, sizes, (one, two)))
    zero = spread(join(kept, ahead, landed))
    one, zero, weights = fence((one, zero, settle(weights, one[1:], 50.0)))
    partial, sigma = work([zero], partial, weights, spilled=True)
    (partial,) = work(one, partial, weights, older=(zero, sigma))
    partial, two = fence((partial, two))
    (partial,) = work(two, partial, weights)
    owned = jnp.sum(spread(partial), axis=0)
    share = LANES // 8
    shares = owned.reshape(2, PAIRS, 8, share).transpose(0, 2, 1, 3).reshape(PLANE, 1, PAIRS * share)
    shares = lax.all_to_all(shares, ("zh", "zl", "core"), split_axis=0, concat_axis=0)
    summed = jnp.sum(shares, axis=(0, 1)).reshape(PAIRS, share)
    none = jnp.zeros_like(summed[0])
    real = [summed[0], summed[3], summed[5], summed[3], summed[1], summed[7], summed[5], summed[7], summed[2]]
    imag = [none, summed[4], summed[6], -summed[4], none, summed[8], -summed[6], -summed[8], none]
    return jnp.stack(real + imag).reshape(2, ORB, ORB, -1)


def solution(mesh):
    axes = ("y", "zh", "x", "zl", "core")
    finer = Mesh(mesh.devices.reshape(4, 2, 4, 4, 2), axes)
    mom, hist = axes[:3], axes[3:]
    return jax.shard_map(
        per_device,
        mesh=finer,
        in_specs=(P(None, None, None, None, hist, mom), P()),
        out_specs=P(None, None, None, axes),
        check_vma=False,
    )
```
